128 devices in a mesh: lon: 64 (over x, y, z), lat: 2 (over core).
Axes of the slice: x: 4, y: 4, z: 4, core: 2. Of those that a mesh axis runs over, the one named last changes fastest.
Arguments:
- right_side: float32 [3072, 16384], P('lat', 'lon'), may hold values from -26.2 to 26.2
- east_face: bfloat16 [3072, 16384], P('lat', 'lon'), may hold values from 0.5 to 2
- north_face: bfloat16 [3072, 16384], P('lat', 'lon'), may hold values from 0.5 to 2
- left_factor: bfloat16 [2, 1536, 128, 128], P('lat', 'lon'), may hold values from -0.008 to 1.8
- right_factor: bfloat16 [2, 1536, 128, 128], P('lat', 'lon'), may hold values from -0.008 to 1.8
- wet_list: int32 [2, 1536], P('lat', 'lon'), may hold values from 0 to 24, as said below
Outputs:
- solution: float32 [3072, 16384], P('lat', 'lon')
- precond_residual: bfloat16 [3072, 16384], P('lat', 'lon')
The draws below stay inside these ranges and needn't reach their ends.
Inputs may be any that keep to these rules, and one draw needn't show every extreme that they name: `wet_list`: each device's slots hold the local indices of its wet tiles in increasing order, then 24 in the remaining slots. Some device has all 24 tiles wet. The two devices of one longitude index whose latitude indices are 2 j and 2 j + 1 hold at most 32 wet tiles together, and their counts differ by at most 16; in every draw some such pair reaches both bounds.
All inputs are finite; a program needn't handle non-finite values.
Results may differ from the reference program's by a relative error of at most 0.012.
The reference program's roundings to bfloat16 on the way count: a program that leaves them out, or rounds other values in their place, can miss the bound.
Values may be sent and summed in bfloat16 or wider, within the bound.
No kernel may reach another device: no remote copies, remote signals or barrier semaphores. Data moves between devices by JAX's collectives and lax.ppermute only.
A program may use at most 128 MiB of HBM per device.

```python
import math
import jax
import jax.numpy as jnp
from jax import lax

EDGE = 128
TX = 2
TY = 12
ITERS = 2
K = 24
BAL = 16
SEND = 8
NY = 3072
NX = 16384
N_LON = 64
N_LAT = 2


off_scale = 0.0039


def factor_draw(key):
    entry_key, diagonal_key = jax.random.split(key)
    full_shape = (N_LAT, N_LON * K, EDGE, EDGE)
    entries = jax.random.uniform(entry_key, full_shape, jnp.float32, -1.0, 1.0)
    symmetric = (entries + jnp.swapaxes(entries, -1, -2)) * off_scale
    diagonal = jax.random.uniform(diagonal_key, (N_LAT, N_LON * K, EDGE), jnp.float32, 1.0, 1.8)
    on_diagonal = jnp.arange(EDGE)[:, None] == jnp.arange(EDGE)[None, :]
    return jnp.where(on_diagonal, diagonal[..., None], symmetric).astype(jnp.bfloat16)


def draw_left_factor(key, part):
    key = jax.random.fold_in(key, 21)
    return factor_draw(key)


def draw_right_factor(key, part):
    key = jax.random.fold_in(key, 37)
    return factor_draw(key)


def draw_right_side(key, part):
    key = jax.random.fold_in(key, 11)
    base_key, row_key, col_key = jax.random.split(key, 3)
    ramp = 3.0 ** (jnp.arange(NX, dtype=jnp.float32) / NX)
    col_scale = jnp.exp(jax.random.uniform(col_key, (NX,), jnp.float32, 0.0, 1.19))
    row_scale = jnp.exp(jax.random.uniform(row_key, (NY,), jnp.float32, 0.0, 1.19))
    base = jnp.clip(jax.random.normal(base_key, (NY, NX), jnp.float32), -4.0, 4.0)
    return 0.2 * base * row_scale[:, None] * (col_scale * ramp)[None, :]


def draw_wet_list(key, part):
    key = jax.random.fold_in(key, 5)
    key_list = jax.random.split(key, 5)
    pair_count = N_LAT // 2 * N_LON
    heavy_count = jax.random.randint(key_list[0], (pair_count,), BAL, K + 1)
    light_lowest = jnp.maximum(0, heavy_count - 2 * SEND)
    light_highest = 2 * BAL - heavy_count
    light_count = jax.random.randint(key_list[1], (pair_count,), light_lowest, light_highest + 1)
    marked_pair = jax.random.randint(key_list[2], (), 0, pair_count)
    is_marked = jnp.arange(pair_count) == marked_pair
    heavy_count = jnp.where(is_marked, K, heavy_count)
    light_count = jnp.where(is_marked, 2 * BAL - K, light_count)
    flipped = jax.random.randint(key_list[3], (pair_count,), 0, 2) == 1
    lower_count = jnp.where(flipped, heavy_count, light_count)
    upper_count = jnp.where(flipped, light_count, heavy_count)
    counts = jnp.stack([lower_count.reshape(N_LAT // 2, N_LON), upper_count.reshape(N_LAT // 2, N_LON)], axis=1).reshape(N_LAT, N_LON)
    scores = jax.random.randint(key_list[4], (N_LAT, N_LON, K), 0, 1 << 20) * K + jnp.arange(K)
    ranking = jnp.argsort(jnp.argsort(scores, axis=-1), axis=-1)
    is_wet = ranking < counts[:, :, None]
    ordered = jnp.sort(jnp.where(is_wet, jnp.arange(K), K + jnp.arange(K)), axis=-1)
    return jnp.where(ordered < K, ordered, K).astype(jnp.int32).reshape(N_LAT, N_LON * K)


def block_scale(own_key, extent, cuts, smallest, top_value):
    gain = 1.0
    for axis_at, blocks in cuts:
        draws = jax.random.uniform(jax.random.fold_in(jax.random.fold_in(own_key, 6), axis_at), (blocks,), jnp.float32, smallest / len(cuts), top_value / len(cuts))
        gain = gain * jnp.repeat(jnp.exp(draws), extent[axis_at] // blocks).reshape((-1,) + (1,) * (len(extent) - 1 - axis_at))
    return gain


def setup_inputs(seed: int = 0) -> dict:
    seeds = jax.random.split(jax.random.key(seed), 7)
    right_side = draw_right_side(jax.random.fold_in(seeds[6], 71), 0)
    east_face = jnp.clip(jnp.exp(math.log(2.0) - 1.3862944 * jax.random.uniform(seeds[1], (NY, NX), jnp.float32) ** block_scale(seeds[1], (NY, NX), ((0, 2), (1, 64)), -0.2, 0.2)), 0.5, 2.0).astype(jnp.bfloat16)
    north_face = jnp.clip(jnp.exp(math.log(2.0) - 1.3862944 * jax.random.uniform(seeds[2], (NY, NX), jnp.float32) ** block_scale(seeds[2], (NY, NX), ((0, 2), (1, 64)), -0.2, 0.2)), 0.5, 2.0).astype(jnp.bfloat16)
    left_factor = draw_left_factor(jax.random.fold_in(seeds[6], 71), 0)
    right_factor = draw_right_factor(jax.random.fold_in(seeds[6], 71), 0)
    wet_list = draw_wet_list(jax.random.fold_in(seeds[6], 71), 0)
    return dict(right_side=right_side, east_face=east_face, north_face=north_face, left_factor=left_factor, right_factor=right_factor, wet_list=wet_list)


surface_term = 1e-4


def cell_mask(wet_list):
    wet_slots = wet_list.reshape(N_LAT, N_LON, K)
    matches = (wet_slots[:, :, :, None] == jnp.arange(K, dtype=jnp.int32)[None, None, None, :]).astype(jnp.float32)
    tile_wet = jnp.sum(matches, axis=2)
    tile_grid = tile_wet.reshape(N_LAT, N_LON, TY, TX).transpose(0, 2, 1, 3).reshape(N_LAT * TY, N_LON * TX)
    return jnp.repeat(jnp.repeat(tile_grid, EDGE, axis=0), EDGE, axis=1)


def east_of(field_in):
    return jnp.roll(field_in, -1, axis=1)


def west_of(field_in):
    return jnp.roll(field_in, 1, axis=1)


def north_of(field_in):
    return jnp.concatenate([field_in[1:], jnp.zeros_like(field_in[:1])], axis=0)


def south_of(field_in):
    return jnp.concatenate([jnp.zeros_like(field_in[:1]), field_in[:-1]], axis=0)


def precondition(residual_in, left_factor, right_factor):
    rounded = residual_in.astype(jnp.bfloat16).reshape(N_LAT, TY, EDGE, N_LON, TX, EDGE)
    lefts = left_factor.reshape(N_LAT, N_LON, TY, TX, EDGE, EDGE)
    rights = right_factor.reshape(N_LAT, N_LON, TY, TX, EDGE, EDGE)
    band_list = []
    for band_index in range(N_LAT):
        partial_rows = jnp.einsum("byxij,yjbxk->yibxk", lefts[band_index].astype(jnp.float32), rounded[band_index].astype(jnp.float32))
        partial_rows = lax.optimization_barrier(partial_rows.astype(jnp.bfloat16)).astype(jnp.float32)
        band_list.append(jnp.einsum("yibxj,byxjk->yibxk", partial_rows, rights[band_index].astype(jnp.float32)).astype(jnp.bfloat16))
    return jnp.stack(band_list).reshape(NY, NX)


def reference(right_side, east_face, north_face, left_factor, right_factor, wet_list):
    wet_mask = cell_mask(wet_list)
    east_coeff = east_face.astype(jnp.float32) * wet_mask * east_of(wet_mask)
    north_coeff = north_face.astype(jnp.float32) * wet_mask * north_of(wet_mask)
    west_coeff = west_of(east_coeff)
    south_coeff = south_of(north_coeff)

    def operate(field_in):
        return (surface_term * wet_mask * field_in
                + east_coeff * (field_in - east_of(field_in))
                + west_coeff * (field_in - west_of(field_in))
                + north_coeff * (field_in - north_of(field_in))
                + south_coeff * (field_in - south_of(field_in)))

    solution = jnp.zeros((NY, NX), jnp.float32)
    residual = wet_mask * right_side
    precond = precondition(residual, left_factor, right_factor)
    direction = precond.astype(jnp.float32)
    current_rz = jnp.sum(residual * direction)
    for iteration in range(ITERS):
        image = operate(direction)
        step_size = current_rz / jnp.sum(direction * image)
        solution = solution + step_size * direction
        residual = residual - step_size * image
        precond = precondition(residual, left_factor, right_factor)
        if iteration + 1 < ITERS:
            precond_wide = precond.astype(jnp.float32)
            next_rz = jnp.sum(residual * precond_wide)
            direction = precond_wide + (next_rz / current_rz) * direction
            current_rz = next_rz
    return solution, precond
```

```python
import functools

import jax
import jax.numpy as jnp
from jax import lax
from jax.experimental import pallas as pl
from jax.experimental.pallas import tpu as pltpu
from jax.sharding import PartitionSpec as P

EDGE = 128
surface_term = 0.0001
F32 = jnp.float32
BF16 = jnp.bfloat16
VMEM_LIMIT = 32 * 1024 * 1024
MSG = 32
FACTOR_ROW = 16


def dot(left, right):
    return jnp.dot(left, right, preferred_element_type=F32)


def lane_index(rows, cols):
    return lax.broadcasted_iota(jnp.int32, (rows, cols), 1)


def row_index(rows, cols):
    return lax.broadcasted_iota(jnp.int32, (rows, cols), 0)


def set_flags(wet_ref, flags_ref):
    tiles = wet_ref.shape[1]
    for t in range(flags_ref.shape[0]):
        flags_ref[t] = 0.0
    for k in range(tiles):
        flags_ref[wet_ref[0, k]] = 1.0
    flags_ref[tiles] = 0.0


def mask_row(flags_ref, i):
    lane = lane_index(1, 2 * EDGE)
    return jnp.where(lane < EDGE, flags_ref[2 * i], flags_ref[2 * i + 1])


def rounded_product(left, tile, right):
    partial = dot(left, tile).astype(BF16)
    return dot(partial, right).astype(BF16)


def split(value):
    high = value.astype(BF16)
    return high, (value - high.astype(F32)).astype(BF16)


def wide_product(left, tile, right):
    both = dot(left, jnp.concatenate(split(tile), axis=1))
    partial = both[:, :EDGE] + both[:, EDGE:]
    both = dot(jnp.concatenate(split(partial), axis=0), right)
    return both[:EDGE] + both[EDGE:]


def fold(block):
    total = block[0:8]
    for k in range(1, block.shape[0] // 8):
        total = total + block[8 * k : 8 * k + 8]
    return total


def column(rows_ref, i):
    return jnp.broadcast_to(rows_ref[pl.ds(i, 1), :], (EDGE, EDGE)).T


def stencil(i, tile_rows, field_ref, ef_ref, nf_ref, flags_ref, east_flux, west_flux, south_flux, top_flux):
    rows = pl.ds(i * EDGE, EDGE)
    field = field_ref[rows, :]
    wet_w, wet_e = flags_ref[2 * i], flags_ref[2 * i + 1]
    north_w, north_e = flags_ref[2 * i + 2], flags_ref[2 * i + 3]
    lane = lane_index(1, 2 * EDGE)
    wet = jnp.where(lane < EDGE, wet_w, wet_e)
    east_wet = jnp.where(lane == EDGE - 1, wet_w * wet_e, jnp.where(lane == 2 * EDGE - 1, 0.0, wet))
    flux_e = (ef_ref[rows, :].astype(F32) * east_wet) * (field - pltpu.roll(field, 2 * EDGE - 1, 1))
    wide_lane = lane_index(EDGE, 2 * EDGE)
    if east_flux is not None:
        wide = jnp.concatenate([east_flux, east_flux], axis=1)
        flux_e = jnp.where(wide_lane == 2 * EDGE - 1, wide, flux_e)
    flux_w = pltpu.roll(flux_e, 1, 1)
    if west_flux is None:
        flux_w = jnp.where(wide_lane == 0, 0.0, flux_w)
    else:
        flux_w = jnp.where(wide_lane == 0, jnp.concatenate([west_flux, west_flux], axis=1), flux_w)
    row = row_index(EDGE, 2 * EDGE)
    north_wet = jnp.where(lane < EDGE, wet_w * north_w, wet_e * north_e)
    above = field_ref[pl.ds(jnp.minimum((i + 1) * EDGE, tile_rows * EDGE - 1), 1), :]
    north = jnp.where(row == EDGE - 1, above, pltpu.roll(field, EDGE - 1, 0))
    flux_n = nf_ref[rows, :].astype(F32) * jnp.where(row == EDGE - 1, north_wet, wet) * (field - north)
    last = jnp.where(i == tile_rows - 1, top_flux, flux_n[EDGE - 1 :, :])
    flux_n = jnp.where(row == EDGE - 1, last, flux_n)
    flux_s = jnp.where(row == 0, south_flux, pltpu.roll(flux_n, 1, 0))
    image = surface_term * wet * field + (flux_e - flux_w) + (flux_n - flux_s)
    return field, image, last


def edge_fluxes(own_e, own_w, own_l, from_e, from_w, from_l, coef_e, coef_w, coef_l, east_ref, west_ref):
    east_ref[...] = coef_e * (own_e - from_e)
    west_ref[...] = coef_w * (from_w - own_w)
    flux = coef_l * (own_l - from_l)
    low = lax.axis_index("lat") == 0
    return jnp.where(low, flux, 0.0), jnp.where(low, 0.0, -flux)


def coefficients(to_e, to_w, to_l, from_e, from_w, from_l):
    coef_e = to_e[FACTOR_ROW:, :] * from_e[FACTOR_ROW:, :]
    coef_w = to_w[FACTOR_ROW:, :] * from_w[FACTOR_ROW:, :]
    coef_l = to_l[1:2, :] * from_l[1:2, :]
    return coef_e, coef_w, coef_l


def send_edges(i, tile_rows, block, to_e, to_w, to_l):
    to_w[pl.ds(i, 1), :] = block[:, :EDGE].T[0:1, :]
    to_e[pl.ds(i, 1), :] = block[:, EDGE:].T[EDGE - 1 :, :]

    low = lax.axis_index("lat") == 0

    @pl.when(low & (i == tile_rows - 1))
    def _():
        to_l[0:1, :] = block[EDGE - 1 :, :]

    @pl.when(jnp.logical_not(low) & (i == 0))
    def _():
        to_l[0:1, :] = block[0:1, :]


def first_kernel(wet_ref, rhs_ref, left_ref, right_ref, ef_ref, nf_ref, z_ref, to_e, to_w, to_l, sum_ref, flags_ref):
    tile_rows = rhs_ref.shape[0] // EDGE
    set_flags(wet_ref, flags_ref)
    to_e[...] = jnp.zeros_like(to_e)
    to_w[...] = jnp.zeros_like(to_w)
    to_l[...] = jnp.zeros_like(to_l)

    def step(i, total):
        rows = pl.ds(i * EDGE, EDGE)
        residual = rhs_ref[rows, :] * mask_row(flags_ref, i)
        rounded = residual.astype(BF16)
        parts = [
            rounded_product(left_ref[0, 2 * i + k], rounded[:, k * EDGE : (k + 1) * EDGE], right_ref[0, 2 * i + k])
            for k in range(2)
        ]
        precond = jnp.concatenate(parts, axis=1).astype(F32)
        z_ref[rows, :] = precond
        send_edges(i, tile_rows, precond, to_e, to_w, to_l)
        to_w[pl.ds(FACTOR_ROW + i, 1), :] = jnp.full((1, EDGE), flags_ref[2 * i], F32)
        face = ef_ref[rows, EDGE:].astype(F32) * flags_ref[2 * i + 1]
        to_e[pl.ds(FACTOR_ROW + i, 1), :] = face.T[EDGE - 1 :, :]
        return total + fold(residual * precond)

    sum_ref[...] = lax.fori_loop(0, tile_rows, step, jnp.zeros(sum_ref.shape, F32))
    low = lax.axis_index("lat") == 0
    last = nf_ref[pl.ds((tile_rows - 1) * EDGE, EDGE), :].astype(F32)[EDGE - 1 :, :]
    to_l[1:2, :] = jnp.where(low, last * mask_row(flags_ref, tile_rows - 1), mask_row(flags_ref, 0))


def second_kernel(
    wet_ref, z_ref, rhs_ref, left_ref, right_ref, ef_ref, nf_ref, to_e, to_w, to_l, from_e, from_w, from_l, sum_in,
    q_ref, w_ref, out_e, out_w, out_l, sums_ref, flags_ref, east_ref, west_ref,
):
    tile_rows = z_ref.shape[0] // EDGE
    set_flags(wet_ref, flags_ref)
    out_e[...] = jnp.zeros_like(out_e)
    out_w[...] = jnp.zeros_like(out_w)
    out_l[...] = jnp.zeros_like(out_l)
    coefs = coefficients(to_e, to_w, to_l, from_e, from_w, from_l)
    top, bottom = edge_fluxes(
        to_e[:FACTOR_ROW, :], to_w[:FACTOR_ROW, :], to_l[0:1, :],
        from_e[:FACTOR_ROW, :], from_w[:FACTOR_ROW, :], from_l[0:1, :], *coefs, east_ref, west_ref,
    )

    def step(i, carry):
        south, zq, rw, qw = carry
        rows = pl.ds(i * EDGE, EDGE)
        field, image, south = stencil(
            i, tile_rows, z_ref, ef_ref, nf_ref, flags_ref, column(east_ref, i), column(west_ref, i), south, top
        )
        q_ref[rows, :] = image
        parts = [
            wide_product(left_ref[0, 2 * i + k], image[:, k * EDGE : (k + 1) * EDGE], right_ref[0, 2 * i + k])
            for k in range(2)
        ]
        product = jnp.concatenate(parts, axis=1)
        w_ref[rows, :] = product
        send_edges(i, tile_rows, product, out_e, out_w, out_l)
        residual = rhs_ref[rows, :] * mask_row(flags_ref, i)
        return south, zq + fold(field * image), rw + fold(residual * product), qw + fold(image * product)

    zero = jnp.zeros((8, 2 * EDGE), F32)
    _, zq, rw, qw = lax.fori_loop(0, tile_rows, step, (bottom, zero, zero, zero))
    sums_ref[0] = sum_in[...]
    sums_ref[1] = zq
    sums_ref[2] = rw
    sums_ref[3] = qw


def third_kernel(
    wet_ref, w_ref, ef_ref, nf_ref, to_e, to_w, to_l, from_e, from_w, from_l,
    out_e, out_w, out_l, in_e, in_w, in_l, sums_in, aw_ref, sums_ref, flags_ref, east_ref, west_ref,
):
    tile_rows = w_ref.shape[0] // EDGE
    set_flags(wet_ref, flags_ref)
    coefs = coefficients(to_e, to_w, to_l, from_e, from_w, from_l)
    top, bottom = edge_fluxes(
        out_e[...], out_w[...], out_l[0:1, :], in_e[...], in_w[...], in_l[0:1, :], *coefs, east_ref, west_ref
    )

    def step(i, carry):
        south, total = carry
        field, image, south = stencil(
            i, tile_rows, w_ref, ef_ref, nf_ref, flags_ref, column(east_ref, i), column(west_ref, i), south, top
        )
        aw_ref[pl.ds(i * EDGE, EDGE), :] = image
        return south, total + fold(field * image)

    _, waw = lax.fori_loop(0, tile_rows, step, (bottom, jnp.zeros((8, 2 * EDGE), F32)))
    lane = lane_index(1, EDGE)
    packed = jnp.zeros((1, EDGE), F32)
    for k in range(5):
        total = waw if k == 4 else sums_in[k]
        value = jnp.sum(jnp.sum(total, axis=0, keepdims=True), axis=1, keepdims=True)
        packed = jnp.where(lane == k, value, packed)
    sums_ref[...] = jnp.broadcast_to(packed, sums_ref.shape)


def last_kernel(
    wet_ref, all_ref, rhs_ref, z_ref, w_ref, q_ref, aw_ref, left_ref, right_ref, sol_ref, pre_ref, flags_ref
):
    tile_rows = z_ref.shape[0] // EDGE
    set_flags(wet_ref, flags_ref)
    totals = jnp.sum(all_ref[...], axis=0, keepdims=True)
    lane = lane_index(1, EDGE)
    rz, zq, rw, qw, waw = (
        jnp.sum(jnp.where(lane == k, totals, 0.0), axis=1, keepdims=True) for k in range(5)
    )
    step0 = rz / zq
    rz1 = step0 * (step0 * qw - rw)
    grow = 1.0 + rz1 / rz
    step1 = rz1 / (grow * grow * zq - 2.0 * grow * step0 * qw + step0 * step0 * waw)
    with_z = step0 + step1 * grow
    with_w = -step1 * step0

    def step(i, carry):
        rows = pl.ds(i * EDGE, EDGE)
        sol_ref[rows, :] = with_z * z_ref[rows, :] + with_w * w_ref[rows, :]
        residual = rhs_ref[rows, :] * mask_row(flags_ref, i) - with_z * q_ref[rows, :] - with_w * aw_ref[rows, :]
        rounded = residual.astype(BF16)
        parts = [
            rounded_product(left_ref[0, 2 * i + k], rounded[:, k * EDGE : (k + 1) * EDGE], right_ref[0, 2 * i + k])
            for k in range(2)
        ]
        pre_ref[rows, :] = jnp.concatenate(parts, axis=1)
        return carry

    lax.fori_loop(0, tile_rows, step, 0)


def call(kernel, outs, args, scratch, flops, name):
    vmem = pl.BlockSpec(memory_space=pltpu.VMEM)
    smem = pl.BlockSpec(memory_space=pltpu.SMEM)
    moved = sum(a.size * a.dtype.itemsize for a in args) + sum(o.size * o.dtype.itemsize for o in outs)
    return pl.pallas_call(
        kernel,
        out_shape=outs,
        in_specs=[smem] + [vmem] * (len(args) - 1),
        out_specs=[vmem] * len(outs),
        scratch_shapes=[pltpu.SMEM((32,), F32)] + scratch,
        compiler_params=pltpu.CompilerParams(vmem_limit_bytes=VMEM_LIMIT),
        cost_estimate=pl.CostEstimate(flops=flops, bytes_accessed=moved, transcendentals=0),
        name=name,
    )(*args)


def per_device(right_side, east_face, north_face, left_factor, right_factor, wet_list):
    rows, cols = right_side.shape
    lons, lats = lax.axis_size("lon"), lax.axis_size("lat")
    shape = functools.partial(jax.ShapeDtypeStruct, dtype=F32)
    to_west = [(i, (i - 1) % lons) for i in range(lons)]
    to_east = [(i, (i + 1) % lons) for i in range(lons)]
    across = [(0, 1), (1, 0)]
    edges = [pltpu.VMEM((FACTOR_ROW, EDGE), F32)] * 2

    def exchange(to_e, to_w, to_l):
        from_w = lax.ppermute(to_e, "lon", to_east)
        from_e = lax.ppermute(to_w, "lon", to_west)
        from_l = lax.ppermute(to_l, "lat", across)
        return from_e, from_w, from_l

    z, *to, rz = call(
        first_kernel,
        [shape((rows, cols)), shape((MSG, EDGE)), shape((MSG, EDGE)), shape((8, cols)), shape((8, cols))],
        (wet_list, right_side, left_factor, right_factor, east_face, north_face),
        [], 4 * rows * cols * EDGE, "first",
    )
    came = exchange(*to)
    q, w, *out, sums = call(
        second_kernel,
        [shape((rows, cols)), shape((rows, cols)), shape((FACTOR_ROW, EDGE)), shape((FACTOR_ROW, EDGE)),
         shape((8, cols)), shape((4, 8, cols))],
        (wet_list, z, right_side, left_factor, right_factor, east_face, north_face, *to, *came, rz),
        edges, 8 * rows * cols * EDGE, "second",
    )
    arrived = exchange(*out)
    aw, partial = call(
        third_kernel,
        [shape((rows, cols)), shape((lons * lats, EDGE))],
        (wet_list, w, east_face, north_face, *to, *came, *out, *arrived, sums),
        edges, 20 * rows * cols, "third",
    )
    everyone = lax.all_to_all(partial, ("lon", "lat"), 0, 0, tiled=True)
    return tuple(
        call(
            last_kernel,
            [shape((rows, cols)), jax.ShapeDtypeStruct((rows, cols), BF16)],
            (wet_list, everyone, right_side, z, w, q, aw, left_factor, right_factor),
            [], 4 * rows * cols * EDGE, "last",
        )
    )


def solution(mesh):
    tiles = P("lat", "lon", None, None)
    cells = P("lat", "lon")
    return jax.shard_map(
        per_device,
        mesh=mesh,
        in_specs=(cells, cells, cells, tiles, tiles, cells),
        out_specs=(cells, cells),
        check_vma=False,
    )
```

```python
import functools

import jax
import jax.numpy as jnp
from jax import lax
from jax.experimental import pallas as pl
from jax.experimental.pallas import tpu as pltpu
from jax.sharding import PartitionSpec as P

EDGE = 128
CELLS = 2 * EDGE
surface_term = 0.0001
F32 = jnp.float32
BF16 = jnp.bfloat16
VMEM_LIMIT = 32 * 1024 * 1024
ROWS = 16


def dot(left, right):
    return jnp.dot(left, right, preferred_element_type=F32)


def dot_nt(left, right):
    return lax.dot_general(left, right, (((1,), (1,)), ((), ())), preferred_element_type=F32)


def lane_index(rows, cols):
    return lax.broadcasted_iota(jnp.int32, (rows, cols), 1)


def row_index(rows, cols):
    return lax.broadcasted_iota(jnp.int32, (rows, cols), 0)


def rounded_product(left, tile, right):
    partial = dot(left, tile).astype(BF16)
    return dot(partial, right).astype(BF16)


def split(value):
    high = value.astype(BF16)
    return high, (value - high.astype(F32)).astype(BF16)


def wide_product(left, tile, right):
    partial = dot(jnp.concatenate([left, left], axis=1), jnp.concatenate(split(tile), axis=0))
    return dot(jnp.concatenate(split(partial), axis=1), jnp.concatenate([right, right], axis=0))


def fold(block):
    total = block[0:8]
    for k in range(1, block.shape[0] // 8):
        total = total + block[8 * k : 8 * k + 8]
    return total


def column(rows_ref, i):
    return jnp.broadcast_to(rows_ref[i : i + 1, :], (EDGE, EDGE)).T


def on_low_band():
    return lax.axis_index("lat") == 0


def on_odd_sector():
    return lax.axis_index("lon") % 2 == 1


def pair_up(to_e, to_w):
    odd = on_odd_sector()
    return jnp.where(odd, to_e, to_w), jnp.where(odd, to_w, to_e)


def stencil(i, tile_rows, field_ref, ef_ref, nf_ref, wet_ref, south_flux, top_flux):
    rows = slice(i * EDGE, (i + 1) * EDGE)
    field = field_ref[rows, :]
    wet = wet_ref[i : i + 1, :]
    lane = lane_index(1, CELLS)
    both = wet * pltpu.roll(wet, EDGE, 1)
    east_wet = jnp.where(lane == EDGE - 1, both, jnp.where(lane == CELLS - 1, 0.0, wet))
    flux_e = (ef_ref[rows, :].astype(F32) * east_wet) * (field - pltpu.roll(field, CELLS - 1, 1))
    flux_w = pltpu.roll(flux_e, 1, 1)
    row = row_index(EDGE, CELLS)
    above = min((i + 1) * EDGE, tile_rows * EDGE - 1)
    north = jnp.where(row == EDGE - 1, field_ref[above : above + 1, :], pltpu.roll(field, EDGE - 1, 0))
    flux_n = (nf_ref[rows, :].astype(F32) * wet) * (field - north)
    if i == tile_rows - 1:
        last = top_flux
    else:
        last = flux_n[EDGE - 1 :, :] * wet_ref[i + 1 : i + 2, :]
    flux_n = jnp.where(row == EDGE - 1, last, flux_n)
    flux_s = jnp.where(row == 0, south_flux, pltpu.roll(flux_n, 1, 0))
    return field, surface_term * field + (flux_e - flux_w) + (flux_n - flux_s), last


def lat_flux(coef, own, other):
    flux = coef * (own - other)
    low = on_low_band()
    return jnp.where(low, flux, 0.0), jnp.where(low, 0.0, -flux)


def edge_rows(i, block, east_ref, west_ref):
    west_ref[i : i + 1, :] = block[:, :EDGE].T[0:1, :]
    east_ref[i : i + 1, :] = block[:, EDGE:].T[EDGE - 1 :, :]


def boundary_row(ref):
    return jnp.where(on_low_band(), ref[ref.shape[0] - 1 :, :], ref[0:1, :])


def first_kernel(
    wet_hbm, rhs_hbm, left_hbm, right_hbm, ef_hbm, nf_hbm,
    z_ref, r_ref, left_ref, right_ref, ef_ref, nf_ref, wet_ref, to_e, to_w, to_a, to_b, to_l, sum_ref,
    list_ref, flags_ref, rhs_ref, sems,
):
    tile_rows = rhs_hbm.shape[0] // EDGE
    tiles = 2 * tile_rows
    step = 2
    listing = pltpu.make_async_copy(wet_hbm, list_ref, sems.at[0])
    listing.start()
    loads = []
    for k in range(tile_rows // step):
        rows = pl.ds(k * step * EDGE, step * EDGE)
        some = pl.ds(k * step * 2, step * 2)
        group = [
            pltpu.make_async_copy(rhs_hbm.at[rows], rhs_ref.at[rows], sems.at[3 + 3 * k]),
            pltpu.make_async_copy(left_hbm.at[0, some], left_ref.at[0, some], sems.at[4 + 3 * k]),
            pltpu.make_async_copy(right_hbm.at[0, some], right_ref.at[0, some], sems.at[5 + 3 * k]),
        ]
        for copy in group:
            copy.start()
        loads.append(group)
    faces = [
        pltpu.make_async_copy(ef_hbm, ef_ref, sems.at[1]),
        pltpu.make_async_copy(nf_hbm, nf_ref, sems.at[2]),
    ]
    for copy in faces:
        copy.start()
    for ref in (wet_ref, to_e, to_w, to_l):
        ref[...] = jnp.zeros_like(ref)
    listing.wait()
    for t in range(flags_ref.shape[0]):
        flags_ref[t] = 0.0
    for k in range(tiles):
        flags_ref[list_ref[0, k]] = 1.0
    lane = lane_index(1, CELLS)
    for i in range(tile_rows):
        wet_ref[i : i + 1, :] = jnp.where(lane < EDGE, flags_ref[2 * i], flags_ref[2 * i + 1])
    total = jnp.zeros(sum_ref.shape, F32)
    for i in range(tile_rows):
        if i % step == 0:
            for copy in loads[i // step]:
                copy.wait()
        rows = slice(i * EDGE, (i + 1) * EDGE)
        residual = rhs_ref[rows, :] * wet_ref[i : i + 1, :]
        r_ref[rows, :] = residual
        rounded = residual.astype(BF16)
        parts = [
            rounded_product(left_ref[0, 2 * i + k], rounded[:, k * EDGE : (k + 1) * EDGE], right_ref[0, 2 * i + k])
            for k in range(2)
        ]
        precond = jnp.concatenate(parts, axis=1).astype(F32)
        z_ref[rows, :] = precond
        edge_rows(i, precond, to_e, to_w)
        total = total + fold(residual * precond)
    sum_ref[...] = total
    for copy in faces:
        copy.wait()
    for i in range(tile_rows):
        face = ef_ref[i * EDGE : (i + 1) * EDGE, EDGE:].astype(F32) * wet_ref[i : i + 1, EDGE:]
        to_e[ROWS + i : ROWS + i + 1, :] = face.T[EDGE - 1 :, :]
    to_w[ROWS : ROWS + tile_rows, :] = wet_ref[:tile_rows, :EDGE]
    to_l[0:1, :] = boundary_row(z_ref)
    rows = tile_rows * EDGE
    last = nf_ref[rows - 16 : rows, :].astype(F32)[15:16, :] * wet_ref[tile_rows - 1 : tile_rows, :]
    to_l[1:2, :] = jnp.where(on_low_band(), last, wet_ref[0:1, :])
    to_a[...], to_b[...] = pair_up(to_e[...], to_w[...])


def inner_kernel(z_ref, left_ref, right_ref, ef_ref, nf_ref, wet_ref, to_l, in_l, q_ref, w_ref, east_ref, west_ref):
    tile_rows = z_ref.shape[0] // EDGE
    east_ref[...] = jnp.zeros_like(east_ref)
    west_ref[...] = jnp.zeros_like(west_ref)
    top, south = lat_flux(to_l[1:2, :] * in_l[1:2, :], to_l[0:1, :], in_l[0:1, :])
    for i in range(tile_rows):
        rows = slice(i * EDGE, (i + 1) * EDGE)
        _, image, south = stencil(i, tile_rows, z_ref, ef_ref, nf_ref, wet_ref, south, top)
        q_ref[rows, :] = image
        parts = [
            wide_product(left_ref[0, 2 * i + k], image[:, k * EDGE : (k + 1) * EDGE], right_ref[0, 2 * i + k])
            for k in range(2)
        ]
        product = jnp.concatenate(parts, axis=1)
        w_ref[rows, :] = product
        edge_rows(i, product, east_ref, west_ref)


def edge_kernel(
    w_ref, left_ref, right_ref, east_in, west_in, to_e, to_w, in_a, in_b,
    east_ref, west_ref, to_a, to_b, to_l, coef_e, coef_w, flux_e, flux_w, turn_e, turn_w, right_e, right_w,
):
    tile_rows = w_ref.shape[0] // EDGE
    odd = on_odd_sector()
    from_e = jnp.where(odd, in_a[...], in_b[...])
    from_w = jnp.where(odd, in_b[...], in_a[...])
    coef_e[...] = to_e[ROWS:, :] * from_e[ROWS:, :]
    coef_w[...] = to_w[ROWS:, :] * from_w[ROWS:, :]
    flux_e[...] = coef_e[...] * (to_e[:ROWS, :] - from_e[:ROWS, :])
    flux_w[...] = coef_w[...] * (to_w[:ROWS, :] - from_w[:ROWS, :])
    for ref in (turn_e, turn_w, right_e, right_w, to_l):
        ref[...] = jnp.zeros_like(ref)
    spread = jnp.concatenate(split(flux_e[...]) + split(flux_w[...]), axis=0)
    for i in range(tile_rows):
        moved_e = dot_nt(spread[: 2 * ROWS], left_ref[0, 2 * i + 1])
        moved_w = dot_nt(spread[2 * ROWS :], left_ref[0, 2 * i])
        turn_e[i : i + 1, :] = moved_e[i : i + 1, :] + moved_e[ROWS + i : ROWS + i + 1, :]
        turn_w[i : i + 1, :] = moved_w[i : i + 1, :] + moved_w[ROWS + i : ROWS + i + 1, :]
        right_e[i : i + 1, :] = right_ref[0, 2 * i + 1, EDGE - 16 :, :].astype(F32)[15:16, :]
        right_w[i : i + 1, :] = right_ref[0, 2 * i, 0:16, :].astype(F32)[0:1, :]
    east_ref[...] = east_in[...] + turn_e[...] * right_e[:, EDGE - 1 :]
    west_ref[...] = west_in[...] + turn_w[...] * right_w[:, 0:1]
    to_a[...], to_b[...] = pair_up(east_ref[...], west_ref[...])
    low = on_low_band()
    end = tile_rows - 1
    by_e = jnp.where(low, turn_e[end : end + 1, EDGE - 1 :] * right_e[end : end + 1, :], turn_e[0:1, 0:1] * right_e[0:1, :])
    by_w = jnp.where(low, turn_w[end : end + 1, EDGE - 1 :] * right_w[end : end + 1, :], turn_w[0:1, 0:1] * right_w[0:1, :])
    to_l[0:1, :] = boundary_row(w_ref) + jnp.concatenate([by_w, by_e], axis=1)


def middle_kernel(
    z_ref, r_ref, q_in, w_in, ef_ref, nf_ref, wet_ref, flux_e, flux_w, turn_e, turn_w, right_e, right_w, sum_in,
    q_ref, w_ref, aw_ref, sums_ref,
):
    tile_rows = z_ref.shape[0] // EDGE
    lane = lane_index(EDGE, EDGE)
    zero = jnp.zeros((8, CELLS), F32)
    zq, rw, qw, waw = zero, zero, zero, zero

    def complete(i, zq, rw, qw):
        rows = slice(i * EDGE, (i + 1) * EDGE)
        image = q_in[rows, :] + jnp.concatenate(
            [jnp.where(lane == 0, column(flux_w, i), 0.0), jnp.where(lane == EDGE - 1, column(flux_e, i), 0.0)], axis=1
        )
        product = w_in[rows, :] + jnp.concatenate(
            [column(turn_w, i) * right_w[i : i + 1, :], column(turn_e, i) * right_e[i : i + 1, :]], axis=1
        )
        q_ref[rows, :] = image
        w_ref[rows, :] = product
        return zq + fold(z_ref[rows, :] * image), rw + fold(r_ref[rows, :] * product), qw + fold(image * product)

    south = jnp.zeros((1, CELLS), F32)
    top = south
    zq, rw, qw = complete(0, zq, rw, qw)
    for i in range(tile_rows):
        if i + 1 < tile_rows:
            zq, rw, qw = complete(i + 1, zq, rw, qw)
        field, image, south = stencil(i, tile_rows, w_ref, ef_ref, nf_ref, wet_ref, south, top)
        aw_ref[i * EDGE : (i + 1) * EDGE, :] = image
        waw = waw + fold(field * image)
    for k, total in enumerate((sum_in[...], zq, rw, qw, waw)):
        sums_ref[k] = total


def sums_kernel(
    sums_in, east_ref, west_ref, coef_e, coef_w, own_l, own_l2, in_l, in_l2, in_a, in_b,
    packed_ref, flux_e, flux_w, flux_l,
):
    odd = on_odd_sector()
    from_e = jnp.where(odd, in_a[...], in_b[...])
    from_w = jnp.where(odd, in_b[...], in_a[...])
    flux_e[...] = coef_e[...] * (east_ref[...] - from_e)
    flux_w[...] = coef_w[...] * (west_ref[...] - from_w)
    top, bottom = lat_flux(own_l[1:2, :] * in_l[1:2, :], own_l2[0:1, :], in_l2[0:1, :])
    flux_l[...] = jnp.zeros_like(flux_l)
    flux_l[0:1, :] = top
    flux_l[1:2, :] = -bottom
    outer = flux_e[...] * east_ref[...] + flux_w[...] * west_ref[...]
    across = (top - bottom) * own_l2[0:1, :]
    extra = jnp.sum(jnp.sum(outer, axis=0, keepdims=True), axis=1, keepdims=True)
    extra = extra + jnp.sum(across, axis=1, keepdims=True)
    lane = lane_index(1, EDGE)
    packed = jnp.zeros((1, EDGE), F32)
    for k in range(5):
        value = jnp.sum(jnp.sum(sums_in[k], axis=0, keepdims=True), axis=1, keepdims=True)
        packed = jnp.where(lane == k, value + extra if k == 4 else value, packed)
    packed_ref[...] = jnp.broadcast_to(packed, packed_ref.shape)


def last_kernel(
    all_ref, r_ref, z_ref, w_ref, q_ref, aw_ref, left_ref, right_ref, flux_e, flux_w, flux_l,
    sol_hbm, pre_hbm, sol_ref, pre_ref, sems,
):
    tile_rows = z_ref.shape[0] // EDGE
    totals = jnp.sum(all_ref[...], axis=0, keepdims=True)
    lane = lane_index(1, EDGE)
    rz, zq, rw, qw, waw = (jnp.sum(jnp.where(lane == k, totals, 0.0), axis=1, keepdims=True) for k in range(5))
    step0 = rz / zq
    rz1 = step0 * (step0 * qw - rw)
    grow = 1.0 + rz1 / rz
    step1 = rz1 / (grow * grow * zq - 2.0 * grow * step0 * qw + step0 * step0 * waw)
    with_z = step0 + step1 * grow
    with_w = -step1 * step0
    row = row_index(EDGE, CELLS)
    lane = lane_index(EDGE, EDGE)
    stores = []
    for i in range(tile_rows):
        rows = slice(i * EDGE, (i + 1) * EDGE)
        sol_ref[rows, :] = with_z * z_ref[rows, :] + with_w * w_ref[rows, :]
        outer = jnp.concatenate(
            [jnp.where(lane == 0, column(flux_w, i), 0.0), jnp.where(lane == EDGE - 1, column(flux_e, i), 0.0)], axis=1
        )
        if i == 0:
            outer = outer + jnp.where(row == 0, flux_l[1:2, :], 0.0)
        if i == tile_rows - 1:
            outer = outer + jnp.where(row == EDGE - 1, flux_l[0:1, :], 0.0)
        residual = r_ref[rows, :] - with_z * q_ref[rows, :] - with_w * (aw_ref[rows, :] + outer)
        rounded = residual.astype(BF16)
        parts = [
            rounded_product(left_ref[0, 2 * i + k], rounded[:, k * EDGE : (k + 1) * EDGE], right_ref[0, 2 * i + k])
            for k in range(2)
        ]
        pre_ref[rows, :] = jnp.concatenate(parts, axis=1)
        place = pl.ds(i * EDGE, EDGE)
        for k, (source, target) in enumerate(((sol_ref, sol_hbm), (pre_ref, pre_hbm))):
            copy = pltpu.make_async_copy(source.at[place], target.at[place], sems.at[2 * i + k])
            copy.start()
            stores.append(copy)
    for copy in stores:
        copy.wait()


def call(kernel, outs, args, flops, name, scratch=(), in_space=pltpu.VMEM, out_space=pltpu.VMEM):
    moved = sum(a.size * a.dtype.itemsize for a in args) + sum(o.size * o.dtype.itemsize for o in outs)
    return pl.pallas_call(
        kernel,
        out_shape=outs,
        in_specs=[pl.BlockSpec(memory_space=in_space)] * len(args),
        out_specs=[pl.BlockSpec(memory_space=out_space)] * len(outs),
        scratch_shapes=scratch,
        compiler_params=pltpu.CompilerParams(vmem_limit_bytes=VMEM_LIMIT),
        cost_estimate=pl.CostEstimate(flops=flops, bytes_accessed=moved, transcendentals=0),
        name=name,
    )(*args)


def per_device(right_side, east_face, north_face, left_factor, right_factor, wet_list):
    rows, cols = right_side.shape
    lons, lats = lax.axis_size("lon"), lax.axis_size("lat")
    tile_rows = rows // EDGE
    shape = functools.partial(jax.ShapeDtypeStruct, dtype=F32)
    like = lambda a: jax.ShapeDtypeStruct(a.shape, a.dtype)
    field = shape((rows, cols))
    edge = shape((ROWS, EDGE))
    message = shape((2 * ROWS, EDGE))
    strip = shape((8, cols))
    across = [(0, 1), (1, 0)]

    def pairs(parity):
        forward = [(i, (i + 1) % lons) for i in range(parity, lons, 2)]
        return forward + [(b, a) for a, b in forward]

    def exchange(to_a, to_b, to_l):
        in_a = lax.ppermute(to_a, "lon", pairs(1))
        in_b = lax.ppermute(to_b, "lon", pairs(0))
        return in_a, in_b, lax.ppermute(to_l, "lat", across)

    product = 4 * rows * cols * EDGE
    arguments = [
        pltpu.with_memory_space_constraint(a, pltpu.HBM)
        for a in (wet_list, right_side, left_factor, right_factor, east_face, north_face)
    ]
    z, r, left, right, ef, nf, wet, to_e, to_w, to_a, to_b, to_l, rz = call(
        first_kernel,
        [field, field, like(left_factor), like(right_factor), like(east_face), like(north_face), shape((ROWS, cols)),
         message, message, message, message, strip, strip],
        arguments, product, "first",
        [pltpu.SMEM(wet_list.shape, jnp.int32), pltpu.SMEM((32,), F32), pltpu.VMEM((rows, cols), F32),
         pltpu.SemaphoreType.DMA((3 + 3 * tile_rows // 2,))],
        in_space=pltpu.HBM,
    )
    in_a, in_b, in_l = exchange(to_a, to_b, to_l)
    q, w, east, west = call(
        inner_kernel, [field, field, edge, edge], (z, left, right, ef, nf, wet, to_l, in_l), 2 * product, "inner"
    )
    east, west, to_a2, to_b2, to_l2, coef_e, coef_w, *terms = call(
        edge_kernel, [edge, edge, edge, edge, strip] + [edge] * 8,
        (w, left, right, east, west, to_e, to_w, in_a, in_b), product // 8, "edges",
    )
    in_a2, in_b2, in_l2 = exchange(to_a2, to_b2, to_l2)
    q, w, aw, sums = call(
        middle_kernel, [field, field, field, shape((5, 8, cols))],
        (z, r, q, w, ef, nf, wet, *terms, rz), product, "middle",
    )
    packed, *outer = call(
        sums_kernel, [shape((lons * lats, EDGE)), edge, edge, strip],
        (sums, east, west, coef_e, coef_w, to_l, to_l2, in_l, in_l2, in_a2, in_b2), rows * cols, "sums",
    )
    everyone = lax.all_to_all(packed, ("lon", "lat"), 0, 0, tiled=True)
    return tuple(
        call(
            last_kernel, [field, jax.ShapeDtypeStruct((rows, cols), BF16)],
            (everyone, r, z, w, q, aw, left, right, *outer), product, "last",
            [pltpu.VMEM((rows, cols), F32), pltpu.VMEM((rows, cols), BF16),
             pltpu.SemaphoreType.DMA((2 * tile_rows,))],
            out_space=pltpu.HBM,
        )
    )


def solution(mesh):
    tiles = P("lat", "lon", None, None)
    cells = P("lat", "lon")
    return jax.shard_map(
        per_device,
        mesh=mesh,
        in_specs=(cells, cells, cells, tiles, tiles, cells),
        out_specs=(cells, cells),
        check_vma=False,
    )
```

```python
import functools

import jax
import jax.numpy as jnp
from jax import lax
from jax.experimental import pallas as pl
from jax.experimental.pallas import tpu as pltpu
from jax.sharding import PartitionSpec as P

EDGE = 128
CELLS = 2 * EDGE
surface_term = 0.0001
F32 = jnp.float32
BF16 = jnp.bfloat16
VMEM_LIMIT = 32 * 1024 * 1024
ROWS = 16


def dot(left, right):
    return jnp.dot(left, right, preferred_element_type=F32)


def dot_nt(left, right):
    return lax.dot_general(left, right, (((1,), (1,)), ((), ())), preferred_element_type=F32)


def lane_index(rows, cols):
    return lax.broadcasted_iota(jnp.int32, (rows, cols), 1)


def row_index(rows, cols):
    return lax.broadcasted_iota(jnp.int32, (rows, cols), 0)


def rounded_product(left, tile, right):
    partial = dot(left, tile).astype(BF16)
    return dot(partial, right).astype(BF16)


def split(value):
    high = value.astype(BF16)
    return high, (value - high.astype(F32)).astype(BF16)


def wide_product(left, tile, right):
    partial = dot(jnp.concatenate([left, left], axis=1), jnp.concatenate(split(tile), axis=0))
    return dot(jnp.concatenate(split(partial), axis=1), jnp.concatenate([right, right], axis=0))


def fold(block):
    total = block[0:8]
    for k in range(1, block.shape[0] // 8):
        total = total + block[8 * k : 8 * k + 8]
    return total


def column(rows_ref, i):
    return jnp.broadcast_to(rows_ref[i : i + 1, :], (EDGE, EDGE)).T


def on_low_band():
    return lax.axis_index("lat") == 0


def on_odd_sector():
    return lax.axis_index("lon") % 2 == 1


def pair_up(to_e, to_w):
    odd = on_odd_sector()
    return jnp.where(odd, to_e, to_w), jnp.where(odd, to_w, to_e)


def stencil(i, tile_rows, field_ref, ef_ref, nf_ref, wet_ref, south_flux, top_flux):
    rows = slice(i * EDGE, (i + 1) * EDGE)
    field = field_ref[rows, :]
    wet = wet_ref[i : i + 1, :]
    lane = lane_index(1, CELLS)
    both = wet * pltpu.roll(wet, EDGE, 1)
    east_wet = jnp.where(lane == EDGE - 1, both, jnp.where(lane == CELLS - 1, 0.0, wet))
    flux_e = (ef_ref[rows, :].astype(F32) * east_wet) * (field - pltpu.roll(field, CELLS - 1, 1))
    flux_w = pltpu.roll(flux_e, 1, 1)
    row = row_index(EDGE, CELLS)
    above = min((i + 1) * EDGE, tile_rows * EDGE - 1)
    north = jnp.where(row == EDGE - 1, field_ref[above : above + 1, :], pltpu.roll(field, EDGE - 1, 0))
    flux_n = (nf_ref[rows, :].astype(F32) * wet) * (field - north)
    if i == tile_rows - 1:
        last = top_flux
    else:
        last = flux_n[EDGE - 1 :, :] * wet_ref[i + 1 : i + 2, :]
    flux_n = jnp.where(row == EDGE - 1, last, flux_n)
    flux_s = jnp.where(row == 0, south_flux, pltpu.roll(flux_n, 1, 0))
    return field, surface_term * field + (flux_e - flux_w) + (flux_n - flux_s), last


def lat_flux(coef, own, other):
    flux = coef * (own - other)
    low = on_low_band()
    return jnp.where(low, flux, 0.0), jnp.where(low, 0.0, -flux)


def edge_rows(i, block, east_ref, west_ref):
    west_ref[i : i + 1, :] = block[:, :EDGE].T[0:1, :]
    east_ref[i : i + 1, :] = block[:, EDGE:].T[EDGE - 1 :, :]


def boundary_row(ref):
    return jnp.where(on_low_band(), ref[ref.shape[0] - 1 :, :], ref[0:1, :])


def near_side():
    return lax.axis_index("lon") % 2


def near_kernel(
    wet_hbm, rhs_hbm, left_hbm, right_hbm, ef_hbm, nf_hbm,
    rhs_ref, left_ref, right_ref, ef_ref, nf_ref, wet_ref, near_ref, to_a, sum_ref, list_ref, flags_ref, sems,
):
    tile_rows = rhs_hbm.shape[0] // EDGE
    tiles = 2 * tile_rows
    side = near_side()
    used = [0]

    def load(source, target):
        copy = pltpu.make_async_copy(source, target, sems.at[used[0]])
        used[0] += 1
        copy.start()
        return copy

    def load_column(at, first, count):
        rows = pl.ds(first * EDGE, count * EDGE)
        some = pl.ds(first, count)
        place = pl.ds(pl.multiple_of(at * EDGE, EDGE), EDGE)
        return [
            load(rhs_hbm.at[rows, place], rhs_ref.at[rows, place]),
            load(left_hbm.at[some, at], left_ref.at[some, at]),
            load(right_hbm.at[some, at], right_ref.at[some, at]),
        ]

    listing = load(wet_hbm, list_ref)
    head = tile_rows // 3
    near = {0: load_column(side, 0, head), head: load_column(side, head, tile_rows - head)}
    near[head].append(load(ef_hbm.at[:, pl.ds(EDGE, EDGE)], ef_ref.at[:, pl.ds(EDGE, EDGE)]))
    rest = load_column(1 - side, 0, tile_rows)
    rest.append(load(ef_hbm.at[:, pl.ds(0, EDGE)], ef_ref.at[:, pl.ds(0, EDGE)]))
    rest.append(load(nf_hbm, nf_ref))
    wet_ref[...] = jnp.zeros_like(wet_ref)
    to_a[...] = jnp.zeros_like(to_a)
    listing.wait()
    for t in range(flags_ref.shape[0]):
        flags_ref[t] = 0.0
    for k in range(tiles):
        flags_ref[list_ref[0, k]] = 1.0
    lane = lane_index(1, CELLS)
    for i in range(tile_rows):
        wet_ref[i : i + 1, :] = jnp.where(lane < EDGE, flags_ref[2 * i], flags_ref[2 * i + 1])
    total = jnp.zeros(sum_ref.shape, F32)
    odd = side == 1
    for i in range(tile_rows):
        for copy in near.get(i, ()):
            copy.wait()
        place = pl.ds(pl.multiple_of(side * EDGE, EDGE), EDGE)
        rows = slice(i * EDGE, (i + 1) * EDGE)
        residual = rhs_ref[rows, place] * wet_ref[i : i + 1, place]
        precond = rounded_product(left_ref[i, side], residual.astype(BF16), right_ref[i, side]).astype(F32)
        near_ref[rows, :] = precond
        turned = precond.T
        to_a[i : i + 1, :] = jnp.where(odd, turned[EDGE - 1 :, :], turned[0:1, :])
        total = total + fold(residual * precond)
    sum_ref[...] = total
    for i in range(tile_rows):
        face = ef_ref[i * EDGE : (i + 1) * EDGE, EDGE:].astype(F32).T[EDGE - 1 :, :]
        wet = wet_ref[i : i + 1, :]
        to_a[ROWS + i : ROWS + i + 1, :] = jnp.where(odd, face * wet[:, EDGE:], wet[:, :EDGE])
    for copy in rest:
        copy.wait()


def far_kernel(
    rhs_ref, left_ref, right_ref, ef_ref, nf_ref, wet_ref, near_ref, to_a, sum_in,
    z_ref, r_ref, to_e, to_w, to_b, to_l, sum_ref,
):
    tile_rows = rhs_ref.shape[0] // EDGE
    side = 1 - near_side()
    odd = side == 0
    to_b[...] = jnp.zeros_like(to_b)
    to_l[...] = jnp.zeros_like(to_l)
    total = jnp.zeros((8, EDGE), F32)
    place = pl.ds(pl.multiple_of(side * EDGE, EDGE), EDGE)
    other = pl.ds(pl.multiple_of((1 - side) * EDGE, EDGE), EDGE)
    for i in range(tile_rows):
        rows = slice(i * EDGE, (i + 1) * EDGE)
        wet = wet_ref[i : i + 1, :]
        residual = rhs_ref[rows, place] * wet_ref[i : i + 1, place]
        precond = rounded_product(left_ref[i, side], residual.astype(BF16), right_ref[i, side]).astype(F32)
        z_ref[rows, place] = precond
        z_ref[rows, other] = near_ref[rows, :]
        r_ref[rows, place] = residual
        r_ref[rows, other] = rhs_ref[rows, other] * wet_ref[i : i + 1, other]
        turned = precond.T
        to_b[i : i + 1, :] = jnp.where(odd, turned[0:1, :], turned[EDGE - 1 :, :])
        face = ef_ref[rows, EDGE:].astype(F32).T[EDGE - 1 :, :]
        to_b[ROWS + i : ROWS + i + 1, :] = jnp.where(odd, wet[:, :EDGE], face * wet[:, EDGE:])
        total = total + fold(residual * precond)
    sum_ref[...] = jnp.concatenate([total, sum_in[...]], axis=1)
    to_l[0:1, :] = boundary_row(z_ref)
    rows = tile_rows * EDGE
    last = nf_ref[rows - 16 : rows, :].astype(F32)[15:16, :] * wet_ref[tile_rows - 1 : tile_rows, :]
    to_l[1:2, :] = jnp.where(on_low_band(), last, wet_ref[0:1, :])
    to_e[...] = jnp.where(odd, to_a[...], to_b[...])
    to_w[...] = jnp.where(odd, to_b[...], to_a[...])


def inner_kernel(z_ref, left_ref, right_ref, ef_ref, nf_ref, wet_ref, to_l, in_l, q_ref, w_ref, east_ref, west_ref):
    tile_rows = z_ref.shape[0] // EDGE
    east_ref[...] = jnp.zeros_like(east_ref)
    west_ref[...] = jnp.zeros_like(west_ref)
    top, south = lat_flux(to_l[1:2, :] * in_l[1:2, :], to_l[0:1, :], in_l[0:1, :])
    for i in range(tile_rows):
        rows = slice(i * EDGE, (i + 1) * EDGE)
        _, image, south = stencil(i, tile_rows, z_ref, ef_ref, nf_ref, wet_ref, south, top)
        q_ref[rows, :] = image
        parts = [
            wide_product(left_ref[i, k], image[:, k * EDGE : (k + 1) * EDGE], right_ref[i, k])
            for k in range(2)
        ]
        product = jnp.concatenate(parts, axis=1)
        w_ref[rows, :] = product
        edge_rows(i, product, east_ref, west_ref)


def edge_kernel(
    w_ref, left_ref, right_ref, east_in, west_in, to_e, to_w, in_a, in_b,
    east_ref, west_ref, to_a, to_b, to_l, coef_e, coef_w, flux_e, flux_w, turn_e, turn_w, right_e, right_w,
):
    tile_rows = w_ref.shape[0] // EDGE
    odd = on_odd_sector()
    from_e = jnp.where(odd, in_a[...], in_b[...])
    from_w = jnp.where(odd, in_b[...], in_a[...])
    coef_e[...] = to_e[ROWS:, :] * from_e[ROWS:, :]
    coef_w[...] = to_w[ROWS:, :] * from_w[ROWS:, :]
    flux_e[...] = coef_e[...] * (to_e[:ROWS, :] - from_e[:ROWS, :])
    flux_w[...] = coef_w[...] * (to_w[:ROWS, :] - from_w[:ROWS, :])
    for ref in (turn_e, turn_w, right_e, right_w, to_l):
        ref[...] = jnp.zeros_like(ref)
    spread = jnp.concatenate(split(flux_e[...]) + split(flux_w[...]), axis=0)
    for i in range(tile_rows):
        moved_e = dot_nt(spread[: 2 * ROWS], left_ref[i, 1])
        moved_w = dot_nt(spread[2 * ROWS :], left_ref[i, 0])
        turn_e[i : i + 1, :] = moved_e[i : i + 1, :] + moved_e[ROWS + i : ROWS + i + 1, :]
        turn_w[i : i + 1, :] = moved_w[i : i + 1, :] + moved_w[ROWS + i : ROWS + i + 1, :]
        right_e[i : i + 1, :] = right_ref[i, 1, EDGE - 16 :, :].astype(F32)[15:16, :]
        right_w[i : i + 1, :] = right_ref[i, 0, 0:16, :].astype(F32)[0:1, :]
    east_ref[...] = east_in[...] + turn_e[...] * right_e[:, EDGE - 1 :]
    west_ref[...] = west_in[...] + turn_w[...] * right_w[:, 0:1]
    to_a[...], to_b[...] = pair_up(east_ref[...], west_ref[...])
    low = on_low_band()
    end = tile_rows - 1
    by_e = jnp.where(low, turn_e[end : end + 1, EDGE - 1 :] * right_e[end : end + 1, :], turn_e[0:1, 0:1] * right_e[0:1, :])
    by_w = jnp.where(low, turn_w[end : end + 1, EDGE - 1 :] * right_w[end : end + 1, :], turn_w[0:1, 0:1] * right_w[0:1, :])
    to_l[0:1, :] = boundary_row(w_ref) + jnp.concatenate([by_w, by_e], axis=1)


def middle_kernel(
    z_ref, r_ref, q_in, w_in, ef_ref, nf_ref, wet_ref, flux_e, flux_w, turn_e, turn_w, right_e, right_w, sum_in,
    q_ref, w_ref, aw_ref, sums_ref,
):
    tile_rows = z_ref.shape[0] // EDGE
    lane = lane_index(EDGE, EDGE)
    zero = jnp.zeros((8, CELLS), F32)
    zq, rw, qw, waw = zero, zero, zero, zero

    def complete(i, zq, rw, qw):
        rows = slice(i * EDGE, (i + 1) * EDGE)
        image = q_in[rows, :] + jnp.concatenate(
            [jnp.where(lane == 0, column(flux_w, i), 0.0), jnp.where(lane == EDGE - 1, column(flux_e, i), 0.0)], axis=1
        )
        product = w_in[rows, :] + jnp.concatenate(
            [column(turn_w, i) * right_w[i : i + 1, :], column(turn_e, i) * right_e[i : i + 1, :]], axis=1
        )
        q_ref[rows, :] = image
        w_ref[rows, :] = product
        return zq + fold(z_ref[rows, :] * image), rw + fold(r_ref[rows, :] * product), qw + fold(image * product)

    south = jnp.zeros((1, CELLS), F32)
    top = south
    zq, rw, qw = complete(0, zq, rw, qw)
    for i in range(tile_rows):
        if i + 1 < tile_rows:
            zq, rw, qw = complete(i + 1, zq, rw, qw)
        field, image, south = stencil(i, tile_rows, w_ref, ef_ref, nf_ref, wet_ref, south, top)
        aw_ref[i * EDGE : (i + 1) * EDGE, :] = image
        waw = waw + fold(field * image)
    for k, total in enumerate((sum_in[...], zq, rw, qw, waw)):
        sums_ref[k] = total


def sums_kernel(
    sums_in, east_ref, west_ref, coef_e, coef_w, own_l, own_l2, in_l, in_l2, in_a, in_b,
    packed_ref, flux_e, flux_w, flux_l,
):
    odd = on_odd_sector()
    from_e = jnp.where(odd, in_a[...], in_b[...])
    from_w = jnp.where(odd, in_b[...], in_a[...])
    flux_e[...] = coef_e[...] * (east_ref[...] - from_e)
    flux_w[...] = coef_w[...] * (west_ref[...] - from_w)
    top, bottom = lat_flux(own_l[1:2, :] * in_l[1:2, :], own_l2[0:1, :], in_l2[0:1, :])
    flux_l[...] = jnp.zeros_like(flux_l)
    flux_l[0:1, :] = top
    flux_l[1:2, :] = -bottom
    outer = flux_e[...] * east_ref[...] + flux_w[...] * west_ref[...]
    across = (top - bottom) * own_l2[0:1, :]
    extra = jnp.sum(jnp.sum(outer, axis=0, keepdims=True), axis=1, keepdims=True)
    extra = extra + jnp.sum(across, axis=1, keepdims=True)
    lane = lane_index(1, EDGE)
    packed = jnp.zeros((1, EDGE), F32)
    for k in range(5):
        value = jnp.sum(jnp.sum(sums_in[k], axis=0, keepdims=True), axis=1, keepdims=True)
        packed = jnp.where(lane == k, value + extra if k == 4 else value, packed)
    packed_ref[...] = jnp.broadcast_to(packed, packed_ref.shape)


def last_kernel(
    all_ref, r_ref, z_ref, w_ref, q_ref, aw_ref, left_ref, right_ref, flux_e, flux_w, flux_l,
    sol_hbm, pre_hbm, sol_ref, pre_ref, sems,
):
    tile_rows = z_ref.shape[0] // EDGE
    totals = jnp.sum(all_ref[...], axis=0, keepdims=True)
    lane = lane_index(1, EDGE)
    rz, zq, rw, qw, waw = (jnp.sum(jnp.where(lane == k, totals, 0.0), axis=1, keepdims=True) for k in range(5))
    step0 = rz / zq
    rz1 = step0 * (step0 * qw - rw)
    grow = 1.0 + rz1 / rz
    step1 = rz1 / (grow * grow * zq - 2.0 * grow * step0 * qw + step0 * step0 * waw)
    with_z = step0 + step1 * grow
    with_w = -step1 * step0
    row = row_index(EDGE, CELLS)
    lane = lane_index(EDGE, EDGE)
    stores = []
    for i in range(tile_rows):
        rows = slice(i * EDGE, (i + 1) * EDGE)
        sol_ref[rows, :] = with_z * z_ref[rows, :] + with_w * w_ref[rows, :]
        outer = jnp.concatenate(
            [jnp.where(lane == 0, column(flux_w, i), 0.0), jnp.where(lane == EDGE - 1, column(flux_e, i), 0.0)], axis=1
        )
        if i == 0:
            outer = outer + jnp.where(row == 0, flux_l[1:2, :], 0.0)
        if i == tile_rows - 1:
            outer = outer + jnp.where(row == EDGE - 1, flux_l[0:1, :], 0.0)
        residual = r_ref[rows, :] - with_z * q_ref[rows, :] - with_w * (aw_ref[rows, :] + outer)
        rounded = residual.astype(BF16)
        parts = [
            rounded_product(left_ref[i, k], rounded[:, k * EDGE : (k + 1) * EDGE], right_ref[i, k])
            for k in range(2)
        ]
        pre_ref[rows, :] = jnp.concatenate(parts, axis=1)
        place = pl.ds(i * EDGE, EDGE)
        for k, (source, target) in enumerate(((sol_ref, sol_hbm), (pre_ref, pre_hbm))):
            copy = pltpu.make_async_copy(source.at[place], target.at[place], sems.at[2 * i + k])
            copy.start()
            stores.append(copy)
    for copy in stores:
        copy.wait()


def call(kernel, outs, args, flops, name, scratch=(), in_space=pltpu.VMEM, out_space=pltpu.VMEM):
    moved = sum(a.size * a.dtype.itemsize for a in args) + sum(o.size * o.dtype.itemsize for o in outs)
    return pl.pallas_call(
        kernel,
        out_shape=outs,
        in_specs=[pl.BlockSpec(memory_space=in_space)] * len(args),
        out_specs=[pl.BlockSpec(memory_space=out_space)] * len(outs),
        scratch_shapes=scratch,
        compiler_params=pltpu.CompilerParams(vmem_limit_bytes=VMEM_LIMIT),
        cost_estimate=pl.CostEstimate(flops=0, bytes_accessed=0, transcendentals=0),
        name=name,
    )(*args)


def per_device(right_side, east_face, north_face, left_factor, right_factor, wet_list):
    rows, cols = right_side.shape
    lons, lats = lax.axis_size("lon"), lax.axis_size("lat")
    tile_rows = rows // EDGE
    shape = functools.partial(jax.ShapeDtypeStruct, dtype=F32)
    like = lambda a: jax.ShapeDtypeStruct(a.shape, a.dtype)
    field = shape((rows, cols))
    edge = shape((ROWS, EDGE))
    message = shape((2 * ROWS, EDGE))
    strip = shape((8, cols))
    across = [(0, 1), (1, 0)]

    def pairs(parity):
        forward = [(i, (i + 1) % lons) for i in range(parity, lons, 2)]
        return forward + [(b, a) for a, b in forward]

    def exchange(to_a, to_b, to_l):
        in_a = lax.ppermute(to_a, "lon", pairs(1))
        in_b = lax.ppermute(to_b, "lon", pairs(0))
        return in_a, in_b, lax.ppermute(to_l, "lat", across)

    product = 4 * rows * cols * EDGE
    by_place = (tile_rows, 2, EDGE, EDGE)
    left_factor, right_factor = left_factor.reshape(by_place), right_factor.reshape(by_place)
    arguments = [
        pltpu.with_memory_space_constraint(a, pltpu.HBM)
        for a in (wet_list, right_side, left_factor, right_factor, east_face, north_face)
    ]
    rhs, left, right, ef, nf, wet, near, to_a, rz = call(
        near_kernel,
        [field, like(left_factor), like(right_factor), like(east_face), like(north_face), shape((ROWS, cols)),
         shape((rows, EDGE)), message, shape((8, EDGE))],
        arguments, product // 2, "near",
        [pltpu.SMEM(wet_list.shape, jnp.int32), pltpu.SMEM((32,), F32), pltpu.SemaphoreType.DMA((16,))],
        in_space=pltpu.HBM,
    )
    in_a = lax.ppermute(to_a, "lon", pairs(1))
    z, r, to_e, to_w, to_b, to_l, rz = call(
        far_kernel, [field, field, message, message, message, strip, strip],
        (rhs, left, right, ef, nf, wet, near, to_a, rz), product // 2, "far",
    )
    in_b = lax.ppermute(to_b, "lon", pairs(0))
    in_l = lax.ppermute(to_l, "lat", across)
    q, w, east, west = call(
        inner_kernel, [field, field, edge, edge], (z, left, right, ef, nf, wet, to_l, in_l), 2 * product, "inner"
    )
    east, west, to_a2, to_b2, to_l2, coef_e, coef_w, *terms = call(
        edge_kernel, [edge, edge, edge, edge, strip] + [edge] * 8,
        (w, left, right, east, west, to_e, to_w, in_a, in_b), product // 8, "edges",
    )
    in_a2, in_b2, in_l2 = exchange(to_a2, to_b2, to_l2)
    q, w, aw, sums = call(
        middle_kernel, [field, field, field, shape((5, 8, cols))],
        (z, r, q, w, ef, nf, wet, *terms, rz), product, "middle",
    )
    packed, *outer = call(
        sums_kernel, [shape((lons * lats, EDGE)), edge, edge, strip],
        (sums, east, west, coef_e, coef_w, to_l, to_l2, in_l, in_l2, in_a2, in_b2), rows * cols, "sums",
    )
    everyone = lax.all_to_all(packed, ("lon", "lat"), 0, 0, tiled=True)
    return tuple(
        call(
            last_kernel, [field, jax.ShapeDtypeStruct((rows, cols), BF16)],
            (everyone, r, z, w, q, aw, left, right, *outer), product, "last",
            [pltpu.VMEM((rows, cols), F32), pltpu.VMEM((rows, cols), BF16),
             pltpu.SemaphoreType.DMA((2 * tile_rows,))],
            out_space=pltpu.HBM,
        )
    )


def solution(mesh):
    tiles = P("lat", "lon", None, None)
    cells = P("lat", "lon")
    return jax.shard_map(
        per_device,
        mesh=mesh,
        in_specs=(cells, cells, cells, tiles, tiles, cells),
        out_specs=(cells, cells),
        check_vma=False,
    )
```

```python
import functools

import jax
import jax.numpy as jnp
from jax import lax
from jax.experimental import pallas as pl
from jax.experimental.pallas import tpu as pltpu
from jax.sharding import PartitionSpec as P

EDGE = 128
CELLS = 2 * EDGE
surface_term = 0.0001
F32 = jnp.float32
BF16 = jnp.bfloat16
VMEM_LIMIT = 8 * 1024 * 1024
ROWS = 16


def dot(left, right):
    return jnp.dot(left, right, preferred_element_type=F32)


def dot_nt(left, right):
    return lax.dot_general(left, right, (((1,), (1,)), ((), ())), preferred_element_type=F32)


def lane_index(rows, cols):
    return lax.broadcasted_iota(jnp.int32, (rows, cols), 1)


def row_index(rows, cols):
    return lax.broadcasted_iota(jnp.int32, (rows, cols), 0)


def rounded_product(left, tile, right):
    partial = dot(left, tile).astype(BF16)
    return dot(partial, right).astype(BF16)


def split(value):
    high = value.astype(BF16)
    return high, (value - high.astype(F32)).astype(BF16)


def wide_product(left, tile, right):
    partial = dot(jnp.concatenate([left, left], axis=1), jnp.concatenate(split(tile), axis=0))
    return dot(jnp.concatenate(split(partial), axis=1), jnp.concatenate([right, right], axis=0))


def fold(block):
    total = block[0:8]
    for k in range(1, block.shape[0] // 8):
        total = total + block[8 * k : 8 * k + 8]
    return total


def column(rows_ref, i):
    return jnp.broadcast_to(rows_ref[i : i + 1, :], (EDGE, EDGE)).T


def on_low_band():
    return lax.axis_index("lat") == 0


def on_odd_sector():
    return lax.axis_index("lon") % 2 == 1


def set_row(block, at, value):
    row = row_index(8, CELLS)
    if at == 0:
        return jnp.concatenate([jnp.where(row == 0, value, block[:8]), block[8:]], axis=0)
    return jnp.concatenate([block[:-8], jnp.where(row == 7, value, block[-8:])], axis=0)


def differences(i, tile_rows, field_ref, wet_ref):
    field = field_ref[i * EDGE : (i + 1) * EDGE, :]
    wet = wet_ref[i : i + 1, :]
    lane = lane_index(1, CELLS)
    both = wet * pltpu.roll(wet, EDGE, 1)
    east_wet = jnp.where(lane == EDGE - 1, both, jnp.where(lane == CELLS - 1, 0.0, 1.0))
    above = min((i + 1) * EDGE, tile_rows * EDGE - 1)
    north = set_row(pltpu.roll(field, EDGE - 1, 0), -1, field_ref[above : above + 1, :])
    north_wet = wet * wet_ref[i + 1 : i + 2, :]
    return field, field - pltpu.roll(field, CELLS - 1, 1), field - north, east_wet, north_wet


def stencil(i, tile_rows, field_ref, ef_ref, nf_ref, wet_ref, south_flux, top_flux):
    rows = slice(i * EDGE, (i + 1) * EDGE)
    field, over_e, over_n, east_wet, north_wet = differences(i, tile_rows, field_ref, wet_ref)
    flux_e = (ef_ref[rows, :].astype(F32) * east_wet) * over_e
    flux_n = nf_ref[rows, :].astype(F32) * over_n
    last = top_flux if i == tile_rows - 1 else flux_n[EDGE - 1 :, :] * north_wet
    flux_n = set_row(flux_n, -1, last)
    flux_s = set_row(pltpu.roll(flux_n, 1, 0), 0, south_flux)
    image = surface_term * field + (flux_e - pltpu.roll(flux_e, 1, 1)) + (flux_n - flux_s)
    return field, image, last


def lat_flux(coef, own, other):
    flux = coef * (own - other)
    low = on_low_band()
    return jnp.where(low, flux, 0.0), jnp.where(low, 0.0, -flux)


def edge_rows(i, block, east_ref, west_ref):
    west_ref[i : i + 1, :] = block[:, :EDGE].T[0:1, :]
    east_ref[i : i + 1, :] = block[:, EDGE:].T[EDGE - 1 :, :]


def boundary_row(ref):
    return jnp.where(on_low_band(), ref[ref.shape[0] - 1 :, :], ref[0:1, :])


def near_side():
    return lax.axis_index("lon") % 2


def near_kernel(
    wet_hbm, rhs_hbm, left_hbm, right_hbm, ef_hbm, nf_hbm,
    rhs_ref, left_ref, right_ref, ef_ref, nf_ref, wet_ref, near_ref, to_a, sum_ref, list_ref, flags_ref, sems,
):
    tile_rows = rhs_hbm.shape[0] // EDGE
    tiles = 2 * tile_rows
    side = near_side()
    used = [0]

    def load(source, target):
        copy = pltpu.make_async_copy(source, target, sems.at[used[0]])
        used[0] += 1
        copy.start()
        return copy

    def load_column(at, first, count):
        rows = pl.ds(first * EDGE, count * EDGE)
        some = pl.ds(first, count)
        place = pl.ds(pl.multiple_of(at * EDGE, EDGE), EDGE)
        return [
            load(rhs_hbm.at[rows, place], rhs_ref.at[rows, place]),
            load(left_hbm.at[some, at], left_ref.at[some, at]),
            load(right_hbm.at[some, at], right_ref.at[some, at]),
        ]

    listing = load(wet_hbm, list_ref)
    head = tile_rows // 3
    near = {0: load_column(side, 0, head), head: load_column(side, head, tile_rows - head)}
    near[head].append(load(ef_hbm.at[:, pl.ds(EDGE, EDGE)], ef_ref.at[:, pl.ds(EDGE, EDGE)]))
    rest = load_column(1 - side, 0, tile_rows)
    rest.append(load(ef_hbm.at[:, pl.ds(0, EDGE)], ef_ref.at[:, pl.ds(0, EDGE)]))
    rest.append(load(nf_hbm, nf_ref))
    wet_ref[...] = jnp.zeros_like(wet_ref)
    to_a[...] = jnp.zeros_like(to_a)
    listing.wait()
    for t in range(flags_ref.shape[0]):
        flags_ref[t] = 0.0
    for k in range(tiles):
        flags_ref[list_ref[0, k]] = 1.0
    lane = lane_index(1, CELLS)
    for i in range(tile_rows):
        wet_ref[i : i + 1, :] = jnp.where(lane < EDGE, flags_ref[2 * i], flags_ref[2 * i + 1])
    total = jnp.zeros(sum_ref.shape, F32)
    odd = side == 1
    for i in range(tile_rows):
        for copy in near.get(i, ()):
            copy.wait()
        place = pl.ds(pl.multiple_of(side * EDGE, EDGE), EDGE)
        rows = slice(i * EDGE, (i + 1) * EDGE)
        residual = rhs_ref[rows, place] * wet_ref[i : i + 1, place]
        precond = rounded_product(left_ref[i, side], residual.astype(BF16), right_ref[i, side]).astype(F32)
        near_ref[rows, :] = precond
        turned = precond.T
        to_a[i : i + 1, :] = jnp.where(odd, turned[EDGE - 1 :, :], turned[0:1, :])
        total = total + fold(residual * precond)
    sum_ref[...] = total
    for i in range(tile_rows):
        face = ef_ref[i * EDGE : (i + 1) * EDGE, EDGE:].astype(F32).T[EDGE - 1 :, :]
        wet = wet_ref[i : i + 1, :]
        to_a[ROWS + i : ROWS + i + 1, :] = jnp.where(odd, face * wet[:, EDGE:], wet[:, :EDGE])
    for copy in rest:
        copy.wait()


def far_kernel(
    rhs_ref, left_ref, right_ref, ef_ref, nf_ref, wet_ref, near_ref, to_a, sum_in,
    z_ref, short_ref, r_ref, to_e, to_w, to_b, to_l, sum_ref,
):
    tile_rows = rhs_ref.shape[0] // EDGE
    side = 1 - near_side()
    odd = side == 0
    to_b[...] = jnp.zeros_like(to_b)
    to_l[...] = jnp.zeros_like(to_l)
    total = jnp.zeros((8, EDGE), F32)
    place = pl.ds(pl.multiple_of(side * EDGE, EDGE), EDGE)
    other = pl.ds(pl.multiple_of((1 - side) * EDGE, EDGE), EDGE)
    for i in range(tile_rows):
        rows = slice(i * EDGE, (i + 1) * EDGE)
        wet = wet_ref[i : i + 1, :]
        residual = rhs_ref[rows, place] * wet_ref[i : i + 1, place]
        precond = rounded_product(left_ref[i, side], residual.astype(BF16), right_ref[i, side]).astype(F32)
        z_ref[rows, place] = precond
        z_ref[rows, other] = near_ref[rows, :]
        short_ref[rows, place] = precond.astype(BF16)
        short_ref[rows, other] = near_ref[rows, :].astype(BF16)
        r_ref[rows, place] = residual
        r_ref[rows, other] = rhs_ref[rows, other] * wet_ref[i : i + 1, other]
        turned = precond.T
        to_b[i : i + 1, :] = jnp.where(odd, turned[0:1, :], turned[EDGE - 1 :, :])
        face = ef_ref[rows, EDGE:].astype(F32).T[EDGE - 1 :, :]
        to_b[ROWS + i : ROWS + i + 1, :] = jnp.where(odd, wet[:, :EDGE], face * wet[:, EDGE:])
        total = total + fold(residual * precond)
    sum_ref[...] = jnp.concatenate([total, sum_in[...]], axis=1)
    to_l[0:1, :] = boundary_row(z_ref)
    rows = tile_rows * EDGE
    last = nf_ref[rows - 16 : rows, :].astype(F32)[15:16, :] * wet_ref[tile_rows - 1 : tile_rows, :]
    to_l[1:2, :] = jnp.where(on_low_band(), last, wet_ref[0:1, :])
    to_e[...] = jnp.where(odd, to_a[...], to_b[...])
    to_w[...] = jnp.where(odd, to_b[...], to_a[...])


def inner_kernel(z_ref, left_ref, right_ref, ef_ref, nf_ref, wet_ref, to_l, in_l, q_ref, w_ref, east_ref, west_ref):
    tile_rows = z_ref.shape[0] // EDGE
    east_ref[...] = jnp.zeros_like(east_ref)
    west_ref[...] = jnp.zeros_like(west_ref)
    top, south = lat_flux(to_l[1:2, :] * in_l[1:2, :], to_l[0:1, :], in_l[0:1, :])
    for i in range(tile_rows):
        rows = slice(i * EDGE, (i + 1) * EDGE)
        _, image, south = stencil(i, tile_rows, z_ref, ef_ref, nf_ref, wet_ref, south, top)
        q_ref[rows, :] = image
        parts = [
            wide_product(left_ref[i, k], image[:, k * EDGE : (k + 1) * EDGE], right_ref[i, k])
            for k in range(2)
        ]
        product = jnp.concatenate(parts, axis=1)
        w_ref[rows, :] = product
        edge_rows(i, product, east_ref, west_ref)


def edge_kernel(
    w_ref, left_ref, right_ref, east_in, west_in, to_e, to_w, in_a, in_b,
    east_ref, west_ref, to_l, coef_e, coef_w, flux_e, flux_w, turn_e, turn_w, right_e, right_w,
):
    tile_rows = w_ref.shape[0] // EDGE
    odd = on_odd_sector()
    from_e = jnp.where(odd, in_a[...], in_b[...])
    from_w = jnp.where(odd, in_b[...], in_a[...])
    coef_e[...] = to_e[ROWS:, :] * from_e[ROWS:, :]
    coef_w[...] = to_w[ROWS:, :] * from_w[ROWS:, :]
    flux_e[...] = coef_e[...] * (to_e[:ROWS, :] - from_e[:ROWS, :])
    flux_w[...] = coef_w[...] * (to_w[:ROWS, :] - from_w[:ROWS, :])
    for ref in (turn_e, turn_w, right_e, right_w, to_l):
        ref[...] = jnp.zeros_like(ref)
    spread = jnp.concatenate(split(flux_e[...]) + split(flux_w[...]), axis=0)
    for i in range(tile_rows):
        moved_e = dot_nt(spread[: 2 * ROWS], left_ref[i, 1])
        moved_w = dot_nt(spread[2 * ROWS :], left_ref[i, 0])
        turn_e[i : i + 1, :] = moved_e[i : i + 1, :] + moved_e[ROWS + i : ROWS + i + 1, :]
        turn_w[i : i + 1, :] = moved_w[i : i + 1, :] + moved_w[ROWS + i : ROWS + i + 1, :]
        right_e[i : i + 1, :] = right_ref[i, 1, EDGE - 16 :, :].astype(F32)[15:16, :]
        right_w[i : i + 1, :] = right_ref[i, 0, 0:16, :].astype(F32)[0:1, :]
    east_ref[...] = east_in[...] + turn_e[...] * right_e[:, EDGE - 1 :]
    west_ref[...] = west_in[...] + turn_w[...] * right_w[:, 0:1]
    low = on_low_band()
    end = tile_rows - 1
    by_e = jnp.where(low, turn_e[end : end + 1, EDGE - 1 :] * right_e[end : end + 1, :], turn_e[0:1, 0:1] * right_e[0:1, :])
    by_w = jnp.where(low, turn_w[end : end + 1, EDGE - 1 :] * right_w[end : end + 1, :], turn_w[0:1, 0:1] * right_w[0:1, :])
    to_l[0:1, :] = boundary_row(w_ref) + jnp.concatenate([by_w, by_e], axis=1)


def middle_kernel(
    z_ref, r_ref, q_ref, w_in, ef_ref, nf_ref, wet_ref, turn_e, turn_w, right_e, right_w, sum_in, w_ref, sums_ref
):
    tile_rows = z_ref.shape[0] // EDGE
    zero = jnp.zeros((8, CELLS), F32)
    zq, rw, qw, faces, squares = zero, zero, zero, zero, zero

    def complete(i, zq, rw, qw):
        rows = slice(i * EDGE, (i + 1) * EDGE)
        image = q_ref[rows, :]
        product = w_in[rows, :] + jnp.concatenate(
            [column(turn_w, i) * right_w[i : i + 1, :], column(turn_e, i) * right_e[i : i + 1, :]], axis=1
        )
        w_ref[rows, :] = product
        return zq + fold(z_ref[rows, :] * image), rw + fold(r_ref[rows, :] * product), qw + fold(image * product)

    zq, rw, qw = complete(0, zq, rw, qw)
    for i in range(tile_rows):
        if i + 1 < tile_rows:
            zq, rw, qw = complete(i + 1, zq, rw, qw)
        rows = slice(i * EDGE, (i + 1) * EDGE)
        field, over_e, over_n, east_wet, north_wet = differences(i, tile_rows, w_ref, wet_ref)
        by_e = ef_ref[rows, :].astype(F32) * east_wet * (over_e * over_e)
        by_n = nf_ref[rows, :].astype(F32) * (over_n * over_n)
        by_n = set_row(by_n, -1, 0.0 if i == tile_rows - 1 else by_n[EDGE - 1 :, :] * north_wet)
        faces = faces + fold(by_e + by_n)
        squares = squares + fold(field * field)
    for k, total in enumerate((sum_in[...], zq, rw, qw, faces + surface_term * squares)):
        sums_ref[k] = total


def sums_kernel(
    sums_in, east_ref, west_ref, to_e, to_w, flux_e1, flux_w1, coef_w, own_l, own_l2, in_l, in_l2, from_w,
    packed_ref, flux_w, flux_l,
):
    over_w = west_ref[...] - from_w[...]
    flux_w[...] = coef_w[...] * over_w
    top, bottom = lat_flux(own_l[1:2, :] * in_l[1:2, :], own_l2[0:1, :], in_l2[0:1, :])
    flux_l[...] = jnp.zeros_like(flux_l)
    flux_l[0:1, :] = top
    flux_l[1:2, :] = -bottom

    def total(value):
        return jnp.sum(jnp.sum(value, axis=0, keepdims=True), axis=1, keepdims=True)

    outer = {
        1: total(flux_e1[...] * to_e[:ROWS, :] + flux_w1[...] * to_w[:ROWS, :]),
        3: total(flux_e1[...] * east_ref[...] + flux_w1[...] * west_ref[...]),
        4: total(flux_w[...] * over_w) + total((top - bottom) * own_l2[0:1, :]),
    }
    lane = lane_index(1, EDGE)
    packed = jnp.zeros((1, EDGE), F32)
    for k in range(5):
        value = total(sums_in[k])
        packed = jnp.where(lane == k, value + outer[k] if k in outer else value, packed)
    packed_ref[...] = jnp.broadcast_to(packed, packed_ref.shape)


def outer_kernel(
    left_hbm, right_hbm, ef_hbm, nf_hbm, w_ref, wet_ref, east_ref, coef_e, from_e, flux_w, flux_l,
    u_ref, left_ref, right_ref, ef_ref, nf_ref, flux_e, sems,
):
    tile_rows = w_ref.shape[0] // EDGE
    step = tile_rows // 2
    loads = []
    for k in range(tile_rows // step):
        rows, some = pl.ds(k * step * EDGE, step * EDGE), pl.ds(k * step, step)
        group = [
            pltpu.make_async_copy(source.at[place], target.at[place], sems.at[4 * k + n])
            for n, (source, target, place) in enumerate(
                ((ef_hbm, ef_ref, rows), (nf_hbm, nf_ref, rows), (left_hbm, left_ref, some), (right_hbm, right_ref, some))
            )
        ]
        for copy in group:
            copy.start()
        loads.append(group)
    flux_e[...] = coef_e[...] * (east_ref[...] - from_e[...])
    lane = lane_index(EDGE, EDGE)
    south, top = -flux_l[1:2, :], flux_l[0:1, :]
    for i in range(tile_rows):
        if i % step == 0:
            for copy in loads[i // step]:
                copy.wait()
        _, image, south = stencil(i, tile_rows, w_ref, ef_ref, nf_ref, wet_ref, south, top)
        image = image + jnp.concatenate(
            [jnp.where(lane == 0, column(flux_w, i), 0.0), jnp.where(lane == EDGE - 1, column(flux_e, i), 0.0)], axis=1
        )
        parts = [
            wide_product(left_ref[i, k], image[:, k * EDGE : (k + 1) * EDGE], right_ref[i, k]) for k in range(2)
        ]
        u_ref[i * EDGE : (i + 1) * EDGE, :] = jnp.concatenate(parts, axis=1).astype(BF16)


def last_kernel(all_ref, z_ref, w_ref, u_ref, sol_hbm, pre_hbm, sol_ref, pre_ref, sems):
    tile_rows = z_ref.shape[0] // EDGE
    totals = jnp.sum(all_ref[...], axis=0, keepdims=True)
    lane = lane_index(1, EDGE)
    rz, zq, rw, qw, waw = (jnp.sum(jnp.where(lane == k, totals, 0.0), axis=1, keepdims=True) for k in range(5))
    step0 = rz / zq
    rz1 = step0 * (step0 * qw - rw)
    grow = 1.0 + rz1 / rz
    step1 = rz1 / (grow * grow * zq - 2.0 * grow * step0 * qw + step0 * step0 * waw)
    with_z = step0 + step1 * grow
    with_w = -step1 * step0
    group = 2 * EDGE
    stores = []
    for i in range(tile_rows * EDGE // group):
        rows = slice(i * group, (i + 1) * group)
        precond, product = z_ref[rows, :].astype(F32), w_ref[rows, :]
        sol_ref[rows, :] = with_z * precond + with_w * product
        pre_ref[rows, :] = (precond - with_z * product - with_w * u_ref[rows, :].astype(F32)).astype(BF16)
        place = pl.ds(i * group, group)
        for k, (source, target) in enumerate(((sol_ref, sol_hbm), (pre_ref, pre_hbm))):
            copy = pltpu.make_async_copy(source.at[place], target.at[place], sems.at[2 * i + k])
            copy.start()
            stores.append(copy)
    for copy in stores:
        copy.wait()


def call(kernel, outs, args, name, scratch=(), in_space=pltpu.VMEM, out_space=pltpu.VMEM, flops=0):
    if not isinstance(in_space, list):
        in_space = [in_space] * len(args)
    return pl.pallas_call(
        kernel,
        out_shape=outs,
        in_specs=[pl.BlockSpec(memory_space=space) for space in in_space],
        out_specs=[pl.BlockSpec(memory_space=out_space)] * len(outs),
        scratch_shapes=scratch,
        compiler_params=pltpu.CompilerParams(vmem_limit_bytes=VMEM_LIMIT),
        cost_estimate=pl.CostEstimate(flops=flops, bytes_accessed=0, transcendentals=0),
        name=name,
    )(*args)


def per_device(right_side, east_face, north_face, left_factor, right_factor, wet_list):
    rows, cols = right_side.shape
    lons, lats = lax.axis_size("lon"), lax.axis_size("lat")
    tile_rows = rows // EDGE
    shape = functools.partial(jax.ShapeDtypeStruct, dtype=F32)
    like = lambda a: jax.ShapeDtypeStruct(a.shape, a.dtype)
    field = shape((rows, cols))
    half = jax.ShapeDtypeStruct((rows, cols), BF16)
    edge = shape((ROWS, EDGE))
    message = shape((2 * ROWS, EDGE))
    strip = shape((8, cols))
    across = [(0, 1), (1, 0)]

    def pairs(parity):
        forward = [(i, (i + 1) % lons) for i in range(parity, lons, 2)]
        return forward + [(b, a) for a, b in forward]

    by_place = (tile_rows, 2, EDGE, EDGE)
    left_factor, right_factor = left_factor.reshape(by_place), right_factor.reshape(by_place)
    arguments = [
        pltpu.with_memory_space_constraint(a, pltpu.HBM)
        for a in (wet_list, right_side, left_factor, right_factor, east_face, north_face)
    ]
    rhs, left, right, ef, nf, wet, near, to_a, rz = call(
        near_kernel,
        [field, like(left_factor), like(right_factor), like(east_face), like(north_face), shape((ROWS, cols)),
         shape((rows, EDGE)), message, shape((8, EDGE))],
        arguments, "near",
        [pltpu.SMEM(wet_list.shape, jnp.int32), pltpu.SMEM((32,), F32), pltpu.SemaphoreType.DMA((16,))],
        in_space=pltpu.HBM,
    )
    in_a = lax.ppermute(to_a, "lon", pairs(1))
    z, short, r, to_e, to_w, to_b, to_l, rz = call(
        far_kernel, [field, half, field, message, message, message, strip, strip],
        (rhs, left, right, ef, nf, wet, near, to_a, rz), "far",
    )
    in_b = lax.ppermute(to_b, "lon", pairs(0))
    in_l = lax.ppermute(to_l, "lat", across)
    q, w, east, west = call(
        inner_kernel, [field, field, edge, edge], (z, left, right, ef, nf, wet, to_l, in_l), "inner"
    )
    east, west, to_l2, coef_e, coef_w, flux_e1, flux_w1, *terms = call(
        edge_kernel, [edge, edge, strip] + [edge] * 8,
        (w, left, right, east, west, to_e, to_w, in_a, in_b), "edges",
    )
    from_w2 = lax.ppermute(east, "lon", [(i, (i + 1) % lons) for i in range(lons)])
    in_l2 = lax.ppermute(to_l2, "lat", across)
    from_e2 = lax.ppermute(west, "lon", [((i + 1) % lons, i) for i in range(lons)])
    w, sums = call(
        middle_kernel, [field, shape((5, 8, cols))], (z, r, q, w, ef, nf, wet, *terms, rz), "middle"
    )
    packed, flux_w, flux_l = call(
        sums_kernel, [shape((lons * lats, EDGE)), edge, strip],
        (sums, east, west, to_e, to_w, flux_e1, flux_w1, coef_w, to_l, to_l2, in_l, in_l2, from_w2), "sums",
    )
    everyone = lax.all_to_all(packed, ("lon", "lat"), 0, 0, tiled=True)
    u = call(
        outer_kernel, [half],
        (*arguments[2:], w, wet, east, coef_e, from_e2, flux_w, flux_l), "outer",
        [pltpu.VMEM(a.shape, a.dtype) for a in arguments[2:]]
        + [pltpu.VMEM((ROWS, EDGE), F32), pltpu.SemaphoreType.DMA((8,))],
        in_space=[pltpu.HBM] * 4 + [pltpu.VMEM] * 7, flops=100_000_000_000,
    )[0]
    return tuple(
        call(
            last_kernel, [field, half], (everyone, short, w, u), "last",
            [pltpu.VMEM((rows, cols), F32), pltpu.VMEM((rows, cols), BF16), pltpu.SemaphoreType.DMA((tile_rows,))],
            out_space=pltpu.HBM,
        )
    )


def solution(mesh):
    tiles = P("lat", "lon", None, None)
    cells = P("lat", "lon")
    return jax.shard_map(
        per_device,
        mesh=mesh,
        in_specs=(cells, cells, cells, tiles, tiles, cells),
        out_specs=(cells, cells),
        check_vma=False,
    )
```

```python
import functools

import jax
import jax.numpy as jnp
from jax import lax
from jax.experimental import pallas as pl
from jax.experimental.pallas import tpu as pltpu
from jax.sharding import PartitionSpec as P

EDGE = 128
CELLS = 2 * EDGE
surface_term = 0.0001
F32 = jnp.float32
BF16 = jnp.bfloat16
VMEM_LIMIT = 8 * 1024 * 1024
CHUNKS = 3
ROWS = 16


def dot(left, right):
    return jnp.dot(left, right, preferred_element_type=F32)


def dot_nt(left, right):
    return lax.dot_general(left, right, (((1,), (1,)), ((), ())), preferred_element_type=F32)


def lane_index(rows, cols):
    return lax.broadcasted_iota(jnp.int32, (rows, cols), 1)


def row_index(rows, cols):
    return lax.broadcasted_iota(jnp.int32, (rows, cols), 0)


def rounded_product(left, tile, right):
    partial = dot(left, tile).astype(BF16)
    return dot(partial, right).astype(BF16)


def split(value):
    high = value.astype(BF16)
    return high, (value - high.astype(F32)).astype(BF16)


def wide_product(left, tile, right):
    partial = dot(jnp.concatenate([left, left], axis=1), jnp.concatenate(split(tile), axis=0))
    return dot(jnp.concatenate(split(partial), axis=1), jnp.concatenate([right, right], axis=0))


def fold(block):
    total = block[0:8]
    for k in range(1, block.shape[0] // 8):
        total = total + block[8 * k : 8 * k + 8]
    return total


def total(value):
    return jnp.sum(jnp.sum(value, axis=0, keepdims=True), axis=1, keepdims=True)


def column(rows_ref, i):
    return jnp.broadcast_to(rows_ref[i : i + 1, :], (EDGE, EDGE)).T


def on_low_band():
    return lax.axis_index("lat") == 0


def on_odd_sector():
    return lax.axis_index("lon") % 2 == 1


def set_row(block, at, value):
    row = row_index(8, CELLS)
    if at == 0:
        return jnp.concatenate([jnp.where(row == 0, value, block[:8]), block[8:]], axis=0)
    return jnp.concatenate([block[:-8], jnp.where(row == 7, value, block[-8:])], axis=0)


def differences(i, tile_rows, field_ref, wet_ref):
    field = field_ref[i * EDGE : (i + 1) * EDGE, :]
    wet = wet_ref[i : i + 1, :]
    lane = lane_index(1, CELLS)
    both = wet * pltpu.roll(wet, EDGE, 1)
    east_wet = jnp.where(lane == EDGE - 1, both, jnp.where(lane == CELLS - 1, 0.0, 1.0))
    above = min((i + 1) * EDGE, tile_rows * EDGE - 1)
    north = set_row(pltpu.roll(field, EDGE - 1, 0), -1, field_ref[above : above + 1, :])
    north_wet = wet * wet_ref[i + 1 : i + 2, :]
    return field, field - pltpu.roll(field, CELLS - 1, 1), field - north, east_wet, north_wet


def stencil(i, tile_rows, field_ref, ef_ref, nf_ref, wet_ref, south_flux, top_flux):
    rows = slice(i * EDGE, (i + 1) * EDGE)
    field, over_e, over_n, east_wet, north_wet = differences(i, tile_rows, field_ref, wet_ref)
    flux_e = (ef_ref[rows, :].astype(F32) * east_wet) * over_e
    flux_n = nf_ref[rows, :].astype(F32) * over_n
    last = top_flux if i == tile_rows - 1 else flux_n[EDGE - 1 :, :] * north_wet
    flux_n = set_row(flux_n, -1, last)
    flux_s = set_row(pltpu.roll(flux_n, 1, 0), 0, south_flux)
    image = surface_term * field + (flux_e - pltpu.roll(flux_e, 1, 1)) + (flux_n - flux_s)
    return field, image, last


def lat_flux(coef, own, other):
    flux = coef * (own - other)
    low = on_low_band()
    return jnp.where(low, flux, 0.0), jnp.where(low, 0.0, -flux)


def edge_rows(i, block, east_ref, west_ref):
    west_ref[i : i + 1, :] = block[:, :EDGE].T[0:1, :]
    east_ref[i : i + 1, :] = block[:, EDGE:].T[EDGE - 1 :, :]


def boundary_row(ref):
    return jnp.where(on_low_band(), ref[ref.shape[0] - 1 :, :], ref[0:1, :])


def first_kernel(
    wet_hbm, rhs_hbm, left_hbm, right_hbm, ef_hbm, nf_hbm,
    z_ref, short_ref, r_ref, left_ref, right_ref, ef_ref, nf_ref, wet_ref, to_e, to_w, to_a, to_b, to_l, sum_ref,
    list_ref, flags_ref, rhs_ref, sems,
):
    tile_rows = rhs_hbm.shape[0] // EDGE
    tiles = 2 * tile_rows
    used = [0]

    def load(source, target):
        copy = pltpu.make_async_copy(source, target, sems.at[used[0]])
        used[0] += 1
        copy.start()
        return copy

    listing = load(wet_hbm, list_ref)
    step = tile_rows // CHUNKS
    loads = {}
    for k in range(CHUNKS):
        rows, some = pl.ds(k * step * EDGE, step * EDGE), pl.ds(k * step, step)
        loads[k * step] = [
            load(rhs_hbm.at[rows], rhs_ref.at[rows]),
            load(left_hbm.at[some], left_ref.at[some]),
            load(right_hbm.at[some], right_ref.at[some]),
        ]
    faces = [load(ef_hbm, ef_ref), load(nf_hbm, nf_ref)]
    for ref in (wet_ref, to_e, to_w, to_l):
        ref[...] = jnp.zeros_like(ref)
    listing.wait()
    for t in range(flags_ref.shape[0]):
        flags_ref[t] = 0.0
    for k in range(tiles):
        flags_ref[list_ref[0, k]] = 1.0
    lane = lane_index(1, CELLS)
    for i in range(tile_rows):
        wet_ref[i : i + 1, :] = jnp.where(lane < EDGE, flags_ref[2 * i], flags_ref[2 * i + 1])
    sums = jnp.zeros(sum_ref.shape, F32)
    for i in range(tile_rows):
        for copy in loads.get(i, ()):
            copy.wait()
        rows = slice(i * EDGE, (i + 1) * EDGE)
        residual = rhs_ref[rows, :] * wet_ref[i : i + 1, :]
        r_ref[rows, :] = residual
        rounded = residual.astype(BF16)
        parts = [
            rounded_product(left_ref[i, k], rounded[:, k * EDGE : (k + 1) * EDGE], right_ref[i, k]) for k in range(2)
        ]
        short = jnp.concatenate(parts, axis=1)
        short_ref[rows, :] = short
        precond = short.astype(F32)
        z_ref[rows, :] = precond
        edge_rows(i, precond, to_e, to_w)
        sums = sums + fold(residual * precond)
    sum_ref[...] = sums
    for copy in faces:
        copy.wait()
    for i in range(tile_rows):
        face = ef_ref[i * EDGE : (i + 1) * EDGE, EDGE:].astype(F32).T[EDGE - 1 :, :]
        to_e[ROWS + i : ROWS + i + 1, :] = face * wet_ref[i : i + 1, EDGE:]
    to_w[ROWS : ROWS + tile_rows, :] = wet_ref[:tile_rows, :EDGE]
    to_l[0:1, :] = boundary_row(z_ref)
    rows = tile_rows * EDGE
    last = nf_ref[rows - 16 : rows, :].astype(F32)[15:16, :] * wet_ref[tile_rows - 1 : tile_rows, :]
    to_l[1:2, :] = jnp.where(on_low_band(), last, wet_ref[0:1, :])
    odd = on_odd_sector()
    to_a[...] = jnp.where(odd, to_e[...], to_w[...])
    to_b[...] = jnp.where(odd, to_w[...], to_e[...])


def inner_kernel(z_ref, left_ref, right_ref, ef_ref, nf_ref, wet_ref, q_ref, w_ref, east_ref, west_ref):
    tile_rows = z_ref.shape[0] // EDGE
    east_ref[...] = jnp.zeros_like(east_ref)
    west_ref[...] = jnp.zeros_like(west_ref)
    south = top = jnp.zeros((1, CELLS), F32)
    for i in range(tile_rows):
        rows = slice(i * EDGE, (i + 1) * EDGE)
        _, image, south = stencil(i, tile_rows, z_ref, ef_ref, nf_ref, wet_ref, south, top)
        q_ref[rows, :] = image
        parts = [
            wide_product(left_ref[i, k], image[:, k * EDGE : (k + 1) * EDGE], right_ref[i, k])
            for k in range(2)
        ]
        product = jnp.concatenate(parts, axis=1)
        w_ref[rows, :] = product
        edge_rows(i, product, east_ref, west_ref)


def edge_kernel(
    w_ref, left_ref, right_ref, east_in, west_in, to_e, to_w, to_l, in_b, in_a, in_l,
    east_ref, west_ref, to_l2, lat_ref, coef_e, coef_w, flux_e, flux_w, turn_e, turn_w, right_e, right_w,
):
    tile_rows = w_ref.shape[0] // EDGE
    odd = on_odd_sector()
    from_e = jnp.where(odd, in_a[...], in_b[...])
    from_w = jnp.where(odd, in_b[...], in_a[...])
    coef_e[...] = to_e[ROWS:, :] * from_e[ROWS:, :]
    coef_w[...] = to_w[ROWS:, :] * from_w[ROWS:, :]
    flux_e[...] = coef_e[...] * (to_e[:ROWS, :] - from_e[:ROWS, :])
    flux_w[...] = coef_w[...] * (to_w[:ROWS, :] - from_w[:ROWS, :])
    for ref in (turn_e, turn_w, right_e, right_w, to_l2, lat_ref):
        ref[...] = jnp.zeros_like(ref)
    spread = jnp.concatenate(split(flux_e[...]) + split(flux_w[...]), axis=0)
    for i in range(tile_rows):
        moved_e = dot_nt(spread[: 2 * ROWS], left_ref[i, 1])
        moved_w = dot_nt(spread[2 * ROWS :], left_ref[i, 0])
        turn_e[i : i + 1, :] = moved_e[i : i + 1, :] + moved_e[ROWS + i : ROWS + i + 1, :]
        turn_w[i : i + 1, :] = moved_w[i : i + 1, :] + moved_w[ROWS + i : ROWS + i + 1, :]
        right_e[i : i + 1, :] = right_ref[i, 1, EDGE - 16 :, :].astype(F32)[15:16, :]
        right_w[i : i + 1, :] = right_ref[i, 0, 0:16, :].astype(F32)[0:1, :]
    east_ref[...] = east_in[...] + turn_e[...] * right_e[:, EDGE - 1 :]
    west_ref[...] = west_in[...] + turn_w[...] * right_w[:, 0:1]
    low = on_low_band()
    end = tile_rows - 1
    flux_l = to_l[1:2, :] * in_l[1:2, :] * (to_l[0:1, :] - in_l[0:1, :])
    lat_ref[2:3, :] = flux_l
    pick = jnp.where((lane_index(16, EDGE) == jnp.where(low, EDGE - 1, 0)) & (row_index(16, EDGE) == 0), 1.0, 0.0)
    for k in range(2):
        at = slice(k * EDGE, (k + 1) * EDGE)
        left = jnp.where(low, left_ref[end, k], left_ref[0, k])
        right = jnp.where(low, right_ref[end, k], right_ref[0, k])
        lat_ref[0:1, at] = dot_nt(pick.astype(BF16), left)[0:1, :]
        spread = jnp.concatenate(split(jnp.broadcast_to(flux_l[:, at], (16, EDGE))), axis=0)
        moved = dot(spread, right)
        lat_ref[1:2, at] = moved[0:1, :] + moved[16:17, :]
    by_col, by_row = lat_ref[0:1, :], lat_ref[1:2, :]
    row = row_index(ROWS, EDGE)
    here = row == jnp.where(low, end, 0)
    east_ref[...] += jnp.where(here, by_col[:, EDGE:] * by_row[:, CELLS - 1 :], 0.0)
    west_ref[...] += jnp.where(here, by_col[:, :EDGE] * by_row[:, 0:1], 0.0)
    by_e = jnp.where(low, turn_e[end : end + 1, EDGE - 1 :] * right_e[end : end + 1, :], turn_e[0:1, 0:1] * right_e[0:1, :])
    by_w = jnp.where(low, turn_w[end : end + 1, EDGE - 1 :] * right_w[end : end + 1, :], turn_w[0:1, 0:1] * right_w[0:1, :])
    own_w = jnp.where(low, by_col[:, EDGE - 1 : EDGE], by_col[:, 0:1])
    own_e = jnp.where(low, by_col[:, CELLS - 1 :], by_col[:, EDGE : EDGE + 1])
    to_l2[0:1, :] = boundary_row(w_ref) + jnp.concatenate(
        [by_w + own_w * by_row[:, :EDGE], by_e + own_e * by_row[:, EDGE:]], axis=1
    )


def middle_kernel(
    z_ref, r_ref, q_ref, w_in, ef_ref, nf_ref, wet_ref, lat_ref, turn_e, turn_w, right_e, right_w, sum_in, w_ref, sums_ref
):
    tile_rows = z_ref.shape[0] // EDGE
    zero = jnp.zeros((8, CELLS), F32)
    zq, rw, qw, faces, squares = zero, zero, zero, zero, zero

    def complete(i, zq, rw, qw):
        rows = slice(i * EDGE, (i + 1) * EDGE)
        image = q_ref[rows, :]
        product = w_in[rows, :] + jnp.concatenate(
            [column(turn_w, i) * right_w[i : i + 1, :], column(turn_e, i) * right_e[i : i + 1, :]], axis=1
        )
        if i in (0, tile_rows - 1):
            here = on_low_band() == (i > 0)
            by_row = jnp.where(here, lat_ref[1:2, :], 0.0)
            by_col = [jnp.broadcast_to(lat_ref[0:1, k * EDGE : (k + 1) * EDGE], (EDGE, EDGE)).T for k in range(2)]
            product = product + jnp.concatenate(by_col, axis=1) * by_row
        w_ref[rows, :] = product
        return zq + fold(z_ref[rows, :] * image), rw + fold(r_ref[rows, :] * product), qw + fold(image * product)

    zq, rw, qw = complete(0, zq, rw, qw)
    for i in range(tile_rows):
        if i + 1 < tile_rows:
            zq, rw, qw = complete(i + 1, zq, rw, qw)
        rows = slice(i * EDGE, (i + 1) * EDGE)
        field, over_e, over_n, east_wet, north_wet = differences(i, tile_rows, w_ref, wet_ref)
        by_e = ef_ref[rows, :].astype(F32) * east_wet * (over_e * over_e)
        by_n = nf_ref[rows, :].astype(F32) * (over_n * over_n)
        by_n = set_row(by_n, -1, 0.0 if i == tile_rows - 1 else by_n[EDGE - 1 :, :] * north_wet)
        faces = faces + fold(by_e + by_n)
        squares = squares + fold(field * field)
    for k, total in enumerate((sum_in[...], zq, rw, qw, faces + surface_term * squares)):
        sums_ref[k] = total


def sums_kernel(
    sums_in, east_ref, west_ref, to_e, to_w, lat_ref, flux_e1, flux_w1, coef_w, own_l, own_l2, in_l, in_l2, from_w,
    packed_ref, flux_w, flux_l,
):
    over_w = west_ref[...] - from_w[...]
    flux_w[...] = coef_w[...] * over_w
    top, bottom = lat_flux(own_l[1:2, :] * in_l[1:2, :], own_l2[0:1, :], in_l2[0:1, :])
    flux_l[...] = jnp.zeros_like(flux_l)
    flux_l[0:1, :] = top
    flux_l[1:2, :] = -bottom

    outer = {
        1: total(flux_e1[...] * to_e[:ROWS, :] + flux_w1[...] * to_w[:ROWS, :])
        + total(lat_ref[2:3, :] * own_l[0:1, :]),
        3: total(flux_e1[...] * east_ref[...] + flux_w1[...] * west_ref[...])
        + total(lat_ref[2:3, :] * own_l2[0:1, :]),
        4: total(flux_w[...] * over_w) + total((top - bottom) * own_l2[0:1, :]),
    }
    lane = lane_index(1, EDGE)
    packed = jnp.zeros((1, EDGE), F32)
    for k in range(5):
        value = total(sums_in[k])
        packed = jnp.where(lane == k, value + outer[k] if k in outer else value, packed)
    packed_ref[...] = jnp.broadcast_to(packed, packed_ref.shape)


def outer_kernel(
    left_hbm, right_hbm, ef_hbm, nf_hbm, w_ref, wet_ref, east_ref, coef_e, from_e, flux_w, flux_l, sums_ref,
    u_ref, share_ref, left_ref, right_ref, ef_ref, nf_ref, flux_e, sems,
):
    tile_rows = w_ref.shape[0] // EDGE
    step = tile_rows // 2
    loads = []
    for k in range(tile_rows // step):
        rows, some = pl.ds(k * step * EDGE, step * EDGE), pl.ds(k * step, step)
        group = [
            pltpu.make_async_copy(source.at[place], target.at[place], sems.at[4 * k + n])
            for n, (source, target, place) in enumerate(
                ((ef_hbm, ef_ref, rows), (nf_hbm, nf_ref, rows), (left_hbm, left_ref, some), (right_hbm, right_ref, some))
            )
        ]
        for copy in group:
            copy.start()
        loads.append(group)
    flux_e[...] = coef_e[...] * (east_ref[...] - from_e[...])
    lane = lane_index(EDGE, EDGE)
    south, top = -flux_l[1:2, :], flux_l[0:1, :]
    zq, qw = (total(sums_ref[k]) for k in (1, 3))
    share = jnp.where(zq > 0.0, qw / jnp.where(zq > 0.0, zq, 1.0), 0.0)
    share_ref[...] = jnp.broadcast_to(share, share_ref.shape)
    for i in range(tile_rows):
        if i % step == 0:
            for copy in loads[i // step]:
                copy.wait()
        _, image, south = stencil(i, tile_rows, w_ref, ef_ref, nf_ref, wet_ref, south, top)
        image = image + jnp.concatenate(
            [jnp.where(lane == 0, column(flux_w, i), 0.0), jnp.where(lane == EDGE - 1, column(flux_e, i), 0.0)], axis=1
        )
        parts = [
            wide_product(left_ref[i, k], image[:, k * EDGE : (k + 1) * EDGE], right_ref[i, k]) for k in range(2)
        ]
        rows = slice(i * EDGE, (i + 1) * EDGE)
        u_ref[rows, :] = (jnp.concatenate(parts, axis=1) - share * w_ref[rows, :]).astype(BF16)


def last_kernel(all_ref, z_ref, w_ref, u_ref, share_ref, sol_hbm, pre_hbm, sol_ref, pre_ref, sems):
    tile_rows = z_ref.shape[0] // EDGE
    totals = jnp.sum(all_ref[...], axis=0, keepdims=True)
    lane = lane_index(1, EDGE)
    rz, zq, rw, qw, waw = (jnp.sum(jnp.where(lane == k, totals, 0.0), axis=1, keepdims=True) for k in range(5))
    step0 = rz / zq
    rz1 = step0 * (step0 * qw - rw)
    grow = 1.0 + rz1 / rz
    step1 = rz1 / (grow * grow * zq - 2.0 * grow * step0 * qw + step0 * step0 * waw)
    with_z = step0 + step1 * grow
    with_w = -step1 * step0
    less_w = with_z + with_w * share_ref[0:1, 0:1]
    group = 2 * EDGE
    stores = []
    for i in range(tile_rows * EDGE // group):
        rows = slice(i * group, (i + 1) * group)
        precond, product = z_ref[rows, :].astype(F32), w_ref[rows, :]
        sol_ref[rows, :] = with_z * precond + with_w * product
        pre_ref[rows, :] = (precond - less_w * product - with_w * u_ref[rows, :].astype(F32)).astype(BF16)
        place = pl.ds(i * group, group)
        for k, (source, target) in enumerate(((sol_ref, sol_hbm), (pre_ref, pre_hbm))):
            copy = pltpu.make_async_copy(source.at[place], target.at[place], sems.at[2 * i + k])
            copy.start()
            stores.append(copy)
    for copy in stores:
        copy.wait()


def call(kernel, outs, args, name, scratch=(), in_space=pltpu.VMEM, out_space=pltpu.VMEM, flops=0):
    if not isinstance(in_space, list):
        in_space = [in_space] * len(args)
    return pl.pallas_call(
        kernel,
        out_shape=outs,
        in_specs=[pl.BlockSpec(memory_space=space) for space in in_space],
        out_specs=[pl.BlockSpec(memory_space=out_space)] * len(outs),
        scratch_shapes=scratch,
        compiler_params=pltpu.CompilerParams(vmem_limit_bytes=VMEM_LIMIT),
        cost_estimate=pl.CostEstimate(flops=flops, bytes_accessed=0, transcendentals=0),
        name=name,
    )(*args)


def per_device(right_side, east_face, north_face, left_factor, right_factor, wet_list):
    rows, cols = right_side.shape
    lons, lats = lax.axis_size("lon"), lax.axis_size("lat")
    tile_rows = rows // EDGE
    shape = functools.partial(jax.ShapeDtypeStruct, dtype=F32)
    like = lambda a: jax.ShapeDtypeStruct(a.shape, a.dtype)
    field = shape((rows, cols))
    half = jax.ShapeDtypeStruct((rows, cols), BF16)
    edge = shape((ROWS, EDGE))
    message = shape((2 * ROWS, EDGE))
    strip = shape((8, cols))
    across = [(0, 1), (1, 0)]

    def pairs(parity):
        forward = [(i, (i + 1) % lons) for i in range(parity, lons, 2)]
        return forward + [(b, a) for a, b in forward]

    by_place = (tile_rows, 2, EDGE, EDGE)
    left_factor, right_factor = left_factor.reshape(by_place), right_factor.reshape(by_place)
    arguments = [
        pltpu.with_memory_space_constraint(a, pltpu.HBM)
        for a in (wet_list, right_side, left_factor, right_factor, east_face, north_face)
    ]
    z, short, r, left, right, ef, nf, wet, to_e, to_w, to_a, to_b, to_l, rz = call(
        first_kernel,
        [field, half, field, like(left_factor), like(right_factor), like(east_face), like(north_face),
         shape((ROWS, cols)), message, message, message, message, strip, strip],
        arguments, "first",
        [pltpu.SMEM(wet_list.shape, jnp.int32), pltpu.SMEM((32,), F32), pltpu.VMEM((rows, cols), F32),
         pltpu.SemaphoreType.DMA((3 * CHUNKS + 3,))],
        in_space=pltpu.HBM,
    )
    in_b = lax.ppermute(to_b, "lon", pairs(0))
    in_a = lax.ppermute(to_a, "lon", pairs(1))
    in_l = lax.ppermute(to_l, "lat", across)
    q, w, east, west = call(
        inner_kernel, [field, field, edge, edge], (z, left, right, ef, nf, wet), "inner"
    )
    east, west, to_l2, lat, coef_e, coef_w, flux_e1, flux_w1, *terms = call(
        edge_kernel, [edge, edge, strip, strip] + [edge] * 8,
        (w, left, right, east, west, to_e, to_w, to_l, in_b, in_a, in_l), "edges",
    )
    from_w2 = lax.ppermute(east, "lon", [(i, (i + 1) % lons) for i in range(lons)])
    in_l2 = lax.ppermute(to_l2, "lat", across)
    from_e2 = lax.ppermute(west, "lon", [((i + 1) % lons, i) for i in range(lons)])
    w, sums = call(
        middle_kernel, [field, shape((5, 8, cols))], (z, r, q, w, ef, nf, wet, lat, *terms, rz), "middle"
    )
    packed, flux_w, flux_l = call(
        sums_kernel, [shape((lons * lats, EDGE)), edge, strip],
        (sums, east, west, to_e, to_w, lat, flux_e1, flux_w1, coef_w, to_l, to_l2, in_l, in_l2, from_w2), "sums",
    )
    everyone = lax.all_to_all(packed, ("lon", "lat"), 0, 0, tiled=True)
    u, share = call(
        outer_kernel, [half, shape((8, EDGE))],
        (*arguments[2:], w, wet, east, coef_e, from_e2, flux_w, flux_l, sums), "outer",
        [pltpu.VMEM(a.shape, a.dtype) for a in arguments[2:]]
        + [pltpu.VMEM((ROWS, EDGE), F32), pltpu.SemaphoreType.DMA((8,))],
        in_space=[pltpu.HBM] * 4 + [pltpu.VMEM] * 8, flops=100_000_000_000,
    )
    return tuple(
        call(
            last_kernel, [field, half], (everyone, short, w, u, share), "last",
            [pltpu.VMEM((rows, cols), F32), pltpu.VMEM((rows, cols), BF16), pltpu.SemaphoreType.DMA((tile_rows,))],
            out_space=pltpu.HBM,
        )
    )


def solution(mesh):
    tiles = P("lat", "lon", None, None)
    cells = P("lat", "lon")
    return jax.shard_map(
        per_device,
        mesh=mesh,
        in_specs=(cells, cells, cells, tiles, tiles, cells),
        out_specs=(cells, cells),
        check_vma=False,
    )
```

```python
import functools

import jax
import jax.numpy as jnp
from jax import lax
from jax.experimental import pallas as pl
from jax.experimental.pallas import tpu as pltpu
from jax.sharding import PartitionSpec as P

EDGE = 128
CELLS = 2 * EDGE
surface_term = 0.0001
F32 = jnp.float32
BF16 = jnp.bfloat16
VMEM_LIMIT = 8 * 1024 * 1024
HEAD = 6
SPAN = 16
ROWS = 16


def dot(left, right):
    return jnp.dot(left, right, preferred_element_type=F32)


def dot_nt(left, right):
    return lax.dot_general(left, right, (((1,), (1,)), ((), ())), preferred_element_type=F32)


def lane_index(rows, cols):
    return lax.broadcasted_iota(jnp.int32, (rows, cols), 1)


def row_index(rows, cols):
    return lax.broadcasted_iota(jnp.int32, (rows, cols), 0)


def rounded_product(left, tile, right):
    partial = dot(left, tile).astype(BF16)
    return dot(partial, right).astype(BF16)


def split(value):
    high = value.astype(BF16)
    return high, (value - high.astype(F32)).astype(BF16)


def wide_product(left, tile, right):
    partial = dot(jnp.concatenate([left, left], axis=1), jnp.concatenate(split(tile), axis=0))
    return dot(jnp.concatenate(split(partial), axis=1), jnp.concatenate([right, right], axis=0))


def fold(block):
    total = block[0:8]
    for k in range(1, block.shape[0] // 8):
        total = total + block[8 * k : 8 * k + 8]
    return total


def total(value):
    return jnp.sum(jnp.sum(value, axis=0, keepdims=True), axis=1, keepdims=True)


def column(rows_ref, i):
    return jnp.broadcast_to(rows_ref[i : i + 1, :], (EDGE, EDGE)).T


def on_low_band():
    return lax.axis_index("lat") == 0


def on_odd_sector():
    return lax.axis_index("lon") % 2 == 1


def held_up():
    return lax.axis_index("lon") % SPAN == 0


def set_row(block, at, value):
    row = row_index(8, CELLS)
    if at == 0:
        return jnp.concatenate([jnp.where(row == 0, value, block[:8]), block[8:]], axis=0)
    return jnp.concatenate([block[:-8], jnp.where(row == 7, value, block[-8:])], axis=0)


def differences(i, tile_rows, field_ref, wet_ref):
    field = field_ref[i * EDGE : (i + 1) * EDGE, :]
    wet = wet_ref[i : i + 1, :]
    lane = lane_index(1, CELLS)
    both = wet * pltpu.roll(wet, EDGE, 1)
    east_wet = jnp.where(lane == EDGE - 1, both, jnp.where(lane == CELLS - 1, 0.0, 1.0))
    above = min((i + 1) * EDGE, tile_rows * EDGE - 1)
    north = set_row(pltpu.roll(field, EDGE - 1, 0), -1, field_ref[above : above + 1, :])
    north_wet = wet * wet_ref[i + 1 : i + 2, :]
    return field, field - pltpu.roll(field, CELLS - 1, 1), field - north, east_wet, north_wet


def stencil(i, tile_rows, field_ref, ef_ref, nf_ref, wet_ref, south_flux, top_flux):
    rows = slice(i * EDGE, (i + 1) * EDGE)
    field, over_e, over_n, east_wet, north_wet = differences(i, tile_rows, field_ref, wet_ref)
    flux_e = (ef_ref[rows, :].astype(F32) * east_wet) * over_e
    flux_n = nf_ref[rows, :].astype(F32) * over_n
    last = top_flux if i == tile_rows - 1 else flux_n[EDGE - 1 :, :] * north_wet
    flux_n = set_row(flux_n, -1, last)
    flux_s = set_row(pltpu.roll(flux_n, 1, 0), 0, south_flux)
    image = surface_term * field + (flux_e - pltpu.roll(flux_e, 1, 1)) + (flux_n - flux_s)
    return field, image, last


def lat_flux(coef, own, other):
    flux = coef * (own - other)
    low = on_low_band()
    return jnp.where(low, flux, 0.0), jnp.where(low, 0.0, -flux)


def edge_rows(i, block, east_ref, west_ref):
    west_ref[i : i + 1, :] = block[:, :EDGE].T[0:1, :]
    east_ref[i : i + 1, :] = block[:, EDGE:].T[EDGE - 1 :, :]


def boundary_row(ref):
    return jnp.where(on_low_band(), ref[ref.shape[0] - 1 :, :], ref[0:1, :])


def first_kernel(
    wet_hbm, rhs_hbm, left_hbm, right_hbm, ef_hbm, nf_hbm,
    z_ref, short_ref, rhs_ref, left_ref, right_ref, ef_ref, nf_ref, wet_ref, to_e, to_w, to_a, to_b, to_l, sum_ref,
    list_ref, flags_ref, sems,
):
    tile_rows = rhs_hbm.shape[0] // EDGE
    tiles = 2 * tile_rows
    used = [0]

    def load(source, target):
        copy = pltpu.make_async_copy(source, target, sems.at[used[0]])
        used[0] += 1
        copy.start()
        return copy

    listing = load(wet_hbm, list_ref)
    loads = {}
    for at, stop in ((0, HEAD), (HEAD, tile_rows)):
        rows, some = pl.ds(at * EDGE, (stop - at) * EDGE), pl.ds(at, stop - at)
        loads[at] = [
            load(rhs_hbm.at[rows], rhs_ref.at[rows]),
            load(left_hbm.at[some], left_ref.at[some]),
            load(right_hbm.at[some], right_ref.at[some]),
        ]
    faces = [load(ef_hbm, ef_ref), load(nf_hbm, nf_ref)]
    for ref in (wet_ref, to_e, to_w, to_l):
        ref[...] = jnp.zeros_like(ref)
    listing.wait()
    for t in range(flags_ref.shape[0]):
        flags_ref[t] = 0.0
    for k in range(tiles):
        flags_ref[list_ref[0, k]] = 1.0
    lane = lane_index(1, CELLS)
    for i in range(tile_rows):
        wet_ref[i : i + 1, :] = jnp.where(lane < EDGE, flags_ref[2 * i], flags_ref[2 * i + 1])
    sums = jnp.zeros(sum_ref.shape, F32)
    for i in range(tile_rows):
        for copy in loads.get(i, ()):
            copy.wait()
        rows = slice(i * EDGE, (i + 1) * EDGE)
        residual = rhs_ref[rows, :] * wet_ref[i : i + 1, :]
        rounded = residual.astype(BF16)
        parts = [
            rounded_product(left_ref[i, k], rounded[:, k * EDGE : (k + 1) * EDGE], right_ref[i, k]) for k in range(2)
        ]
        short = jnp.concatenate(parts, axis=1)
        short_ref[rows, :] = short
        precond = short.astype(F32)
        z_ref[rows, :] = precond
        edge_rows(i, precond, to_e, to_w)
        sums = sums + fold(residual * precond)
    sum_ref[...] = sums
    for copy in faces:
        copy.wait()
    for i in range(tile_rows):
        face = ef_ref[i * EDGE : (i + 1) * EDGE, EDGE:].astype(F32).T[EDGE - 1 :, :]
        to_e[ROWS + i : ROWS + i + 1, :] = face * wet_ref[i : i + 1, EDGE:]
    to_w[ROWS : ROWS + tile_rows, :] = wet_ref[:tile_rows, :EDGE]
    to_l[0:1, :] = boundary_row(z_ref)
    rows = tile_rows * EDGE
    last = nf_ref[rows - 16 : rows, :].astype(F32)[15:16, :] * wet_ref[tile_rows - 1 : tile_rows, :]
    to_l[1:2, :] = jnp.where(on_low_band(), last, wet_ref[0:1, :])
    odd = on_odd_sector()
    to_a[...] = jnp.where(odd, to_e[...], to_w[...])
    to_b[...] = jnp.where(odd, to_w[...], to_e[...])


def inner(z_ref, left_ref, right_ref, ef_ref, nf_ref, wet_ref, q_ref, w_ref, east_ref, west_ref):
    tile_rows = z_ref.shape[0] // EDGE
    east_ref[...] = jnp.zeros_like(east_ref)
    west_ref[...] = jnp.zeros_like(west_ref)
    south = top = jnp.zeros((1, CELLS), F32)
    for i in range(tile_rows):
        rows = slice(i * EDGE, (i + 1) * EDGE)
        _, image, south = stencil(i, tile_rows, z_ref, ef_ref, nf_ref, wet_ref, south, top)
        q_ref[rows, :] = image
        parts = [
            wide_product(left_ref[i, k], image[:, k * EDGE : (k + 1) * EDGE], right_ref[i, k]) for k in range(2)
        ]
        product = jnp.concatenate(parts, axis=1)
        w_ref[rows, :] = product
        edge_rows(i, product, east_ref, west_ref)


def early_inner_kernel(a_in, b_in, *refs):
    *arrays, to_a, to_b = refs
    to_a[...] = a_in[...]
    to_b[...] = b_in[...]

    @pl.when(held_up())
    def _():
        inner(*arrays)


def late_inner_kernel(*refs):
    @pl.when(jnp.logical_not(held_up()))
    def _():
        inner(*refs)


def edge_kernel(
    early_w, late_w, left_ref, right_ref, early_e, early_west, late_e, late_west, to_e, to_w, to_l, in_b, in_a, in_l,
    east_ref, west_ref, to_l2, lat_ref, coef_e, coef_w, flux_e, flux_w, turn_e, turn_w, right_e, right_w,
):
    tile_rows = early_w.shape[0] // EDGE
    early = held_up()
    odd = on_odd_sector()
    from_e = jnp.where(odd, in_a[...], in_b[...])
    from_w = jnp.where(odd, in_b[...], in_a[...])
    coef_e[...] = to_e[ROWS:, :] * from_e[ROWS:, :]
    coef_w[...] = to_w[ROWS:, :] * from_w[ROWS:, :]
    flux_e[...] = coef_e[...] * (to_e[:ROWS, :] - from_e[:ROWS, :])
    flux_w[...] = coef_w[...] * (to_w[:ROWS, :] - from_w[:ROWS, :])
    for ref in (turn_e, turn_w, right_e, right_w, to_l2, lat_ref):
        ref[...] = jnp.zeros_like(ref)
    spread = jnp.concatenate(split(flux_e[...]) + split(flux_w[...]), axis=0)
    for i in range(tile_rows):
        moved_e = dot_nt(spread[: 2 * ROWS], left_ref[i, 1])
        moved_w = dot_nt(spread[2 * ROWS :], left_ref[i, 0])
        turn_e[i : i + 1, :] = moved_e[i : i + 1, :] + moved_e[ROWS + i : ROWS + i + 1, :]
        turn_w[i : i + 1, :] = moved_w[i : i + 1, :] + moved_w[ROWS + i : ROWS + i + 1, :]
        right_e[i : i + 1, :] = right_ref[i, 1, EDGE - 16 :, :].astype(F32)[15:16, :]
        right_w[i : i + 1, :] = right_ref[i, 0, 0:16, :].astype(F32)[0:1, :]
    east_ref[...] = jnp.where(early, early_e[...], late_e[...]) + turn_e[...] * right_e[:, EDGE - 1 :]
    west_ref[...] = jnp.where(early, early_west[...], late_west[...]) + turn_w[...] * right_w[:, 0:1]
    low = on_low_band()
    end = tile_rows - 1
    flux_l = to_l[1:2, :] * in_l[1:2, :] * (to_l[0:1, :] - in_l[0:1, :])
    lat_ref[2:3, :] = flux_l
    pick = jnp.where((lane_index(16, EDGE) == jnp.where(low, EDGE - 1, 0)) & (row_index(16, EDGE) == 0), 1.0, 0.0)
    for k in range(2):
        at = slice(k * EDGE, (k + 1) * EDGE)
        left = jnp.where(low, left_ref[end, k], left_ref[0, k])
        right = jnp.where(low, right_ref[end, k], right_ref[0, k])
        lat_ref[0:1, at] = dot_nt(pick.astype(BF16), left)[0:1, :]
        spread = jnp.concatenate(split(jnp.broadcast_to(flux_l[:, at], (16, EDGE))), axis=0)
        moved = dot(spread, right)
        lat_ref[1:2, at] = moved[0:1, :] + moved[16:17, :]
    by_col, by_row = lat_ref[0:1, :], lat_ref[1:2, :]
    row = row_index(ROWS, EDGE)
    here = row == jnp.where(low, end, 0)
    east_ref[...] += jnp.where(here, by_col[:, EDGE:] * by_row[:, CELLS - 1 :], 0.0)
    west_ref[...] += jnp.where(here, by_col[:, :EDGE] * by_row[:, 0:1], 0.0)
    by_e = jnp.where(low, turn_e[end : end + 1, EDGE - 1 :] * right_e[end : end + 1, :], turn_e[0:1, 0:1] * right_e[0:1, :])
    by_w = jnp.where(low, turn_w[end : end + 1, EDGE - 1 :] * right_w[end : end + 1, :], turn_w[0:1, 0:1] * right_w[0:1, :])
    own_w = jnp.where(low, by_col[:, EDGE - 1 : EDGE], by_col[:, 0:1])
    own_e = jnp.where(low, by_col[:, CELLS - 1 :], by_col[:, EDGE : EDGE + 1])
    to_l2[0:1, :] = jnp.where(early, boundary_row(early_w), boundary_row(late_w)) + jnp.concatenate(
        [by_w + own_w * by_row[:, :EDGE], by_e + own_e * by_row[:, EDGE:]], axis=1
    )


def middle(
    z_ref, rhs_ref, q_ref, w_in, ef_ref, nf_ref, wet_ref, lat_ref, turn_e, turn_w, right_e, right_w, sum_in, w_ref, sums_ref
):
    tile_rows = z_ref.shape[0] // EDGE
    zero = jnp.zeros((8, CELLS), F32)
    zq, rw, qw, faces, squares = zero, zero, zero, zero, zero

    def complete(i, zq, rw, qw):
        rows = slice(i * EDGE, (i + 1) * EDGE)
        image = q_ref[rows, :]
        product = w_in[rows, :] + jnp.concatenate(
            [column(turn_w, i) * right_w[i : i + 1, :], column(turn_e, i) * right_e[i : i + 1, :]], axis=1
        )
        if i in (0, tile_rows - 1):
            here = on_low_band() == (i > 0)
            by_row = jnp.where(here, lat_ref[1:2, :], 0.0)
            by_col = [jnp.broadcast_to(lat_ref[0:1, k * EDGE : (k + 1) * EDGE], (EDGE, EDGE)).T for k in range(2)]
            product = product + jnp.concatenate(by_col, axis=1) * by_row
        w_ref[rows, :] = product
        return zq + fold(z_ref[rows, :] * image), rw + fold(rhs_ref[rows, :] * product), qw + fold(image * product)

    zq, rw, qw = complete(0, zq, rw, qw)
    for i in range(tile_rows):
        if i + 1 < tile_rows:
            zq, rw, qw = complete(i + 1, zq, rw, qw)
        rows = slice(i * EDGE, (i + 1) * EDGE)
        field, over_e, over_n, east_wet, north_wet = differences(i, tile_rows, w_ref, wet_ref)
        by_e = ef_ref[rows, :].astype(F32) * east_wet * (over_e * over_e)
        by_n = nf_ref[rows, :].astype(F32) * (over_n * over_n)
        by_n = set_row(by_n, -1, 0.0 if i == tile_rows - 1 else by_n[EDGE - 1 :, :] * north_wet)
        faces = faces + fold(by_e + by_n)
        squares = squares + fold(field * field)
    for k, total in enumerate((sum_in[...], zq, rw, qw, faces + surface_term * squares)):
        sums_ref[k] = total


def early_middle_kernel(west_in, *refs):
    *arrays, to_w = refs
    to_w[...] = west_in[...]

    @pl.when(held_up())
    def _():
        middle(*arrays)


def late_middle_kernel(early_w, early_sums, *refs):
    w_ref, sums_ref = refs[-2:]
    early = held_up()

    @pl.when(early)
    def _():
        w_ref[...] = early_w[...]
        sums_ref[...] = early_sums[...]

    @pl.when(jnp.logical_not(early))
    def _():
        middle(*refs)


def sums_kernel(
    sums_in, east_ref, west_ref, to_e, to_w, lat_ref, flux_e1, flux_w1, coef_w, own_l, own_l2, in_l, in_l2, from_w,
    packed_ref, flux_w, flux_l,
):
    over_w = west_ref[...] - from_w[...]
    flux_w[...] = coef_w[...] * over_w
    top, bottom = lat_flux(own_l[1:2, :] * in_l[1:2, :], own_l2[0:1, :], in_l2[0:1, :])
    flux_l[...] = jnp.zeros_like(flux_l)
    flux_l[0:1, :] = top
    flux_l[1:2, :] = -bottom

    outer = {
        1: total(flux_e1[...] * to_e[:ROWS, :] + flux_w1[...] * to_w[:ROWS, :])
        + total(lat_ref[2:3, :] * own_l[0:1, :]),
        3: total(flux_e1[...] * east_ref[...] + flux_w1[...] * west_ref[...])
        + total(lat_ref[2:3, :] * own_l2[0:1, :]),
        4: total(flux_w[...] * over_w) + total((top - bottom) * own_l2[0:1, :]),
    }
    lane = lane_index(1, EDGE)
    packed = jnp.zeros((1, EDGE), F32)
    for k in range(5):
        value = total(sums_in[k])
        packed = jnp.where(lane == k, value + outer[k] if k in outer else value, packed)
    packed_ref[...] = jnp.broadcast_to(packed, packed_ref.shape)


def outer_kernel(
    left_hbm, right_hbm, ef_hbm, nf_hbm, w_ref, wet_ref, east_ref, coef_e, from_e, flux_w, flux_l, sums_ref,
    u_ref, share_ref, left_ref, right_ref, ef_ref, nf_ref, flux_e, sems,
):
    tile_rows = w_ref.shape[0] // EDGE
    step = tile_rows // 2
    loads = []
    for k in range(tile_rows // step):
        rows, some = pl.ds(k * step * EDGE, step * EDGE), pl.ds(k * step, step)
        group = [
            pltpu.make_async_copy(source.at[place], target.at[place], sems.at[4 * k + n])
            for n, (source, target, place) in enumerate(
                ((ef_hbm, ef_ref, rows), (nf_hbm, nf_ref, rows), (left_hbm, left_ref, some), (right_hbm, right_ref, some))
            )
        ]
        for copy in group:
            copy.start()
        loads.append(group)
    flux_e[...] = coef_e[...] * (east_ref[...] - from_e[...])
    lane = lane_index(EDGE, EDGE)
    south, top = -flux_l[1:2, :], flux_l[0:1, :]
    zq, qw = (total(sums_ref[k]) for k in (1, 3))
    share = jnp.where(zq > 0.0, qw / jnp.where(zq > 0.0, zq, 1.0), 0.0)
    share_ref[...] = jnp.broadcast_to(share, share_ref.shape)
    for i in range(tile_rows):
        if i % step == 0:
            for copy in loads[i // step]:
                copy.wait()
        _, image, south = stencil(i, tile_rows, w_ref, ef_ref, nf_ref, wet_ref, south, top)
        image = image + jnp.concatenate(
            [jnp.where(lane == 0, column(flux_w, i), 0.0), jnp.where(lane == EDGE - 1, column(flux_e, i), 0.0)], axis=1
        )
        parts = [
            wide_product(left_ref[i, k], image[:, k * EDGE : (k + 1) * EDGE], right_ref[i, k]) for k in range(2)
        ]
        rows = slice(i * EDGE, (i + 1) * EDGE)
        u_ref[rows, :] = (jnp.concatenate(parts, axis=1) - share * w_ref[rows, :]).astype(BF16)


def last_kernel(all_ref, z_ref, w_ref, u_ref, share_ref, sol_hbm, pre_hbm, sol_ref, pre_ref, sems):
    tile_rows = z_ref.shape[0] // EDGE
    totals = jnp.sum(all_ref[...], axis=0, keepdims=True)
    lane = lane_index(1, EDGE)
    rz, zq, rw, qw, waw = (jnp.sum(jnp.where(lane == k, totals, 0.0), axis=1, keepdims=True) for k in range(5))
    step0 = rz / zq
    rz1 = step0 * (step0 * qw - rw)
    grow = 1.0 + rz1 / rz
    step1 = rz1 / (grow * grow * zq - 2.0 * grow * step0 * qw + step0 * step0 * waw)
    with_z = step0 + step1 * grow
    with_w = -step1 * step0
    less_w = with_z + with_w * share_ref[0:1, 0:1]
    group = 2 * EDGE
    stores = []
    for i in range(tile_rows * EDGE // group):
        rows = slice(i * group, (i + 1) * group)
        precond, product = z_ref[rows, :].astype(F32), w_ref[rows, :]
        sol_ref[rows, :] = with_z * precond + with_w * product
        pre_ref[rows, :] = (precond - less_w * product - with_w * u_ref[rows, :].astype(F32)).astype(BF16)
        place = pl.ds(i * group, group)
        for k, (source, target) in enumerate(((sol_ref, sol_hbm), (pre_ref, pre_hbm))):
            copy = pltpu.make_async_copy(source.at[place], target.at[place], sems.at[2 * i + k])
            copy.start()
            stores.append(copy)
    for copy in stores:
        copy.wait()


def call(kernel, outs, args, name, scratch=(), in_space=pltpu.VMEM, out_space=pltpu.VMEM, flops=0):
    if not isinstance(in_space, list):
        in_space = [in_space] * len(args)
    return pl.pallas_call(
        kernel,
        out_shape=outs,
        in_specs=[pl.BlockSpec(memory_space=space) for space in in_space],
        out_specs=[pl.BlockSpec(memory_space=out_space)] * len(outs),
        scratch_shapes=scratch,
        compiler_params=pltpu.CompilerParams(vmem_limit_bytes=VMEM_LIMIT),
        cost_estimate=pl.CostEstimate(flops=flops, bytes_accessed=0, transcendentals=0),
        name=name,
    )(*args)


def per_device(right_side, east_face, north_face, left_factor, right_factor, wet_list):
    rows, cols = right_side.shape
    lons, lats = lax.axis_size("lon"), lax.axis_size("lat")
    tile_rows = rows // EDGE
    shape = functools.partial(jax.ShapeDtypeStruct, dtype=F32)
    like = lambda a: jax.ShapeDtypeStruct(a.shape, a.dtype)
    field = shape((rows, cols))
    half = jax.ShapeDtypeStruct((rows, cols), BF16)
    edge = shape((ROWS, EDGE))
    message = shape((2 * ROWS, EDGE))
    strip = shape((8, cols))
    across = [(0, 1), (1, 0)]

    def pairs(parity):
        forward = [(i, (i + 1) % lons) for i in range(parity, lons, 2)]
        return forward + [(b, a) for a, b in forward]

    by_place = (tile_rows, 2, EDGE, EDGE)
    left_factor, right_factor = left_factor.reshape(by_place), right_factor.reshape(by_place)
    arguments = [
        pltpu.with_memory_space_constraint(a, pltpu.HBM)
        for a in (wet_list, right_side, left_factor, right_factor, east_face, north_face)
    ]
    z, short, rhs, left, right, ef, nf, wet, to_e, to_w, to_a, to_b, to_l, rz = call(
        first_kernel,
        [field, half, field, like(left_factor), like(right_factor), like(east_face), like(north_face),
         shape((ROWS, cols)), message, message, message, message, strip, strip],
        arguments, "first",
        [pltpu.SMEM(wet_list.shape, jnp.int32), pltpu.SMEM((32,), F32),
         pltpu.SemaphoreType.DMA((9,))],
        in_space=pltpu.HBM,
    )
    arrays = (z, left, right, ef, nf, wet)
    results = [field, field, edge, edge]
    *early, far_a, far_b = call(early_inner_kernel, results + [message, message], (to_a, to_b, *arrays), "early_inner")
    in_b = lax.ppermute(far_b, "lon", pairs(0))
    in_a = lax.ppermute(far_a, "lon", pairs(1))
    in_l = lax.ppermute(to_l, "lat", across)
    late = call(late_inner_kernel, results, arrays, "late_inner")
    east, west, to_l2, lat, coef_e, coef_w, flux_e1, flux_w1, *terms = call(
        edge_kernel, [edge, edge, strip, strip] + [edge] * 8,
        (early[1], late[1], left, right, *early[2:], *late[2:], to_e, to_w, to_l, in_b, in_a, in_l), "edges",
    )
    from_w2 = lax.ppermute(east, "lon", [(i, (i + 1) % lons) for i in range(lons)])
    in_l2 = lax.ppermute(to_l2, "lat", across)
    results = [field, shape((5, 8, cols))]
    faces = (ef, nf, wet, lat, *terms, rz)
    *done, to_w2 = call(early_middle_kernel, results + [edge], (west, z, rhs, *early[:2], *faces), "early_middle")
    from_e2 = lax.ppermute(to_w2, "lon", [((i + 1) % lons, i) for i in range(lons)])
    w, sums = call(late_middle_kernel, results, (*done, z, rhs, *late[:2], *faces), "late_middle")
    packed, flux_w, flux_l = call(
        sums_kernel, [shape((lons * lats, EDGE)), edge, strip],
        (sums, east, west, to_e, to_w, lat, flux_e1, flux_w1, coef_w, to_l, to_l2, in_l, in_l2, from_w2), "sums",
    )
    everyone = lax.all_to_all(packed, ("lon", "lat"), 0, 0, tiled=True)
    u, share = call(
        outer_kernel, [half, shape((8, EDGE))],
        (*arguments[2:], w, wet, east, coef_e, from_e2, flux_w, flux_l, sums), "outer",
        [pltpu.VMEM(a.shape, a.dtype) for a in arguments[2:]]
        + [pltpu.VMEM((ROWS, EDGE), F32), pltpu.SemaphoreType.DMA((8,))],
        in_space=[pltpu.HBM] * 4 + [pltpu.VMEM] * 8, flops=100_000_000_000,
    )
    return tuple(
        call(
            last_kernel, [field, half], (everyone, short, w, u, share), "last",
            [pltpu.VMEM((rows, cols), F32), pltpu.VMEM((rows, cols), BF16), pltpu.SemaphoreType.DMA((tile_rows,))],
            out_space=pltpu.HBM,
        )
    )


def solution(mesh):
    tiles = P("lat", "lon", None, None)
    cells = P("lat", "lon")
    return jax.shard_map(
        per_device,
        mesh=mesh,
        in_specs=(cells, cells, cells, tiles, tiles, cells),
        out_specs=(cells, cells),
        check_vma=False,
    )
```

```python
import functools

import jax
import jax.numpy as jnp
from jax import lax
from jax.experimental import pallas as pl
from jax.experimental.pallas import tpu as pltpu
from jax.sharding import PartitionSpec as P

EDGE = 128
CELLS = 2 * EDGE
surface_term = 0.0001
F32 = jnp.float32
BF16 = jnp.bfloat16
VMEM_LIMIT = 8 * 1024 * 1024
HEAD = 6
SPAN = 16
ROWS = 16


def dot(left, right):
    return jnp.dot(left, right, preferred_element_type=F32)


def dot_nt(left, right):
    return lax.dot_general(left, right, (((1,), (1,)), ((), ())), preferred_element_type=F32)


def lane_index(rows, cols):
    return lax.broadcasted_iota(jnp.int32, (rows, cols), 1)


def row_index(rows, cols):
    return lax.broadcasted_iota(jnp.int32, (rows, cols), 0)


def rounded_product(left, tile, right):
    partial = dot(left, tile).astype(BF16)
    return dot(partial, right).astype(BF16)


def split(value):
    high = value.astype(BF16)
    return high, (value - high.astype(F32)).astype(BF16)


def wide_product(left, tile, right):
    partial = dot(jnp.concatenate([left, left], axis=1), jnp.concatenate(split(tile), axis=0))
    return dot(jnp.concatenate(split(partial), axis=1), jnp.concatenate([right, right], axis=0))


def fold(block):
    total = block[0:8]
    for k in range(1, block.shape[0] // 8):
        total = total + block[8 * k : 8 * k + 8]
    return total


def total(value):
    return jnp.sum(jnp.sum(value, axis=0, keepdims=True), axis=1, keepdims=True)


def column(rows_ref, i):
    return jnp.broadcast_to(rows_ref[i : i + 1, :], (EDGE, EDGE)).T


def on_low_band():
    return lax.axis_index("lat") == 0


def on_odd_sector():
    return lax.axis_index("lon") % 2 == 1


def held_up():
    return lax.axis_index("lon") % SPAN == 0


def set_row(block, at, value):
    row = row_index(8, CELLS)
    if at == 0:
        return jnp.concatenate([jnp.where(row == 0, value, block[:8]), block[8:]], axis=0)
    return jnp.concatenate([block[:-8], jnp.where(row == 7, value, block[-8:])], axis=0)


def differences(i, tile_rows, field_ref, wet_ref):
    field = field_ref[i * EDGE : (i + 1) * EDGE, :]
    wet = wet_ref[i : i + 1, :]
    lane = lane_index(1, CELLS)
    both = wet * pltpu.roll(wet, EDGE, 1)
    east_wet = jnp.where(lane == EDGE - 1, both, jnp.where(lane == CELLS - 1, 0.0, 1.0))
    above = min((i + 1) * EDGE, tile_rows * EDGE - 1)
    north = set_row(pltpu.roll(field, EDGE - 1, 0), -1, field_ref[above : above + 1, :])
    north_wet = wet * wet_ref[i + 1 : i + 2, :]
    return field, field - pltpu.roll(field, CELLS - 1, 1), field - north, east_wet, north_wet


def stencil(i, tile_rows, field_ref, ef_ref, nf_ref, wet_ref, south_flux, top_flux):
    rows = slice(i * EDGE, (i + 1) * EDGE)
    field, over_e, over_n, east_wet, north_wet = differences(i, tile_rows, field_ref, wet_ref)
    flux_e = (ef_ref[rows, :].astype(F32) * east_wet) * over_e
    flux_n = nf_ref[rows, :].astype(F32) * over_n
    last = top_flux if i == tile_rows - 1 else flux_n[EDGE - 1 :, :] * north_wet
    flux_n = set_row(flux_n, -1, last)
    flux_s = set_row(pltpu.roll(flux_n, 1, 0), 0, south_flux)
    image = surface_term * field + (flux_e - pltpu.roll(flux_e, 1, 1)) + (flux_n - flux_s)
    return field, image, last


def lat_flux(coef, own, other):
    flux = coef * (own - other)
    low = on_low_band()
    return jnp.where(low, flux, 0.0), jnp.where(low, 0.0, -flux)


def edge_rows(i, block, east_ref, west_ref):
    west_ref[i : i + 1, :] = block[:, :EDGE].T[0:1, :]
    east_ref[i : i + 1, :] = block[:, EDGE:].T[EDGE - 1 :, :]


def boundary_row(ref):
    return jnp.where(on_low_band(), ref[ref.shape[0] - 1 :, :], ref[0:1, :])


def first_kernel(
    wet_hbm, rhs_hbm, left_hbm, right_hbm, ef_hbm, nf_hbm,
    z_ref, short_ref, rhs_ref, left_ref, right_ref, ef_ref, nf_ref, wet_ref, to_e, to_w, to_a, to_b, to_l, sum_ref,
    list_ref, flags_ref, sems,
):
    tile_rows = rhs_hbm.shape[0] // EDGE
    tiles = 2 * tile_rows
    used = [0]

    def load(source, target):
        copy = pltpu.make_async_copy(source, target, sems.at[used[0]])
        used[0] += 1
        copy.start()
        return copy

    listing = load(wet_hbm, list_ref)
    loads = {}
    for at, stop in ((0, HEAD), (HEAD, tile_rows)):
        rows, some = pl.ds(at * EDGE, (stop - at) * EDGE), pl.ds(at, stop - at)
        loads[at] = [
            load(rhs_hbm.at[rows], rhs_ref.at[rows]),
            load(left_hbm.at[some], left_ref.at[some]),
            load(right_hbm.at[some], right_ref.at[some]),
        ]
    faces = [load(ef_hbm, ef_ref), load(nf_hbm, nf_ref)]
    for ref in (wet_ref, to_e, to_w, to_l):
        ref[...] = jnp.zeros_like(ref)
    listing.wait()
    for t in range(flags_ref.shape[0]):
        flags_ref[t] = 0.0
    for k in range(tiles):
        flags_ref[list_ref[0, k]] = 1.0
    lane = lane_index(1, CELLS)
    for i in range(tile_rows):
        wet_ref[i : i + 1, :] = jnp.where(lane < EDGE, flags_ref[2 * i], flags_ref[2 * i + 1])
    sums = jnp.zeros(sum_ref.shape, F32)
    for i in range(tile_rows):
        for copy in loads.get(i, ()):
            copy.wait()
        rows = slice(i * EDGE, (i + 1) * EDGE)
        residual = rhs_ref[rows, :] * wet_ref[i : i + 1, :]
        rounded = residual.astype(BF16)
        parts = [
            rounded_product(left_ref[i, k], rounded[:, k * EDGE : (k + 1) * EDGE], right_ref[i, k]) for k in range(2)
        ]
        short = jnp.concatenate(parts, axis=1)
        short_ref[rows, :] = short
        precond = short.astype(F32)
        z_ref[rows, :] = precond
        edge_rows(i, precond, to_e, to_w)
        sums = sums + fold(residual * precond)
    sum_ref[...] = sums
    for copy in faces:
        copy.wait()
    for i in range(tile_rows):
        face = ef_ref[i * EDGE : (i + 1) * EDGE, EDGE:].astype(F32).T[EDGE - 1 :, :]
        to_e[ROWS + i : ROWS + i + 1, :] = face * wet_ref[i : i + 1, EDGE:]
    to_w[ROWS : ROWS + tile_rows, :] = wet_ref[:tile_rows, :EDGE]
    to_l[0:1, :] = boundary_row(z_ref)
    rows = tile_rows * EDGE
    last = nf_ref[rows - 16 : rows, :].astype(F32)[15:16, :] * wet_ref[tile_rows - 1 : tile_rows, :]
    to_l[1:2, :] = jnp.where(on_low_band(), last, wet_ref[0:1, :])
    odd = on_odd_sector()
    to_a[...] = jnp.where(odd, to_e[...], to_w[...])
    to_b[...] = jnp.where(odd, to_w[...], to_e[...])


def inner(z_ref, left_ref, right_ref, ef_ref, nf_ref, wet_ref, q_ref, w_ref, east_ref, west_ref):
    tile_rows = z_ref.shape[0] // EDGE
    east_ref[...] = jnp.zeros_like(east_ref)
    west_ref[...] = jnp.zeros_like(west_ref)
    south = top = jnp.zeros((1, CELLS), F32)
    for i in range(tile_rows):
        rows = slice(i * EDGE, (i + 1) * EDGE)
        _, image, south = stencil(i, tile_rows, z_ref, ef_ref, nf_ref, wet_ref, south, top)
        q_ref[rows, :] = image
        parts = [
            wide_product(left_ref[i, k], image[:, k * EDGE : (k + 1) * EDGE], right_ref[i, k]) for k in range(2)
        ]
        product = jnp.concatenate(parts, axis=1)
        w_ref[rows, :] = product
        edge_rows(i, product, east_ref, west_ref)


def early_inner_kernel(a_in, b_in, *refs):
    *arrays, to_a, to_b = refs
    to_a[...] = a_in[...]
    to_b[...] = b_in[...]

    @pl.when(held_up())
    def _():
        inner(*arrays)


def late_inner_kernel(*refs):
    @pl.when(jnp.logical_not(held_up()))
    def _():
        inner(*refs)


def lat_kernel(early_w, late_w, left_ref, right_ref, to_l, in_l, lat_ref, row_e, row_w):
    tile_rows = early_w.shape[0] // EDGE
    low = on_low_band()
    end = tile_rows - 1
    flux = to_l[1:2, :] * in_l[1:2, :] * (to_l[0:1, :] - in_l[0:1, :])
    pick = (lane_index(16, EDGE) == jnp.where(low, EDGE - 1, 0)) & (row_index(16, EDGE) == 0)
    pick = jnp.where(pick, 1.0, 0.0).astype(BF16)
    boundary = jnp.where(held_up(), boundary_row(early_w), boundary_row(late_w))
    for ref in (lat_ref, row_e, row_w):
        ref[...] = jnp.zeros_like(ref)
    for k in range(2):
        at = slice(k * EDGE, (k + 1) * EDGE)
        left = jnp.where(low, left_ref[end, k], left_ref[0, k])
        right = jnp.where(low, right_ref[end, k], right_ref[0, k])
        by_col = dot_nt(pick, left)[0:1, :]
        by_row = dot(jnp.concatenate(split(jnp.broadcast_to(flux[:, at], (16, EDGE))), axis=0), right)
        by_row = by_row[0:1, :] + by_row[16:17, :]
        lat_ref[0:1, at] = by_col
        lat_ref[1:2, at] = by_row
        lat_ref[3:4, at] = boundary[:, at] + jnp.where(low, by_col[:, EDGE - 1 :], by_col[:, 0:1]) * by_row
    lat_ref[2:3, :] = flux
    for i in range(tile_rows):
        row_e[i : i + 1, :] = right_ref[i, 1, EDGE - 16 :, :].astype(F32)[15:16, :]
        row_w[i : i + 1, :] = right_ref[i, 0, 0:16, :].astype(F32)[0:1, :]


def one_side(side, left_ref, lat_ref, row_ref, early_rows, late_rows, own, in_b, in_a, edge_ref, coef, flux, turn):
    tile_rows = left_ref.shape[0]
    at = slice(side * EDGE, (side + 1) * EDGE)
    rim = side * (EDGE - 1)
    odd = on_odd_sector()
    other = jnp.where(odd, in_a[...], in_b[...]) if side else jnp.where(odd, in_b[...], in_a[...])
    coef[...] = own[ROWS:, :] * other[ROWS:, :]
    flux[...] = coef[...] * (own[:ROWS, :] - other[:ROWS, :])
    turn[...] = jnp.zeros_like(turn)
    spread = jnp.concatenate(split(flux[...]), axis=0)
    for i in range(tile_rows):
        turned = dot_nt(spread, left_ref[i, side])
        turn[i : i + 1, :] = turned[i : i + 1, :] + turned[ROWS + i : ROWS + i + 1, :]
    here = row_index(ROWS, EDGE) == jnp.where(on_low_band(), tile_rows - 1, 0)
    by_lat = lat_ref[0:1, at] * lat_ref[1:2, at][:, rim : rim + 1]
    rows = jnp.where(held_up(), early_rows[...], late_rows[...]) + jnp.where(here, by_lat, 0.0)
    edge_ref[...] = rows + turn[...] * row_ref[:, rim : rim + 1]


def edge_kernel(
    left_ref, lat_ref, row_e, row_w, early_e, late_e, early_w, late_w, to_e, to_w, in_b, in_a,
    east_ref, coef_e, flux_e, turn_e, west_ref, coef_w, flux_w, turn_w, to_l2,
):
    one_side(1, left_ref, lat_ref, row_e, early_e, late_e, to_e, in_b, in_a, east_ref, coef_e, flux_e, turn_e)
    one_side(0, left_ref, lat_ref, row_w, early_w, late_w, to_w, in_b, in_a, west_ref, coef_w, flux_w, turn_w)
    end = left_ref.shape[0] - 1
    low = on_low_band()
    by_lon = [
        jnp.where(low, turn[end : end + 1, EDGE - 1 :] * row[end : end + 1, :], turn[0:1, 0:1] * row[0:1, :])
        for turn, row in ((turn_w, row_w), (turn_e, row_e))
    ]
    to_l2[...] = jnp.zeros_like(to_l2)
    to_l2[0:1, :] = lat_ref[3:4, :] + jnp.concatenate(by_lon, axis=1)


def middle(
    z_ref, rhs_ref, q_ref, w_in, ef_ref, nf_ref, wet_ref, lat_ref, turn_e, turn_w, right_e, right_w, sum_in, w_ref, sums_ref
):
    tile_rows = z_ref.shape[0] // EDGE
    zero = jnp.zeros((8, CELLS), F32)
    zq, rw, qw, faces, squares = zero, zero, zero, zero, zero

    def complete(i, zq, rw, qw):
        rows = slice(i * EDGE, (i + 1) * EDGE)
        image = q_ref[rows, :]
        product = w_in[rows, :] + jnp.concatenate(
            [column(turn_w, i) * right_w[i : i + 1, :], column(turn_e, i) * right_e[i : i + 1, :]], axis=1
        )
        if i in (0, tile_rows - 1):
            here = on_low_band() == (i > 0)
            by_row = jnp.where(here, lat_ref[1:2, :], 0.0)
            by_col = [jnp.broadcast_to(lat_ref[0:1, k * EDGE : (k + 1) * EDGE], (EDGE, EDGE)).T for k in range(2)]
            product = product + jnp.concatenate(by_col, axis=1) * by_row
        w_ref[rows, :] = product
        return zq + fold(z_ref[rows, :] * image), rw + fold(rhs_ref[rows, :] * product), qw + fold(image * product)

    zq, rw, qw = complete(0, zq, rw, qw)
    for i in range(tile_rows):
        if i + 1 < tile_rows:
            zq, rw, qw = complete(i + 1, zq, rw, qw)
        rows = slice(i * EDGE, (i + 1) * EDGE)
        field, over_e, over_n, east_wet, north_wet = differences(i, tile_rows, w_ref, wet_ref)
        by_e = ef_ref[rows, :].astype(F32) * east_wet * (over_e * over_e)
        by_n = nf_ref[rows, :].astype(F32) * (over_n * over_n)
        by_n = set_row(by_n, -1, 0.0 if i == tile_rows - 1 else by_n[EDGE - 1 :, :] * north_wet)
        faces = faces + fold(by_e + by_n)
        squares = squares + fold(field * field)
    for k, total in enumerate((sum_in[...], zq, rw, qw, faces + surface_term * squares)):
        sums_ref[k] = total


def early_middle_kernel(west_in, *refs):
    *arrays, to_w = refs
    to_w[...] = west_in[...]

    @pl.when(held_up())
    def _():
        middle(*arrays)


def late_middle_kernel(early_w, early_sums, *refs):
    w_ref, sums_ref = refs[-2:]
    early = held_up()

    @pl.when(early)
    def _():
        w_ref[...] = early_w[...]
        sums_ref[...] = early_sums[...]

    @pl.when(jnp.logical_not(early))
    def _():
        middle(*refs)


def sums_kernel(
    sums_in, east_ref, west_ref, to_e, to_w, lat_ref, flux_e1, flux_w1, coef_w, own_l, own_l2, in_l, from_w, in_l2,
    packed_ref, flux_w, flux_l,
):
    over_w = west_ref[...] - from_w[...]
    flux_w[...] = coef_w[...] * over_w
    top, bottom = lat_flux(own_l[1:2, :] * in_l[1:2, :], own_l2[0:1, :], in_l2[0:1, :])
    flux_l[...] = jnp.zeros_like(flux_l)
    flux_l[0:1, :] = top
    flux_l[1:2, :] = -bottom

    outer = {
        1: total(flux_e1[...] * to_e[:ROWS, :] + flux_w1[...] * to_w[:ROWS, :])
        + total(lat_ref[2:3, :] * own_l[0:1, :]),
        3: total(flux_e1[...] * east_ref[...] + flux_w1[...] * west_ref[...])
        + total(lat_ref[2:3, :] * own_l2[0:1, :]),
        4: total(flux_w[...] * over_w) + total((top - bottom) * own_l2[0:1, :]),
    }
    lane = lane_index(1, EDGE)
    packed = jnp.zeros((1, EDGE), F32)
    for k in range(5):
        value = total(sums_in[k])
        packed = jnp.where(lane == k, value + outer[k] if k in outer else value, packed)
    packed_ref[...] = jnp.broadcast_to(packed, packed_ref.shape)


def outer_kernel(
    left_hbm, right_hbm, ef_hbm, nf_hbm, w_ref, wet_ref, east_ref, coef_e, from_e, flux_w, flux_l, sums_ref,
    u_ref, share_ref, left_ref, right_ref, ef_ref, nf_ref, flux_e, sems,
):
    tile_rows = w_ref.shape[0] // EDGE
    step = tile_rows // 2
    loads = []
    for k in range(tile_rows // step):
        rows, some = pl.ds(k * step * EDGE, step * EDGE), pl.ds(k * step, step)
        group = [
            pltpu.make_async_copy(source.at[place], target.at[place], sems.at[4 * k + n])
            for n, (source, target, place) in enumerate(
                ((ef_hbm, ef_ref, rows), (nf_hbm, nf_ref, rows), (left_hbm, left_ref, some), (right_hbm, right_ref, some))
            )
        ]
        for copy in group:
            copy.start()
        loads.append(group)
    flux_e[...] = coef_e[...] * (east_ref[...] - from_e[...])
    lane = lane_index(EDGE, EDGE)
    south, top = -flux_l[1:2, :], flux_l[0:1, :]
    zq, qw = (total(sums_ref[k]) for k in (1, 3))
    share = jnp.where(zq > 0.0, qw / jnp.where(zq > 0.0, zq, 1.0), 0.0)
    share_ref[...] = jnp.broadcast_to(share, share_ref.shape)
    for i in range(tile_rows):
        if i % step == 0:
            for copy in loads[i // step]:
                copy.wait()
        _, image, south = stencil(i, tile_rows, w_ref, ef_ref, nf_ref, wet_ref, south, top)
        image = image + jnp.concatenate(
            [jnp.where(lane == 0, column(flux_w, i), 0.0), jnp.where(lane == EDGE - 1, column(flux_e, i), 0.0)], axis=1
        )
        parts = [
            wide_product(left_ref[i, k], image[:, k * EDGE : (k + 1) * EDGE], right_ref[i, k]) for k in range(2)
        ]
        rows = slice(i * EDGE, (i + 1) * EDGE)
        u_ref[rows, :] = (jnp.concatenate(parts, axis=1) - share * w_ref[rows, :]).astype(BF16)


def last_kernel(all_ref, z_ref, w_ref, u_ref, share_ref, sol_hbm, pre_hbm, sol_ref, pre_ref, sems):
    tile_rows = z_ref.shape[0] // EDGE
    totals = jnp.sum(all_ref[...], axis=0, keepdims=True)
    lane = lane_index(1, EDGE)
    rz, zq, rw, qw, waw = (jnp.sum(jnp.where(lane == k, totals, 0.0), axis=1, keepdims=True) for k in range(5))
    step0 = rz / zq
    rz1 = step0 * (step0 * qw - rw)
    grow = 1.0 + rz1 / rz
    step1 = rz1 / (grow * grow * zq - 2.0 * grow * step0 * qw + step0 * step0 * waw)
    with_z = step0 + step1 * grow
    with_w = -step1 * step0
    less_w = with_z + with_w * share_ref[0:1, 0:1]
    group = 2 * EDGE
    stores = []
    for i in range(tile_rows * EDGE // group):
        rows = slice(i * group, (i + 1) * group)
        precond, product = z_ref[rows, :].astype(F32), w_ref[rows, :]
        sol_ref[rows, :] = with_z * precond + with_w * product
        pre_ref[rows, :] = (precond - less_w * product - with_w * u_ref[rows, :].astype(F32)).astype(BF16)
        place = pl.ds(i * group, group)
        for k, (source, target) in enumerate(((sol_ref, sol_hbm), (pre_ref, pre_hbm))):
            copy = pltpu.make_async_copy(source.at[place], target.at[place], sems.at[2 * i + k])
            copy.start()
            stores.append(copy)
    for copy in stores:
        copy.wait()


def call(kernel, outs, args, name, scratch=(), in_space=pltpu.VMEM, out_space=pltpu.VMEM, flops=0):
    if not isinstance(in_space, list):
        in_space = [in_space] * len(args)
    return pl.pallas_call(
        kernel,
        out_shape=outs,
        in_specs=[pl.BlockSpec(memory_space=space) for space in in_space],
        out_specs=[pl.BlockSpec(memory_space=out_space)] * len(outs),
        scratch_shapes=scratch,
        compiler_params=pltpu.CompilerParams(vmem_limit_bytes=VMEM_LIMIT),
        cost_estimate=pl.CostEstimate(flops=flops, bytes_accessed=0, transcendentals=0),
        name=name,
    )(*args)


def per_device(right_side, east_face, north_face, left_factor, right_factor, wet_list):
    rows, cols = right_side.shape
    lons, lats = lax.axis_size("lon"), lax.axis_size("lat")
    tile_rows = rows // EDGE
    shape = functools.partial(jax.ShapeDtypeStruct, dtype=F32)
    like = lambda a: jax.ShapeDtypeStruct(a.shape, a.dtype)
    field = shape((rows, cols))
    half = jax.ShapeDtypeStruct((rows, cols), BF16)
    edge = shape((ROWS, EDGE))
    message = shape((2 * ROWS, EDGE))
    strip = shape((8, cols))
    across = [(0, 1), (1, 0)]

    def pairs(parity):
        forward = [(i, (i + 1) % lons) for i in range(parity, lons, 2)]
        return forward + [(b, a) for a, b in forward]

    by_place = (tile_rows, 2, EDGE, EDGE)
    left_factor, right_factor = left_factor.reshape(by_place), right_factor.reshape(by_place)
    arguments = [
        pltpu.with_memory_space_constraint(a, pltpu.HBM)
        for a in (wet_list, right_side, left_factor, right_factor, east_face, north_face)
    ]
    z, short, rhs, left, right, ef, nf, wet, to_e, to_w, to_a, to_b, to_l, rz = call(
        first_kernel,
        [field, half, field, like(left_factor), like(right_factor), like(east_face), like(north_face),
         shape((ROWS, cols)), message, message, message, message, strip, strip],
        arguments, "first",
        [pltpu.SMEM(wet_list.shape, jnp.int32), pltpu.SMEM((32,), F32),
         pltpu.SemaphoreType.DMA((9,))],
        in_space=pltpu.HBM,
    )
    arrays = (z, left, right, ef, nf, wet)
    results = [field, field, edge, edge]
    *early, far_a, far_b = call(early_inner_kernel, results + [message, message], (to_a, to_b, *arrays), "early_inner")
    in_b = lax.ppermute(far_b, "lon", pairs(0))
    in_a = lax.ppermute(far_a, "lon", pairs(1))
    in_l = lax.ppermute(to_l, "lat", across)
    late = call(late_inner_kernel, results, arrays, "late_inner")
    lat, row_e, row_w = call(
        lat_kernel, [strip, edge, edge], (early[1], late[1], left, right, to_l, in_l), "lat"
    )
    east, coef_e, flux_e1, turn_e, west, coef_w, flux_w1, turn_w, to_l2 = call(
        edge_kernel, [edge] * 8 + [strip],
        (left, lat, row_e, row_w, early[2], late[2], early[3], late[3], to_e, to_w, in_b, in_a), "edges",
    )
    from_w2 = lax.ppermute(east, "lon", [(i, (i + 1) % lons) for i in range(lons)])
    in_l2 = lax.ppermute(to_l2, "lat", across)
    results = [field, shape((5, 8, cols))]
    faces = (ef, nf, wet, lat, turn_e, turn_w, row_e, row_w, rz)
    *done, to_w2 = call(early_middle_kernel, results + [edge], (west, z, rhs, *early[:2], *faces), "early_middle")
    from_e2 = lax.ppermute(to_w2, "lon", [((i + 1) % lons, i) for i in range(lons)])
    w, sums = call(late_middle_kernel, results, (*done, z, rhs, *late[:2], *faces), "late_middle")
    packed, flux_w, flux_l = call(
        sums_kernel, [shape((lons * lats, EDGE)), edge, strip],
        (sums, east, west, to_e, to_w, lat, flux_e1, flux_w1, coef_w, to_l, to_l2, in_l, from_w2, in_l2), "sums",
    )
    everyone = lax.all_to_all(packed, ("lon", "lat"), 0, 0, tiled=True)
    u, share = call(
        outer_kernel, [half, shape((8, EDGE))],
        (*arguments[2:], w, wet, east, coef_e, from_e2, flux_w, flux_l, sums), "outer",
        [pltpu.VMEM(a.shape, a.dtype) for a in arguments[2:]]
        + [pltpu.VMEM((ROWS, EDGE), F32), pltpu.SemaphoreType.DMA((8,))],
        in_space=[pltpu.HBM] * 4 + [pltpu.VMEM] * 8, flops=100_000_000_000,
    )
    return tuple(
        call(
            last_kernel, [field, half], (everyone, short, w, u, share), "last",
            [pltpu.VMEM((rows, cols), F32), pltpu.VMEM((rows, cols), BF16), pltpu.SemaphoreType.DMA((tile_rows,))],
            out_space=pltpu.HBM,
        )
    )


def solution(mesh):
    tiles = P("lat", "lon", None, None)
    cells = P("lat", "lon")
    return jax.shard_map(
        per_device,
        mesh=mesh,
        in_specs=(cells, cells, cells, tiles, tiles, cells),
        out_specs=(cells, cells),
        check_vma=False,
    )
```

```python
import functools

import jax
import jax.numpy as jnp
from jax import lax
from jax.experimental import pallas as pl
from jax.experimental.pallas import tpu as pltpu
from jax.sharding import PartitionSpec as P

EDGE = 128
CELLS = 2 * EDGE
surface_term = 0.0001
F32 = jnp.float32
BF16 = jnp.bfloat16
VMEM_LIMIT = 8 * 1024 * 1024
HEAD = 6
SPAN = 16
ROWS = 16


def dot(left, right):
    return jnp.dot(left, right, preferred_element_type=F32)


def dot_nt(left, right):
    return lax.dot_general(left, right, (((1,), (1,)), ((), ())), preferred_element_type=F32)


def lane_index(rows, cols):
    return lax.broadcasted_iota(jnp.int32, (rows, cols), 1)


def row_index(rows, cols):
    return lax.broadcasted_iota(jnp.int32, (rows, cols), 0)


def rounded_product(left, tile, right):
    partial = dot(left, tile).astype(BF16)
    return dot(partial, right).astype(BF16)


def split(value):
    high = value.astype(BF16)
    return high, (value - high.astype(F32)).astype(BF16)


def wide_product(left, tile, right):
    partial = dot(jnp.concatenate([left, left], axis=1), jnp.concatenate(split(tile), axis=0))
    return dot(jnp.concatenate(split(partial), axis=1), jnp.concatenate([right, right], axis=0))


def fold(block):
    total = block[0:8]
    for k in range(1, block.shape[0] // 8):
        total = total + block[8 * k : 8 * k + 8]
    return total


def total(value):
    return jnp.sum(jnp.sum(value, axis=0, keepdims=True), axis=1, keepdims=True)


def column(rows_ref, i):
    return jnp.broadcast_to(rows_ref[i : i + 1, :], (EDGE, EDGE)).T


def on_low_band():
    return lax.axis_index("lat") == 0


def on_odd_sector():
    return lax.axis_index("lon") % 2 == 1


def held_up():
    return lax.axis_index("lon") % SPAN == 0


def set_row(block, at, value):
    row = row_index(8, CELLS)
    if at == 0:
        return jnp.concatenate([jnp.where(row == 0, value, block[:8]), block[8:]], axis=0)
    return jnp.concatenate([block[:-8], jnp.where(row == 7, value, block[-8:])], axis=0)


def differences(i, tile_rows, field_ref, wet_ref):
    field = field_ref[i * EDGE : (i + 1) * EDGE, :]
    wet = wet_ref[i : i + 1, :]
    lane = lane_index(1, CELLS)
    both = wet * pltpu.roll(wet, EDGE, 1)
    east_wet = jnp.where(lane == EDGE - 1, both, jnp.where(lane == CELLS - 1, 0.0, 1.0))
    above = min((i + 1) * EDGE, tile_rows * EDGE - 1)
    north = set_row(pltpu.roll(field, EDGE - 1, 0), -1, field_ref[above : above + 1, :])
    north_wet = wet * wet_ref[i + 1 : i + 2, :]
    return field, field - pltpu.roll(field, CELLS - 1, 1), field - north, east_wet, north_wet


def stencil(i, tile_rows, field_ref, ef_ref, nf_ref, wet_ref, south_flux, top_flux):
    rows = slice(i * EDGE, (i + 1) * EDGE)
    field, over_e, over_n, east_wet, north_wet = differences(i, tile_rows, field_ref, wet_ref)
    flux_e = (ef_ref[rows, :].astype(F32) * east_wet) * over_e
    flux_n = nf_ref[rows, :].astype(F32) * over_n
    last = top_flux if i == tile_rows - 1 else flux_n[EDGE - 1 :, :] * north_wet
    flux_n = set_row(flux_n, -1, last)
    flux_s = set_row(pltpu.roll(flux_n, 1, 0), 0, south_flux)
    image = surface_term * field + (flux_e - pltpu.roll(flux_e, 1, 1)) + (flux_n - flux_s)
    return field, image, last


def lat_flux(coef, own, other):
    flux = coef * (own - other)
    low = on_low_band()
    return jnp.where(low, flux, 0.0), jnp.where(low, 0.0, -flux)


def edge_rows(i, block, east_ref, west_ref):
    west_ref[i : i + 1, :] = block[:, :EDGE].T[0:1, :]
    east_ref[i : i + 1, :] = block[:, EDGE:].T[EDGE - 1 :, :]


def boundary_row(ref):
    return jnp.where(on_low_band(), ref[ref.shape[0] - 1 :, :], ref[0:1, :])


def first_kernel(
    wet_hbm, rhs_hbm, left_hbm, right_hbm, ef_hbm, nf_hbm,
    z_ref, short_ref, rhs_ref, left_ref, right_ref, ef_ref, nf_ref, wet_ref, to_e, to_w, to_a, to_b, to_l, sum_ref,
    list_ref, flags_ref, sems,
):
    tile_rows = rhs_hbm.shape[0] // EDGE
    tiles = 2 * tile_rows
    used = [0]

    def load(source, target):
        copy = pltpu.make_async_copy(source, target, sems.at[used[0]])
        used[0] += 1
        copy.start()
        return copy

    listing = load(wet_hbm, list_ref)
    loads = {}
    for at, stop in ((0, HEAD), (HEAD, tile_rows)):
        rows, some = pl.ds(at * EDGE, (stop - at) * EDGE), pl.ds(at, stop - at)
        loads[at] = [
            load(rhs_hbm.at[rows], rhs_ref.at[rows]),
            load(left_hbm.at[some], left_ref.at[some]),
            load(right_hbm.at[some], right_ref.at[some]),
        ]
    faces = [load(ef_hbm, ef_ref), load(nf_hbm, nf_ref)]
    for ref in (wet_ref, to_e, to_w, to_l):
        ref[...] = jnp.zeros_like(ref)
    listing.wait()
    for t in range(flags_ref.shape[0]):
        flags_ref[t] = 0.0
    for k in range(tiles):
        flags_ref[list_ref[0, k]] = 1.0
    lane = lane_index(1, CELLS)
    for i in range(tile_rows):
        wet_ref[i : i + 1, :] = jnp.where(lane < EDGE, flags_ref[2 * i], flags_ref[2 * i + 1])
    sums = jnp.zeros(sum_ref.shape, F32)
    for i in range(tile_rows):
        for copy in loads.get(i, ()):
            copy.wait()
        rows = slice(i * EDGE, (i + 1) * EDGE)
        residual = rhs_ref[rows, :] * wet_ref[i : i + 1, :]
        rounded = residual.astype(BF16)
        parts = [
            rounded_product(left_ref[i, k], rounded[:, k * EDGE : (k + 1) * EDGE], right_ref[i, k]) for k in range(2)
        ]
        short = jnp.concatenate(parts, axis=1)
        short_ref[rows, :] = short
        precond = short.astype(F32)
        z_ref[rows, :] = precond
        edge_rows(i, precond, to_e, to_w)
        sums = sums + fold(residual * precond)
    sum_ref[...] = sums
    for copy in faces:
        copy.wait()
    for i in range(tile_rows):
        face = ef_ref[i * EDGE : (i + 1) * EDGE, EDGE:].astype(F32).T[EDGE - 1 :, :]
        to_e[ROWS + i : ROWS + i + 1, :] = face * wet_ref[i : i + 1, EDGE:]
    to_w[ROWS : ROWS + tile_rows, :] = wet_ref[:tile_rows, :EDGE]
    to_l[0:1, :] = boundary_row(z_ref)
    rows = tile_rows * EDGE
    last = nf_ref[rows - 16 : rows, :].astype(F32)[15:16, :] * wet_ref[tile_rows - 1 : tile_rows, :]
    to_l[1:2, :] = jnp.where(on_low_band(), last, wet_ref[0:1, :])
    odd = on_odd_sector()
    to_a[...] = jnp.where(odd, to_e[...], to_w[...])
    to_b[...] = jnp.where(odd, to_w[...], to_e[...])


def inner(z_ref, left_ref, right_ref, ef_ref, nf_ref, wet_ref, q_ref, w_ref, east_ref, west_ref):
    tile_rows = z_ref.shape[0] // EDGE
    east_ref[...] = jnp.zeros_like(east_ref)
    west_ref[...] = jnp.zeros_like(west_ref)
    south = top = jnp.zeros((1, CELLS), F32)
    for i in range(tile_rows):
        rows = slice(i * EDGE, (i + 1) * EDGE)
        _, image, south = stencil(i, tile_rows, z_ref, ef_ref, nf_ref, wet_ref, south, top)
        q_ref[rows, :] = image
        parts = [
            wide_product(left_ref[i, k], image[:, k * EDGE : (k + 1) * EDGE], right_ref[i, k]) for k in range(2)
        ]
        product = jnp.concatenate(parts, axis=1)
        w_ref[rows, :] = product
        edge_rows(i, product, east_ref, west_ref)


def early_inner_kernel(a_in, b_in, *refs):
    *arrays, to_a, to_b = refs
    to_a[...] = a_in[...]
    to_b[...] = b_in[...]

    @pl.when(held_up())
    def _():
        inner(*arrays)


def late_inner_kernel(*refs):
    @pl.when(jnp.logical_not(held_up()))
    def _():
        inner(*refs)


def lat_kernel(early_w, late_w, left_ref, right_ref, to_l, in_l, lat_ref, row_e, row_w):
    tile_rows = early_w.shape[0] // EDGE
    low = on_low_band()
    end = tile_rows - 1
    flux = to_l[1:2, :] * in_l[1:2, :] * (to_l[0:1, :] - in_l[0:1, :])
    pick = (lane_index(16, EDGE) == jnp.where(low, EDGE - 1, 0)) & (row_index(16, EDGE) == 0)
    pick = jnp.where(pick, 1.0, 0.0).astype(BF16)
    boundary = jnp.where(held_up(), boundary_row(early_w), boundary_row(late_w))
    for ref in (lat_ref, row_e, row_w):
        ref[...] = jnp.zeros_like(ref)
    for k in range(2):
        at = slice(k * EDGE, (k + 1) * EDGE)
        left = jnp.where(low, left_ref[end, k], left_ref[0, k])
        right = jnp.where(low, right_ref[end, k], right_ref[0, k])
        by_col = dot_nt(pick, left)[0:1, :]
        by_row = dot(jnp.concatenate(split(jnp.broadcast_to(flux[:, at], (16, EDGE))), axis=0), right)
        by_row = by_row[0:1, :] + by_row[16:17, :]
        lat_ref[0:1, at] = by_col
        lat_ref[1:2, at] = by_row
        lat_ref[3:4, at] = boundary[:, at] + jnp.where(low, by_col[:, EDGE - 1 :], by_col[:, 0:1]) * by_row
    lat_ref[2:3, :] = flux
    for i in range(tile_rows):
        row_e[i : i + 1, :] = right_ref[i, 1, EDGE - 16 :, :].astype(F32)[15:16, :]
        row_w[i : i + 1, :] = right_ref[i, 0, 0:16, :].astype(F32)[0:1, :]


def one_side(side, left_ref, lat_ref, row_ref, early_rows, late_rows, own, in_b, in_a, edge_ref, coef, flux, turn):
    tile_rows = left_ref.shape[0]
    at = slice(side * EDGE, (side + 1) * EDGE)
    rim = side * (EDGE - 1)
    odd = on_odd_sector()
    other = jnp.where(odd, in_a[...], in_b[...]) if side else jnp.where(odd, in_b[...], in_a[...])
    coef[...] = own[ROWS:, :] * other[ROWS:, :]
    flux[...] = coef[...] * (own[:ROWS, :] - other[:ROWS, :])
    turn[...] = jnp.zeros_like(turn)
    spread = jnp.concatenate(split(flux[...]), axis=0)
    for i in range(tile_rows):
        turned = dot_nt(spread, left_ref[i, side])
        turn[i : i + 1, :] = turned[i : i + 1, :] + turned[ROWS + i : ROWS + i + 1, :]
    here = row_index(ROWS, EDGE) == jnp.where(on_low_band(), tile_rows - 1, 0)
    by_lat = lat_ref[0:1, at] * lat_ref[1:2, at][:, rim : rim + 1]
    rows = jnp.where(held_up(), early_rows[...], late_rows[...]) + jnp.where(here, by_lat, 0.0)
    edge_ref[...] = rows + turn[...] * row_ref[:, rim : rim + 1]


def edge_kernel(
    left_ref, lat_ref, row_e, row_w, early_e, late_e, early_w, late_w, to_e, to_w, in_b, in_a,
    east_ref, coef_e, flux_e, turn_e, west_ref, coef_w, flux_w, turn_w, to_l2,
):
    one_side(1, left_ref, lat_ref, row_e, early_e, late_e, to_e, in_b, in_a, east_ref, coef_e, flux_e, turn_e)
    one_side(0, left_ref, lat_ref, row_w, early_w, late_w, to_w, in_b, in_a, west_ref, coef_w, flux_w, turn_w)
    end = left_ref.shape[0] - 1
    low = on_low_band()
    by_lon = [
        jnp.where(low, turn[end : end + 1, EDGE - 1 :] * row[end : end + 1, :], turn[0:1, 0:1] * row[0:1, :])
        for turn, row in ((turn_w, row_w), (turn_e, row_e))
    ]
    to_l2[...] = jnp.zeros_like(to_l2)
    to_l2[0:1, :] = lat_ref[3:4, :] + jnp.concatenate(by_lon, axis=1)


def middle(
    z_ref, rhs_ref, q_ref, w_in, ef_ref, nf_ref, wet_ref, lat_ref, turn_e, turn_w, right_e, right_w, sum_in, w_ref, sums_ref
):
    tile_rows = z_ref.shape[0] // EDGE
    zero = jnp.zeros((8, CELLS), F32)
    zq, rw, qw, faces, squares = zero, zero, zero, zero, zero

    def complete(i, zq, rw, qw):
        rows = slice(i * EDGE, (i + 1) * EDGE)
        image = q_ref[rows, :]
        product = w_in[rows, :] + jnp.concatenate(
            [column(turn_w, i) * right_w[i : i + 1, :], column(turn_e, i) * right_e[i : i + 1, :]], axis=1
        )
        if i in (0, tile_rows - 1):
            here = on_low_band() == (i > 0)
            by_row = jnp.where(here, lat_ref[1:2, :], 0.0)
            by_col = [jnp.broadcast_to(lat_ref[0:1, k * EDGE : (k + 1) * EDGE], (EDGE, EDGE)).T for k in range(2)]
            product = product + jnp.concatenate(by_col, axis=1) * by_row
        w_ref[rows, :] = product
        return zq + fold(z_ref[rows, :] * image), rw + fold(rhs_ref[rows, :] * product), qw + fold(image * product)

    zq, rw, qw = complete(0, zq, rw, qw)
    for i in range(tile_rows):
        if i + 1 < tile_rows:
            zq, rw, qw = complete(i + 1, zq, rw, qw)
        rows = slice(i * EDGE, (i + 1) * EDGE)
        field, over_e, over_n, east_wet, north_wet = differences(i, tile_rows, w_ref, wet_ref)
        by_e = ef_ref[rows, :].astype(F32) * east_wet * (over_e * over_e)
        by_n = nf_ref[rows, :].astype(F32) * (over_n * over_n)
        by_n = set_row(by_n, -1, 0.0 if i == tile_rows - 1 else by_n[EDGE - 1 :, :] * north_wet)
        faces = faces + fold(by_e + by_n)
        squares = squares + fold(field * field)
    for k, total in enumerate((sum_in[...], zq, rw, qw, faces + surface_term * squares)):
        sums_ref[k] = total


def early_middle_kernel(west_in, *refs):
    *arrays, to_w = refs
    to_w[...] = west_in[...]

    @pl.when(held_up())
    def _():
        middle(*arrays)


def late_middle_kernel(early_w, early_sums, *refs):
    w_ref, sums_ref = refs[-2:]
    early = held_up()

    @pl.when(early)
    def _():
        w_ref[...] = early_w[...]
        sums_ref[...] = early_sums[...]

    @pl.when(jnp.logical_not(early))
    def _():
        middle(*refs)


def sums_kernel(
    sums_in, east_ref, west_ref, to_e, to_w, lat_ref, flux_e1, flux_w1, coef_w, own_l, own_l2, in_l, from_w, in_l2,
    packed_ref, flux_w, flux_l,
):
    over_w = west_ref[...] - from_w[...]
    flux_w[...] = coef_w[...] * over_w
    top, bottom = lat_flux(own_l[1:2, :] * in_l[1:2, :], own_l2[0:1, :], in_l2[0:1, :])
    flux_l[...] = jnp.zeros_like(flux_l)
    flux_l[0:1, :] = top
    flux_l[1:2, :] = -bottom

    outer = {
        1: total(flux_e1[...] * to_e[:ROWS, :] + flux_w1[...] * to_w[:ROWS, :])
        + total(lat_ref[2:3, :] * own_l[0:1, :]),
        3: total(flux_e1[...] * east_ref[...] + flux_w1[...] * west_ref[...])
        + total(lat_ref[2:3, :] * own_l2[0:1, :]),
        4: total(flux_w[...] * over_w) + total((top - bottom) * own_l2[0:1, :]),
    }
    lane = lane_index(1, EDGE)
    packed = jnp.zeros((1, EDGE), F32)
    for k in range(5):
        value = total(sums_in[k])
        packed = jnp.where(lane == k, value + outer[k] if k in outer else value, packed)
    packed_ref[...] = jnp.broadcast_to(packed, packed_ref.shape)


def outer_kernel(
    left_hbm, right_hbm, ef_hbm, nf_hbm, w_ref, wet_ref, east_ref, coef_e, from_e, flux_w, flux_l, sums_ref,
    u_ref, share_ref, left_ref, right_ref, ef_ref, nf_ref, flux_e, sems,
):
    tile_rows = w_ref.shape[0] // EDGE
    step = tile_rows // 2
    loads = []
    for k in range(tile_rows // step):
        rows, some = pl.ds(k * step * EDGE, step * EDGE), pl.ds(k * step, step)
        group = [
            pltpu.make_async_copy(source.at[place], target.at[place], sems.at[4 * k + n])
            for n, (source, target, place) in enumerate(
                ((ef_hbm, ef_ref, rows), (nf_hbm, nf_ref, rows), (left_hbm, left_ref, some), (right_hbm, right_ref, some))
            )
        ]
        for copy in group:
            copy.start()
        loads.append(group)
    flux_e[...] = coef_e[...] * (east_ref[...] - from_e[...])
    lane = lane_index(EDGE, EDGE)
    south, top = -flux_l[1:2, :], flux_l[0:1, :]
    zq, qw = (total(sums_ref[k]) for k in (1, 3))
    share = jnp.where(zq > 0.0, qw / jnp.where(zq > 0.0, zq, 1.0), 0.0)
    share_ref[...] = jnp.broadcast_to(share, share_ref.shape)
    for i in range(tile_rows):
        if i % step == 0:
            for copy in loads[i // step]:
                copy.wait()
        _, image, south = stencil(i, tile_rows, w_ref, ef_ref, nf_ref, wet_ref, south, top)
        image = image + jnp.concatenate(
            [jnp.where(lane == 0, column(flux_w, i), 0.0), jnp.where(lane == EDGE - 1, column(flux_e, i), 0.0)], axis=1
        )
        parts = [
            wide_product(left_ref[i, k], image[:, k * EDGE : (k + 1) * EDGE], right_ref[i, k]) for k in range(2)
        ]
        rows = slice(i * EDGE, (i + 1) * EDGE)
        u_ref[rows, :] = (jnp.concatenate(parts, axis=1) - share * w_ref[rows, :]).astype(BF16)


def last_kernel(all_ref, z_ref, w_ref, u_ref, share_ref, sol_hbm, pre_hbm, sol_ref, pre_ref, sems):
    tile_rows = z_ref.shape[0] // EDGE
    totals = jnp.sum(all_ref[...], axis=0, keepdims=True)
    lane = lane_index(1, EDGE)
    rz, zq, rw, qw, waw = (jnp.sum(jnp.where(lane == k, totals, 0.0), axis=1, keepdims=True) for k in range(5))
    step0 = rz / zq
    rz1 = step0 * (step0 * qw - rw)
    grow = 1.0 + rz1 / rz
    step1 = rz1 / (grow * grow * zq - 2.0 * grow * step0 * qw + step0 * step0 * waw)
    with_z = step0 + step1 * grow
    with_w = -step1 * step0
    less_w = with_z + with_w * share_ref[0:1, 0:1]
    group = EDGE
    stores = []
    for i in range(tile_rows * EDGE // group):
        rows = slice(i * group, (i + 1) * group)
        precond, product = z_ref[rows, :].astype(F32), w_ref[rows, :]
        sol_ref[rows, :] = with_z * precond + with_w * product
        pre_ref[rows, :] = (precond - less_w * product - with_w * u_ref[rows, :].astype(F32)).astype(BF16)
        place = pl.ds(i * group, group)
        for k, (source, target) in enumerate(((sol_ref, sol_hbm), (pre_ref, pre_hbm))):
            copy = pltpu.make_async_copy(source.at[place], target.at[place], sems.at[2 * i + k])
            copy.start()
            stores.append(copy)
    for copy in stores:
        copy.wait()


def call(kernel, outs, args, name, scratch=(), in_space=pltpu.VMEM, out_space=pltpu.VMEM, flops=0):
    if not isinstance(in_space, list):
        in_space = [in_space] * len(args)
    return pl.pallas_call(
        kernel,
        out_shape=outs,
        in_specs=[pl.BlockSpec(memory_space=space) for space in in_space],
        out_specs=[pl.BlockSpec(memory_space=out_space)] * len(outs),
        scratch_shapes=scratch,
        compiler_params=pltpu.CompilerParams(vmem_limit_bytes=VMEM_LIMIT),
        cost_estimate=pl.CostEstimate(flops=flops, bytes_accessed=0, transcendentals=0),
        name=name,
    )(*args)


def per_device(right_side, east_face, north_face, left_factor, right_factor, wet_list):
    rows, cols = right_side.shape
    lons, lats = lax.axis_size("lon"), lax.axis_size("lat")
    tile_rows = rows // EDGE
    shape = functools.partial(jax.ShapeDtypeStruct, dtype=F32)
    like = lambda a: jax.ShapeDtypeStruct(a.shape, a.dtype)
    field = shape((rows, cols))
    half = jax.ShapeDtypeStruct((rows, cols), BF16)
    edge = shape((ROWS, EDGE))
    message = shape((2 * ROWS, EDGE))
    strip = shape((8, cols))
    across = [(0, 1), (1, 0)]

    def pairs(parity):
        forward = [(i, (i + 1) % lons) for i in range(parity, lons, 2)]
        return forward + [(b, a) for a, b in forward]

    by_place = (tile_rows, 2, EDGE, EDGE)
    left_factor, right_factor = left_factor.reshape(by_place), right_factor.reshape(by_place)
    arguments = [
        pltpu.with_memory_space_constraint(a, pltpu.HBM)
        for a in (wet_list, right_side, left_factor, right_factor, east_face, north_face)
    ]
    z, short, rhs, left, right, ef, nf, wet, to_e, to_w, to_a, to_b, to_l, rz = call(
        first_kernel,
        [field, half, field, like(left_factor), like(right_factor), like(east_face), like(north_face),
         shape((ROWS, cols)), message, message, message, message, strip, strip],
        arguments, "first",
        [pltpu.SMEM(wet_list.shape, jnp.int32), pltpu.SMEM((32,), F32),
         pltpu.SemaphoreType.DMA((9,))],
        in_space=pltpu.HBM,
    )
    arrays = (z, left, right, ef, nf, wet)
    results = [field, field, edge, edge]
    *early, far_a, far_b = call(early_inner_kernel, results + [message, message], (to_a, to_b, *arrays), "early_inner")
    in_b = lax.ppermute(far_b, "lon", pairs(0))
    in_a = lax.ppermute(far_a, "lon", pairs(1))
    in_l = lax.ppermute(to_l, "lat", across)
    late = call(late_inner_kernel, results, arrays, "late_inner")
    lat, row_e, row_w = call(
        lat_kernel, [strip, edge, edge], (early[1], late[1], left, right, to_l, in_l), "lat"
    )
    east, coef_e, flux_e1, turn_e, west, coef_w, flux_w1, turn_w, to_l2 = call(
        edge_kernel, [edge] * 8 + [strip],
        (left, lat, row_e, row_w, early[2], late[2], early[3], late[3], to_e, to_w, in_b, in_a), "edges",
    )
    from_w2 = lax.ppermute(east, "lon", [(i, (i + 1) % lons) for i in range(lons)])
    in_l2 = lax.ppermute(to_l2, "lat", across)
    results = [field, shape((5, 8, cols))]
    faces = (ef, nf, wet, lat, turn_e, turn_w, row_e, row_w, rz)
    *done, to_w2 = call(early_middle_kernel, results + [edge], (west, z, rhs, *early[:2], *faces), "early_middle")
    from_e2 = lax.ppermute(to_w2, "lon", [((i + 1) % lons, i) for i in range(lons)])
    w, sums = call(late_middle_kernel, results, (*done, z, rhs, *late[:2], *faces), "late_middle")
    packed, flux_w, flux_l = call(
        sums_kernel, [shape((lons * lats, EDGE)), edge, strip],
        (sums, east, west, to_e, to_w, lat, flux_e1, flux_w1, coef_w, to_l, to_l2, in_l, from_w2, in_l2), "sums",
    )
    everyone = lax.all_to_all(packed, ("lon", "lat"), 0, 0, tiled=True)
    u, share = call(
        outer_kernel, [half, shape((8, EDGE))],
        (*arguments[2:], w, wet, east, coef_e, from_e2, flux_w, flux_l, sums), "outer",
        [pltpu.VMEM(a.shape, a.dtype) for a in arguments[2:]]
        + [pltpu.VMEM((ROWS, EDGE), F32), pltpu.SemaphoreType.DMA((8,))],
        in_space=[pltpu.HBM] * 4 + [pltpu.VMEM] * 8, flops=100_000_000_000,
    )
    return tuple(
        call(
            last_kernel, [field, half], (everyone, short, w, u, share), "last",
            [pltpu.VMEM((rows, cols), F32), pltpu.VMEM((rows, cols), BF16), pltpu.SemaphoreType.DMA((2 * tile_rows,))],
            out_space=pltpu.HBM,
        )
    )


def solution(mesh):
    tiles = P("lat", "lon", None, None)
    cells = P("lat", "lon")
    return jax.shard_map(
        per_device,
        mesh=mesh,
        in_specs=(cells, cells, cells, tiles, tiles, cells),
        out_specs=(cells, cells),
        check_vma=False,
    )
```

```python
import functools

import jax
import jax.numpy as jnp
from jax import lax
from jax.experimental import pallas as pl
from jax.experimental.pallas import tpu as pltpu
from jax.sharding import PartitionSpec as P

EDGE = 128
CELLS = 2 * EDGE
surface_term = 0.0001
F32 = jnp.float32
BF16 = jnp.bfloat16
VMEM_LIMIT = 8 * 1024 * 1024
HEAD = 5
SPAN = 16
ROWS = 16


def dot(left, right):
    return jnp.dot(left, right, preferred_element_type=F32)


def dot_nt(left, right):
    return lax.dot_general(left, right, (((1,), (1,)), ((), ())), preferred_element_type=F32)


def lane_index(rows, cols):
    return lax.broadcasted_iota(jnp.int32, (rows, cols), 1)


def row_index(rows, cols):
    return lax.broadcasted_iota(jnp.int32, (rows, cols), 0)


def rounded_product(left, tile, right):
    partial = dot(left, tile).astype(BF16)
    return dot(partial, right).astype(BF16)


def split(value):
    high = value.astype(BF16)
    return high, (value - high.astype(F32)).astype(BF16)


def wide_product(left, tile, right):
    partial = dot(jnp.concatenate([left, left], axis=1), jnp.concatenate(split(tile), axis=0))
    return dot(jnp.concatenate(split(partial), axis=1), jnp.concatenate([right, right], axis=0))


def fold(block):
    total = block[0:8]
    for k in range(1, block.shape[0] // 8):
        total = total + block[8 * k : 8 * k + 8]
    return total


def total(value):
    return jnp.sum(jnp.sum(value, axis=0, keepdims=True), axis=1, keepdims=True)


def column(rows_ref, i):
    return jnp.broadcast_to(rows_ref[i : i + 1, :], (EDGE, EDGE)).T


def on_low_band():
    return lax.axis_index("lat") == 0


def on_odd_sector():
    return lax.axis_index("lon") % 2 == 1


def held_up():
    return lax.axis_index("lon") % SPAN == 0


def set_row(block, at, value):
    row = row_index(8, CELLS)
    if at == 0:
        return jnp.concatenate([jnp.where(row == 0, value, block[:8]), block[8:]], axis=0)
    return jnp.concatenate([block[:-8], jnp.where(row == 7, value, block[-8:])], axis=0)


def differences(i, tile_rows, field_ref, wet_ref):
    field = field_ref[i * EDGE : (i + 1) * EDGE, :]
    wet = wet_ref[i : i + 1, :]
    lane = lane_index(1, CELLS)
    both = wet * pltpu.roll(wet, EDGE, 1)
    east_wet = jnp.where(lane == EDGE - 1, both, jnp.where(lane == CELLS - 1, 0.0, 1.0))
    above = min((i + 1) * EDGE, tile_rows * EDGE - 1)
    north = set_row(pltpu.roll(field, EDGE - 1, 0), -1, field_ref[above : above + 1, :])
    north_wet = wet * wet_ref[i + 1 : i + 2, :]
    return field, field - pltpu.roll(field, CELLS - 1, 1), field - north, east_wet, north_wet


def stencil(i, tile_rows, field_ref, ef_ref, nf_ref, wet_ref, south_flux, top_flux):
    rows = slice(i * EDGE, (i + 1) * EDGE)
    field, over_e, over_n, east_wet, north_wet = differences(i, tile_rows, field_ref, wet_ref)
    flux_e = (ef_ref[rows, :].astype(F32) * east_wet) * over_e
    flux_n = nf_ref[rows, :].astype(F32) * over_n
    last = top_flux if i == tile_rows - 1 else flux_n[EDGE - 1 :, :] * north_wet
    flux_n = set_row(flux_n, -1, last)
    flux_s = set_row(pltpu.roll(flux_n, 1, 0), 0, south_flux)
    image = surface_term * field + (flux_e - pltpu.roll(flux_e, 1, 1)) + (flux_n - flux_s)
    return field, image, last


def lat_flux(coef, own, other):
    flux = coef * (own - other)
    low = on_low_band()
    return jnp.where(low, flux, 0.0), jnp.where(low, 0.0, -flux)


def edge_rows(i, block, east_ref, west_ref):
    west_ref[i : i + 1, :] = block[:, :EDGE].T[0:1, :]
    east_ref[i : i + 1, :] = block[:, EDGE:].T[EDGE - 1 :, :]


def boundary_row(ref):
    return jnp.where(on_low_band(), ref[ref.shape[0] - 1 :, :], ref[0:1, :])


def first_kernel(
    wet_hbm, rhs_hbm, left_hbm, right_hbm, ef_hbm, nf_hbm,
    short_ref, rhs_ref, left_ref, right_ref, ef_ref, nf_ref, wet_ref, to_e, to_w, to_a, to_b, to_l,
    list_ref, flags_ref, sems,
):
    tile_rows = rhs_hbm.shape[0] // EDGE
    tiles = 2 * tile_rows
    used = [0]

    def load(source, target):
        copy = pltpu.make_async_copy(source, target, sems.at[used[0]])
        used[0] += 1
        copy.start()
        return copy

    listing = load(wet_hbm, list_ref)
    loads = {}
    for at, stop in ((0, HEAD), (HEAD, tile_rows)):
        rows, some = pl.ds(at * EDGE, (stop - at) * EDGE), pl.ds(at, stop - at)
        loads[at] = [
            load(rhs_hbm.at[rows], rhs_ref.at[rows]),
            load(left_hbm.at[some], left_ref.at[some]),
            load(right_hbm.at[some], right_ref.at[some]),
        ]
    faces = [load(ef_hbm, ef_ref), load(nf_hbm, nf_ref)]
    for ref in (wet_ref, to_e, to_w, to_l):
        ref[...] = jnp.zeros_like(ref)
    listing.wait()
    for t in range(flags_ref.shape[0]):
        flags_ref[t] = 0.0
    for k in range(tiles):
        flags_ref[list_ref[0, k]] = 1.0
    lane = lane_index(1, CELLS)
    for i in range(tile_rows):
        wet_ref[i : i + 1, :] = jnp.where(lane < EDGE, flags_ref[2 * i], flags_ref[2 * i + 1])
    for i in range(tile_rows):
        for copy in loads.get(i, ()):
            copy.wait()
        rows = slice(i * EDGE, (i + 1) * EDGE)
        residual = rhs_ref[rows, :] * wet_ref[i : i + 1, :]
        rounded = residual.astype(BF16)
        parts = [
            rounded_product(left_ref[i, k], rounded[:, k * EDGE : (k + 1) * EDGE], right_ref[i, k]) for k in range(2)
        ]
        short = jnp.concatenate(parts, axis=1)
        short_ref[rows, :] = short
        to_w[i : i + 1, :] = parts[0].T[0:16, :].astype(F32)[0:1, :]
        to_e[i : i + 1, :] = parts[1].T[EDGE - 16 :, :].astype(F32)[15:16, :]
    for copy in faces:
        copy.wait()
    for i in range(tile_rows):
        face = ef_ref[i * EDGE : (i + 1) * EDGE, EDGE:].T[EDGE - 16 :, :].astype(F32)[15:16, :]
        to_e[ROWS + i : ROWS + i + 1, :] = face * wet_ref[i : i + 1, EDGE:]
    to_w[ROWS : ROWS + tile_rows, :] = wet_ref[:tile_rows, :EDGE]
    rows = tile_rows * EDGE
    upper, lower = short_ref[rows - 16 : rows, :].astype(F32), short_ref[0:16, :].astype(F32)
    to_l[0:1, :] = jnp.where(on_low_band(), upper[15:16, :], lower[0:1, :])
    last = nf_ref[rows - 16 : rows, :].astype(F32)[15:16, :] * wet_ref[tile_rows - 1 : tile_rows, :]
    to_l[1:2, :] = jnp.where(on_low_band(), last, wet_ref[0:1, :])
    odd = on_odd_sector()
    to_a[...] = jnp.where(odd, to_e[...], to_w[...])
    to_b[...] = jnp.where(odd, to_w[...], to_e[...])


def inner(short_ref, left_ref, right_ref, ef_ref, nf_ref, wet_ref, q_ref, w_ref, east_ref, west_ref, z_ref):
    tile_rows = z_ref.shape[0] // EDGE
    east_ref[...] = jnp.zeros_like(east_ref)
    west_ref[...] = jnp.zeros_like(west_ref)
    south = top = jnp.zeros((1, CELLS), F32)
    z_ref[...] = short_ref[...].astype(F32)
    for i in range(tile_rows):
        rows = slice(i * EDGE, (i + 1) * EDGE)
        _, image, south = stencil(i, tile_rows, z_ref, ef_ref, nf_ref, wet_ref, south, top)
        q_ref[rows, :] = image
        parts = [
            wide_product(left_ref[i, k], image[:, k * EDGE : (k + 1) * EDGE], right_ref[i, k]) for k in range(2)
        ]
        product = jnp.concatenate(parts, axis=1)
        w_ref[rows, :] = product
        edge_rows(i, product, east_ref, west_ref)


def early_inner_kernel(a_in, b_in, *refs):
    *arrays, to_a, to_b, z_ref = refs
    to_a[...] = a_in[...]
    to_b[...] = b_in[...]

    @pl.when(held_up())
    def _():
        inner(*arrays, z_ref)


def late_inner_kernel(*refs):
    @pl.when(jnp.logical_not(held_up()))
    def _():
        inner(*refs)


def lat_kernel(early_w, late_w, left_ref, right_ref, to_l, in_l, lat_ref, row_e, row_w):
    tile_rows = early_w.shape[0] // EDGE
    low = on_low_band()
    end = tile_rows - 1
    flux = to_l[1:2, :] * in_l[1:2, :] * (to_l[0:1, :] - in_l[0:1, :])
    pick = (lane_index(16, EDGE) == jnp.where(low, EDGE - 1, 0)) & (row_index(16, EDGE) == 0)
    pick = jnp.where(pick, 1.0, 0.0).astype(BF16)
    boundary = jnp.where(held_up(), boundary_row(early_w), boundary_row(late_w))
    for ref in (lat_ref, row_e, row_w):
        ref[...] = jnp.zeros_like(ref)
    for k in range(2):
        at = slice(k * EDGE, (k + 1) * EDGE)
        left = jnp.where(low, left_ref[end, k], left_ref[0, k])
        right = jnp.where(low, right_ref[end, k], right_ref[0, k])
        by_col = dot_nt(pick, left)[0:1, :]
        by_row = dot(jnp.concatenate(split(jnp.broadcast_to(flux[:, at], (16, EDGE))), axis=0), right)
        by_row = by_row[0:1, :] + by_row[16:17, :]
        lat_ref[0:1, at] = by_col
        lat_ref[1:2, at] = by_row
        lat_ref[3:4, at] = boundary[:, at] + jnp.where(low, by_col[:, EDGE - 1 :], by_col[:, 0:1]) * by_row
    lat_ref[2:3, :] = flux
    for i in range(tile_rows):
        row_e[i : i + 1, :] = right_ref[i, 1, EDGE - 16 :, :].astype(F32)[15:16, :]
        row_w[i : i + 1, :] = right_ref[i, 0, 0:16, :].astype(F32)[0:1, :]


def one_side(side, left_ref, lat_ref, row_ref, early_rows, late_rows, own, in_b, in_a, edge_ref, coef, flux, turn):
    tile_rows = left_ref.shape[0]
    at = slice(side * EDGE, (side + 1) * EDGE)
    rim = side * (EDGE - 1)
    odd = on_odd_sector()
    other = jnp.where(odd, in_a[...], in_b[...]) if side else jnp.where(odd, in_b[...], in_a[...])
    coef[...] = own[ROWS:, :] * other[ROWS:, :]
    flux[...] = coef[...] * (own[:ROWS, :] - other[:ROWS, :])
    turn[...] = jnp.zeros_like(turn)
    spread = jnp.concatenate(split(flux[...]), axis=0)
    for i in range(tile_rows):
        turned = dot_nt(spread, left_ref[i, side])
        turn[i : i + 1, :] = turned[i : i + 1, :] + turned[ROWS + i : ROWS + i + 1, :]
    here = row_index(ROWS, EDGE) == jnp.where(on_low_band(), tile_rows - 1, 0)
    by_lat = lat_ref[0:1, at] * lat_ref[1:2, at][:, rim : rim + 1]
    rows = jnp.where(held_up(), early_rows[...], late_rows[...]) + jnp.where(here, by_lat, 0.0)
    edge_ref[...] = rows + turn[...] * row_ref[:, rim : rim + 1]


def edge_kernel(
    left_ref, lat_ref, row_e, row_w, early_e, late_e, early_w, late_w, to_e, to_w, in_b, in_a,
    east_ref, coef_e, flux_e, turn_e, west_ref, coef_w, flux_w, turn_w, to_l2,
):
    one_side(1, left_ref, lat_ref, row_e, early_e, late_e, to_e, in_b, in_a, east_ref, coef_e, flux_e, turn_e)
    one_side(0, left_ref, lat_ref, row_w, early_w, late_w, to_w, in_b, in_a, west_ref, coef_w, flux_w, turn_w)
    end = left_ref.shape[0] - 1
    low = on_low_band()
    by_lon = [
        jnp.where(low, turn[end : end + 1, EDGE - 1 :] * row[end : end + 1, :], turn[0:1, 0:1] * row[0:1, :])
        for turn, row in ((turn_w, row_w), (turn_e, row_e))
    ]
    to_l2[...] = jnp.zeros_like(to_l2)
    to_l2[0:1, :] = lat_ref[3:4, :] + jnp.concatenate(by_lon, axis=1)


def middle(
    z_ref, rhs_ref, q_ref, w_in, ef_ref, nf_ref, wet_ref, lat_ref, turn_e, turn_w, right_e, right_w, w_ref, sums_ref
):
    tile_rows = z_ref.shape[0] // EDGE
    zero = jnp.zeros((8, CELLS), F32)
    rz, zq, rw, qw, faces, squares = zero, zero, zero, zero, zero, zero

    def complete(i, rz, zq, rw, qw):
        rows = slice(i * EDGE, (i + 1) * EDGE)
        image = q_ref[rows, :]
        product = w_in[rows, :] + jnp.concatenate(
            [column(turn_w, i) * right_w[i : i + 1, :], column(turn_e, i) * right_e[i : i + 1, :]], axis=1
        )
        if i in (0, tile_rows - 1):
            here = on_low_band() == (i > 0)
            by_row = jnp.where(here, lat_ref[1:2, :], 0.0)
            by_col = [jnp.broadcast_to(lat_ref[0:1, k * EDGE : (k + 1) * EDGE], (EDGE, EDGE)).T for k in range(2)]
            product = product + jnp.concatenate(by_col, axis=1) * by_row
        w_ref[rows, :] = product
        precond, given = z_ref[rows, :].astype(F32), rhs_ref[rows, :]
        rz, zq = rz + fold(given * precond), zq + fold(precond * image)
        return rz, zq, rw + fold(given * product), qw + fold(image * product)

    rz, zq, rw, qw = complete(0, rz, zq, rw, qw)
    for i in range(tile_rows):
        if i + 1 < tile_rows:
            rz, zq, rw, qw = complete(i + 1, rz, zq, rw, qw)
        rows = slice(i * EDGE, (i + 1) * EDGE)
        field, over_e, over_n, east_wet, north_wet = differences(i, tile_rows, w_ref, wet_ref)
        by_e = ef_ref[rows, :].astype(F32) * east_wet * (over_e * over_e)
        by_n = nf_ref[rows, :].astype(F32) * (over_n * over_n)
        by_n = set_row(by_n, -1, 0.0 if i == tile_rows - 1 else by_n[EDGE - 1 :, :] * north_wet)
        faces = faces + fold(by_e + by_n)
        squares = squares + fold(field * field)
    for k, total in enumerate((rz, zq, rw, qw, faces + surface_term * squares)):
        sums_ref[k] = total


def early_middle_kernel(west_in, *refs):
    *arrays, to_w = refs
    to_w[...] = west_in[...]

    @pl.when(held_up())
    def _():
        middle(*arrays)


def late_middle_kernel(early_w, early_sums, *refs):
    w_ref, sums_ref = refs[-2:]
    early = held_up()

    @pl.when(early)
    def _():
        w_ref[...] = early_w[...]
        sums_ref[...] = early_sums[...]

    @pl.when(jnp.logical_not(early))
    def _():
        middle(*refs)


def sums_kernel(
    sums_in, east_ref, west_ref, to_e, to_w, lat_ref, flux_e1, flux_w1, coef_w, own_l, own_l2, in_l, from_w, in_l2,
    packed_ref, flux_w, flux_l,
):
    over_w = west_ref[...] - from_w[...]
    flux_w[...] = coef_w[...] * over_w
    top, bottom = lat_flux(own_l[1:2, :] * in_l[1:2, :], own_l2[0:1, :], in_l2[0:1, :])
    flux_l[...] = jnp.zeros_like(flux_l)
    flux_l[0:1, :] = top
    flux_l[1:2, :] = -bottom

    outer = {
        1: total(flux_e1[...] * to_e[:ROWS, :] + flux_w1[...] * to_w[:ROWS, :])
        + total(lat_ref[2:3, :] * own_l[0:1, :]),
        3: total(flux_e1[...] * east_ref[...] + flux_w1[...] * west_ref[...])
        + total(lat_ref[2:3, :] * own_l2[0:1, :]),
        4: total(flux_w[...] * over_w) + total((top - bottom) * own_l2[0:1, :]),
    }
    lane = lane_index(1, EDGE)
    packed = jnp.zeros((1, EDGE), F32)
    for k in range(5):
        value = total(sums_in[k])
        packed = jnp.where(lane == k, value + outer[k] if k in outer else value, packed)
    packed_ref[...] = jnp.broadcast_to(packed, packed_ref.shape)


def outer_kernel(
    left_hbm, right_hbm, ef_hbm, nf_hbm, w_ref, wet_ref, east_ref, coef_e, from_e, flux_w, flux_l, sums_ref,
    u_ref, share_ref, left_ref, right_ref, ef_ref, nf_ref, flux_e, sems,
):
    tile_rows = w_ref.shape[0] // EDGE
    step = tile_rows // 2
    loads = []
    for k in range(tile_rows // step):
        rows, some = pl.ds(k * step * EDGE, step * EDGE), pl.ds(k * step, step)
        group = [
            pltpu.make_async_copy(source.at[place], target.at[place], sems.at[4 * k + n])
            for n, (source, target, place) in enumerate(
                ((ef_hbm, ef_ref, rows), (nf_hbm, nf_ref, rows), (left_hbm, left_ref, some), (right_hbm, right_ref, some))
            )
        ]
        for copy in group:
            copy.start()
        loads.append(group)
    flux_e[...] = coef_e[...] * (east_ref[...] - from_e[...])
    lane = lane_index(EDGE, EDGE)
    south, top = -flux_l[1:2, :], flux_l[0:1, :]
    zq, qw = (total(sums_ref[k]) for k in (1, 3))
    share = jnp.where(zq > 0.0, qw / jnp.where(zq > 0.0, zq, 1.0), 0.0)
    share_ref[...] = jnp.broadcast_to(share, share_ref.shape)
    for i in range(tile_rows):
        if i % step == 0:
            for copy in loads[i // step]:
                copy.wait()
        _, image, south = stencil(i, tile_rows, w_ref, ef_ref, nf_ref, wet_ref, south, top)
        image = image + jnp.concatenate(
            [jnp.where(lane == 0, column(flux_w, i), 0.0), jnp.where(lane == EDGE - 1, column(flux_e, i), 0.0)], axis=1
        )
        parts = [
            wide_product(left_ref[i, k], image[:, k * EDGE : (k + 1) * EDGE], right_ref[i, k]) for k in range(2)
        ]
        rows = slice(i * EDGE, (i + 1) * EDGE)
        u_ref[rows, :] = (jnp.concatenate(parts, axis=1) - share * w_ref[rows, :]).astype(BF16)


def last_kernel(all_ref, z_ref, w_ref, u_ref, share_ref, sol_hbm, pre_hbm, sol_ref, pre_ref, sems):
    tile_rows = z_ref.shape[0] // EDGE
    totals = jnp.sum(all_ref[...], axis=0, keepdims=True)
    lane = lane_index(1, EDGE)
    rz, zq, rw, qw, waw = (jnp.sum(jnp.where(lane == k, totals, 0.0), axis=1, keepdims=True) for k in range(5))
    step0 = rz / zq
    rz1 = step0 * (step0 * qw - rw)
    grow = 1.0 + rz1 / rz
    step1 = rz1 / (grow * grow * zq - 2.0 * grow * step0 * qw + step0 * step0 * waw)
    with_z = step0 + step1 * grow
    with_w = -step1 * step0
    less_w = with_z + with_w * share_ref[0:1, 0:1]
    group = EDGE
    stores = []
    for i in range(tile_rows * EDGE // group):
        rows = slice(i * group, (i + 1) * group)
        precond, product = z_ref[rows, :].astype(F32), w_ref[rows, :]
        sol_ref[rows, :] = with_z * precond + with_w * product
        pre_ref[rows, :] = (precond - less_w * product - with_w * u_ref[rows, :].astype(F32)).astype(BF16)
        place = pl.ds(i * group, group)
        for k, (source, target) in enumerate(((sol_ref, sol_hbm), (pre_ref, pre_hbm))):
            copy = pltpu.make_async_copy(source.at[place], target.at[place], sems.at[2 * i + k])
            copy.start()
            stores.append(copy)
    for copy in stores:
        copy.wait()


def call(kernel, outs, args, name, scratch=(), in_space=pltpu.VMEM, out_space=pltpu.VMEM, flops=0):
    if not isinstance(in_space, list):
        in_space = [in_space] * len(args)
    return pl.pallas_call(
        kernel,
        out_shape=outs,
        in_specs=[pl.BlockSpec(memory_space=space) for space in in_space],
        out_specs=[pl.BlockSpec(memory_space=out_space)] * len(outs),
        scratch_shapes=scratch,
        compiler_params=pltpu.CompilerParams(vmem_limit_bytes=VMEM_LIMIT),
        cost_estimate=pl.CostEstimate(flops=flops, bytes_accessed=0, transcendentals=0),
        name=name,
    )(*args)


def per_device(right_side, east_face, north_face, left_factor, right_factor, wet_list):
    rows, cols = right_side.shape
    lons, lats = lax.axis_size("lon"), lax.axis_size("lat")
    tile_rows = rows // EDGE
    shape = functools.partial(jax.ShapeDtypeStruct, dtype=F32)
    like = lambda a: jax.ShapeDtypeStruct(a.shape, a.dtype)
    field = shape((rows, cols))
    half = jax.ShapeDtypeStruct((rows, cols), BF16)
    edge = shape((ROWS, EDGE))
    message = shape((2 * ROWS, EDGE))
    strip = shape((8, cols))
    across = [(0, 1), (1, 0)]

    def pairs(parity):
        forward = [(i, (i + 1) % lons) for i in range(parity, lons, 2)]
        return forward + [(b, a) for a, b in forward]

    by_place = (tile_rows, 2, EDGE, EDGE)
    left_factor, right_factor = left_factor.reshape(by_place), right_factor.reshape(by_place)
    arguments = [
        pltpu.with_memory_space_constraint(a, pltpu.HBM)
        for a in (wet_list, right_side, left_factor, right_factor, east_face, north_face)
    ]
    short, rhs, left, right, ef, nf, wet, to_e, to_w, to_a, to_b, to_l = call(
        first_kernel,
        [half, field, like(left_factor), like(right_factor), like(east_face), like(north_face),
         shape((ROWS, cols)), message, message, message, message, strip],
        arguments, "first",
        [pltpu.SMEM(wet_list.shape, jnp.int32), pltpu.SMEM((32,), F32),
         pltpu.SemaphoreType.DMA((9,))],
        in_space=pltpu.HBM,
    )
    arrays = (short, left, right, ef, nf, wet)
    wide = [pltpu.VMEM((rows, cols), F32)]
    results = [field, field, edge, edge]
    *early, far_a, far_b = call(early_inner_kernel, results + [message, message], (to_a, to_b, *arrays), "early_inner", wide)
    in_b = lax.ppermute(far_b, "lon", pairs(0))
    in_a = lax.ppermute(far_a, "lon", pairs(1))
    in_l = lax.ppermute(to_l, "lat", across)
    late = call(late_inner_kernel, results, arrays, "late_inner", wide)
    lat, row_e, row_w = call(
        lat_kernel, [strip, edge, edge], (early[1], late[1], left, right, to_l, in_l), "lat"
    )
    east, coef_e, flux_e1, turn_e, west, coef_w, flux_w1, turn_w, to_l2 = call(
        edge_kernel, [edge] * 8 + [strip],
        (left, lat, row_e, row_w, early[2], late[2], early[3], late[3], to_e, to_w, in_b, in_a), "edges",
    )
    from_w2 = lax.ppermute(east, "lon", [(i, (i + 1) % lons) for i in range(lons)])
    in_l2 = lax.ppermute(to_l2, "lat", across)
    results = [field, shape((5, 8, cols))]
    faces = (ef, nf, wet, lat, turn_e, turn_w, row_e, row_w)
    *done, to_w2 = call(early_middle_kernel, results + [edge], (west, short, rhs, *early[:2], *faces), "early_middle")
    from_e2 = lax.ppermute(to_w2, "lon", [((i + 1) % lons, i) for i in range(lons)])
    w, sums = call(late_middle_kernel, results, (*done, short, rhs, *late[:2], *faces), "late_middle")
    packed, flux_w, flux_l = call(
        sums_kernel, [shape((lons * lats, EDGE)), edge, strip],
        (sums, east, west, to_e, to_w, lat, flux_e1, flux_w1, coef_w, to_l, to_l2, in_l, from_w2, in_l2), "sums",
    )
    everyone = lax.all_to_all(packed, ("lon", "lat"), 0, 0, tiled=True)
    u, share = call(
        outer_kernel, [half, shape((8, EDGE))],
        (*arguments[2:], w, wet, east, coef_e, from_e2, flux_w, flux_l, sums), "outer",
        [pltpu.VMEM(a.shape, a.dtype) for a in arguments[2:]]
        + [pltpu.VMEM((ROWS, EDGE), F32), pltpu.SemaphoreType.DMA((8,))],
        in_space=[pltpu.HBM] * 4 + [pltpu.VMEM] * 8, flops=100_000_000_000,
    )
    return tuple(
        call(
            last_kernel, [field, half], (everyone, short, w, u, share), "last",
            [pltpu.VMEM((rows, cols), F32), pltpu.VMEM((rows, cols), BF16), pltpu.SemaphoreType.DMA((2 * tile_rows,))],
            out_space=pltpu.HBM,
        )
    )


def solution(mesh):
    tiles = P("lat", "lon", None, None)
    cells = P("lat", "lon")
    return jax.shard_map(
        per_device,
        mesh=mesh,
        in_specs=(cells, cells, cells, tiles, tiles, cells),
        out_specs=(cells, cells),
        check_vma=False,
    )
```

```python
import functools

import jax
import jax.numpy as jnp
from jax import lax
from jax.experimental import pallas as pl
from jax.experimental.pallas import tpu as pltpu
from jax.sharding import PartitionSpec as P

EDGE = 128
CELLS = 2 * EDGE
surface_term = 0.0001
F32 = jnp.float32
BF16 = jnp.bfloat16
VMEM_LIMIT = 8 * 1024 * 1024
HEAD = 4
SPAN = 16
ROWS = 16


def dot(left, right):
    return jnp.dot(left, right, preferred_element_type=F32)


def dot_nt(left, right):
    return lax.dot_general(left, right, (((1,), (1,)), ((), ())), preferred_element_type=F32)


def lane_index(rows, cols):
    return lax.broadcasted_iota(jnp.int32, (rows, cols), 1)


def row_index(rows, cols):
    return lax.broadcasted_iota(jnp.int32, (rows, cols), 0)


def rounded_product(left, tile, right):
    partial = dot(left, tile).astype(BF16)
    return dot(partial, right).astype(BF16)


def split(value):
    high = value.astype(BF16)
    return high, (value - high.astype(F32)).astype(BF16)


def wide_product(left, tile, right):
    partial = dot(jnp.concatenate([left, left], axis=1), jnp.concatenate(split(tile), axis=0))
    return dot(jnp.concatenate(split(partial), axis=1), jnp.concatenate([right, right], axis=0))


def fold(block):
    total = block[0:8]
    for k in range(1, block.shape[0] // 8):
        total = total + block[8 * k : 8 * k + 8]
    return total


def total(value):
    return jnp.sum(jnp.sum(value, axis=0, keepdims=True), axis=1, keepdims=True)


def column(rows_ref, i):
    return jnp.broadcast_to(rows_ref[i : i + 1, :], (EDGE, EDGE)).T


def on_low_band():
    return lax.axis_index("lat") == 0


def on_odd_sector():
    return lax.axis_index("lon") % 2 == 1


def held_up():
    return lax.axis_index("lon") % SPAN == 0


def set_row(block, at, value):
    row = row_index(8, CELLS)
    if at == 0:
        return jnp.concatenate([jnp.where(row == 0, value, block[:8]), block[8:]], axis=0)
    return jnp.concatenate([block[:-8], jnp.where(row == 7, value, block[-8:])], axis=0)


def differences(i, tile_rows, field_ref, wet_ref):
    field = field_ref[i * EDGE : (i + 1) * EDGE, :]
    wet = wet_ref[i : i + 1, :]
    lane = lane_index(1, CELLS)
    both = wet * pltpu.roll(wet, EDGE, 1)
    east_wet = jnp.where(lane == EDGE - 1, both, jnp.where(lane == CELLS - 1, 0.0, 1.0))
    above = min((i + 1) * EDGE, tile_rows * EDGE - 1)
    north = set_row(pltpu.roll(field, EDGE - 1, 0), -1, field_ref[above : above + 1, :])
    north_wet = wet * wet_ref[i + 1 : i + 2, :]
    return field, field - pltpu.roll(field, CELLS - 1, 1), field - north, east_wet, north_wet


def stencil(i, tile_rows, field_ref, ef_ref, nf_ref, wet_ref, south_flux, top_flux):
    rows = slice(i * EDGE, (i + 1) * EDGE)
    field, over_e, over_n, east_wet, north_wet = differences(i, tile_rows, field_ref, wet_ref)
    flux_e = (ef_ref[rows, :].astype(F32) * east_wet) * over_e
    flux_n = nf_ref[rows, :].astype(F32) * over_n
    last = top_flux if i == tile_rows - 1 else flux_n[EDGE - 1 :, :] * north_wet
    flux_n = set_row(flux_n, -1, last)
    flux_s = set_row(pltpu.roll(flux_n, 1, 0), 0, south_flux)
    image = surface_term * field + (flux_e - pltpu.roll(flux_e, 1, 1)) + (flux_n - flux_s)
    return field, image, last


def lat_flux(coef, own, other):
    flux = coef * (own - other)
    low = on_low_band()
    return jnp.where(low, flux, 0.0), jnp.where(low, 0.0, -flux)


def edge_rows(i, block, east_ref, west_ref):
    west_ref[i : i + 1, :] = block[:, :EDGE].T[0:1, :]
    east_ref[i : i + 1, :] = block[:, EDGE:].T[EDGE - 1 :, :]


def boundary_row(ref):
    return jnp.where(on_low_band(), ref[ref.shape[0] - 1 :, :], ref[0:1, :])


def first_kernel(
    wet_hbm, rhs_hbm, left_hbm, right_hbm, ef_hbm, nf_hbm,
    short_ref, rhs_ref, left_ref, right_ref, ef_ref, nf_ref, wet_ref, to_e, to_w, to_a, to_b, to_l,
    list_ref, flags_ref, sems,
):
    tile_rows = rhs_hbm.shape[0] // EDGE
    tiles = 2 * tile_rows
    used = [0]

    def load(source, target):
        copy = pltpu.make_async_copy(source, target, sems.at[used[0]])
        used[0] += 1
        copy.start()
        return copy

    listing = load(wet_hbm, list_ref)
    loads = {}
    for at, stop in ((0, HEAD), (HEAD, tile_rows)):
        rows, some = pl.ds(at * EDGE, (stop - at) * EDGE), pl.ds(at, stop - at)
        loads[at] = [
            load(rhs_hbm.at[rows], rhs_ref.at[rows]),
            load(left_hbm.at[some], left_ref.at[some]),
            load(right_hbm.at[some], right_ref.at[some]),
        ]
    faces = [load(ef_hbm, ef_ref), load(nf_hbm, nf_ref)]
    for ref in (wet_ref, to_e, to_w, to_l):
        ref[...] = jnp.zeros_like(ref)
    listing.wait()
    for t in range(flags_ref.shape[0]):
        flags_ref[t] = 0.0
    for k in range(tiles):
        flags_ref[list_ref[0, k]] = 1.0
    lane = lane_index(1, CELLS)
    for i in range(tile_rows):
        wet_ref[i : i + 1, :] = jnp.where(lane < EDGE, flags_ref[2 * i], flags_ref[2 * i + 1])
    for i in range(tile_rows):
        for copy in loads.get(i, ()):
            copy.wait()
        rows = slice(i * EDGE, (i + 1) * EDGE)
        residual = rhs_ref[rows, :] * wet_ref[i : i + 1, :]
        rounded = residual.astype(BF16)
        parts = [
            rounded_product(left_ref[i, k], rounded[:, k * EDGE : (k + 1) * EDGE], right_ref[i, k]) for k in range(2)
        ]
        short = jnp.concatenate(parts, axis=1)
        short_ref[rows, :] = short
        to_w[i : i + 1, :] = parts[0].T[0:16, :].astype(F32)[0:1, :]
        to_e[i : i + 1, :] = parts[1].T[EDGE - 16 :, :].astype(F32)[15:16, :]
    for copy in faces:
        copy.wait()
    for i in range(tile_rows):
        face = ef_ref[i * EDGE : (i + 1) * EDGE, EDGE:].T[EDGE - 16 :, :].astype(F32)[15:16, :]
        to_e[ROWS + i : ROWS + i + 1, :] = face * wet_ref[i : i + 1, EDGE:]
    to_w[ROWS : ROWS + tile_rows, :] = wet_ref[:tile_rows, :EDGE]
    rows = tile_rows * EDGE
    upper, lower = short_ref[rows - 16 : rows, :].astype(F32), short_ref[0:16, :].astype(F32)
    to_l[0:1, :] = jnp.where(on_low_band(), upper[15:16, :], lower[0:1, :])
    last = nf_ref[rows - 16 : rows, :].astype(F32)[15:16, :] * wet_ref[tile_rows - 1 : tile_rows, :]
    to_l[1:2, :] = jnp.where(on_low_band(), last, wet_ref[0:1, :])
    odd = on_odd_sector()
    to_a[...] = jnp.where(odd, to_e[...], to_w[...])
    to_b[...] = jnp.where(odd, to_w[...], to_e[...])


def inner(short_ref, left_ref, right_ref, ef_ref, nf_ref, wet_ref, q_ref, w_ref, east_ref, west_ref, z_ref):
    tile_rows = z_ref.shape[0] // EDGE
    east_ref[...] = jnp.zeros_like(east_ref)
    west_ref[...] = jnp.zeros_like(west_ref)
    south = top = jnp.zeros((1, CELLS), F32)
    z_ref[...] = short_ref[...].astype(F32)
    for i in range(tile_rows):
        rows = slice(i * EDGE, (i + 1) * EDGE)
        _, image, south = stencil(i, tile_rows, z_ref, ef_ref, nf_ref, wet_ref, south, top)
        q_ref[rows, :] = image
        parts = [
            wide_product(left_ref[i, k], image[:, k * EDGE : (k + 1) * EDGE], right_ref[i, k]) for k in range(2)
        ]
        product = jnp.concatenate(parts, axis=1)
        w_ref[rows, :] = product
        edge_rows(i, product, east_ref, west_ref)


def early_inner_kernel(a_in, b_in, *refs):
    *arrays, to_a, to_b, z_ref = refs
    to_a[...] = a_in[...]
    to_b[...] = b_in[...]

    @pl.when(held_up())
    def _():
        inner(*arrays, z_ref)


def late_inner_kernel(*refs):
    @pl.when(jnp.logical_not(held_up()))
    def _():
        inner(*refs)


def lat_kernel(early_w, late_w, left_ref, right_ref, to_l, in_l, lat_ref, row_e, row_w):
    tile_rows = early_w.shape[0] // EDGE
    low = on_low_band()
    end = tile_rows - 1
    flux = to_l[1:2, :] * in_l[1:2, :] * (to_l[0:1, :] - in_l[0:1, :])
    pick = (lane_index(16, EDGE) == jnp.where(low, EDGE - 1, 0)) & (row_index(16, EDGE) == 0)
    pick = jnp.where(pick, 1.0, 0.0).astype(BF16)
    boundary = jnp.where(held_up(), boundary_row(early_w), boundary_row(late_w))
    for ref in (lat_ref, row_e, row_w):
        ref[...] = jnp.zeros_like(ref)
    for k in range(2):
        at = slice(k * EDGE, (k + 1) * EDGE)
        left = jnp.where(low, left_ref[end, k], left_ref[0, k])
        right = jnp.where(low, right_ref[end, k], right_ref[0, k])
        by_col = dot_nt(pick, left)[0:1, :]
        by_row = dot(jnp.concatenate(split(jnp.broadcast_to(flux[:, at], (16, EDGE))), axis=0), right)
        by_row = by_row[0:1, :] + by_row[16:17, :]
        lat_ref[0:1, at] = by_col
        lat_ref[1:2, at] = by_row
        lat_ref[3:4, at] = boundary[:, at] + jnp.where(low, by_col[:, EDGE - 1 :], by_col[:, 0:1]) * by_row
    lat_ref[2:3, :] = flux
    for i in range(tile_rows):
        row_e[i : i + 1, :] = right_ref[i, 1, EDGE - 16 :, :].astype(F32)[15:16, :]
        row_w[i : i + 1, :] = right_ref[i, 0, 0:16, :].astype(F32)[0:1, :]


def one_side(side, left_ref, lat_ref, row_ref, early_rows, late_rows, own, in_b, in_a, edge_ref, coef, flux, turn):
    tile_rows = left_ref.shape[0]
    at = slice(side * EDGE, (side + 1) * EDGE)
    rim = side * (EDGE - 1)
    odd = on_odd_sector()
    other = jnp.where(odd, in_a[...], in_b[...]) if side else jnp.where(odd, in_b[...], in_a[...])
    coef[...] = own[ROWS:, :] * other[ROWS:, :]
    flux[...] = coef[...] * (own[:ROWS, :] - other[:ROWS, :])
    turn[...] = jnp.zeros_like(turn)
    spread = jnp.concatenate(split(flux[...]), axis=0)
    for i in range(tile_rows):
        turned = dot_nt(spread, left_ref[i, side])
        turn[i : i + 1, :] = turned[i : i + 1, :] + turned[ROWS + i : ROWS + i + 1, :]
    here = row_index(ROWS, EDGE) == jnp.where(on_low_band(), tile_rows - 1, 0)
    by_lat = lat_ref[0:1, at] * lat_ref[1:2, at][:, rim : rim + 1]
    rows = jnp.where(held_up(), early_rows[...], late_rows[...]) + jnp.where(here, by_lat, 0.0)
    edge_ref[...] = rows + turn[...] * row_ref[:, rim : rim + 1]


def edge_kernel(
    left_ref, lat_ref, row_e, row_w, early_e, late_e, early_w, late_w, to_e, to_w, in_b, in_a,
    east_ref, coef_e, flux_e, turn_e, west_ref, coef_w, flux_w, turn_w, to_l2, send_e,
):
    one_side(1, left_ref, lat_ref, row_e, early_e, late_e, to_e, in_b, in_a, east_ref, coef_e, flux_e, turn_e)
    one_side(0, left_ref, lat_ref, row_w, early_w, late_w, to_w, in_b, in_a, west_ref, coef_w, flux_w, turn_w)
    send_e[...] = jnp.zeros_like(send_e)
    send_e[:ROWS, :] = east_ref[...]
    end = left_ref.shape[0] - 1
    low = on_low_band()
    by_lon = [
        jnp.where(low, turn[end : end + 1, EDGE - 1 :] * row[end : end + 1, :], turn[0:1, 0:1] * row[0:1, :])
        for turn, row in ((turn_w, row_w), (turn_e, row_e))
    ]
    to_l2[...] = jnp.zeros_like(to_l2)
    to_l2[0:1, :] = lat_ref[3:4, :] + jnp.concatenate(by_lon, axis=1)


def middle(
    z_ref, rhs_ref, q_ref, w_in, ef_ref, nf_ref, wet_ref, lat_ref, turn_e, turn_w, right_e, right_w, w_ref, sums_ref
):
    tile_rows = z_ref.shape[0] // EDGE
    zero = jnp.zeros((8, CELLS), F32)
    rz, zq, rw, qw, faces, squares = zero, zero, zero, zero, zero, zero

    def complete(i, rz, zq, rw, qw):
        rows = slice(i * EDGE, (i + 1) * EDGE)
        image = q_ref[rows, :]
        product = w_in[rows, :] + jnp.concatenate(
            [column(turn_w, i) * right_w[i : i + 1, :], column(turn_e, i) * right_e[i : i + 1, :]], axis=1
        )
        if i in (0, tile_rows - 1):
            here = on_low_band() == (i > 0)
            by_row = jnp.where(here, lat_ref[1:2, :], 0.0)
            by_col = [jnp.broadcast_to(lat_ref[0:1, k * EDGE : (k + 1) * EDGE], (EDGE, EDGE)).T for k in range(2)]
            product = product + jnp.concatenate(by_col, axis=1) * by_row
        w_ref[rows, :] = product
        precond, given = z_ref[rows, :].astype(F32), rhs_ref[rows, :]
        rz, zq = rz + fold(given * precond), zq + fold(precond * image)
        return rz, zq, rw + fold(given * product), qw + fold(image * product)

    rz, zq, rw, qw = complete(0, rz, zq, rw, qw)
    for i in range(tile_rows):
        if i + 1 < tile_rows:
            rz, zq, rw, qw = complete(i + 1, rz, zq, rw, qw)
        rows = slice(i * EDGE, (i + 1) * EDGE)
        field, over_e, over_n, east_wet, north_wet = differences(i, tile_rows, w_ref, wet_ref)
        by_e = ef_ref[rows, :].astype(F32) * east_wet * (over_e * over_e)
        by_n = nf_ref[rows, :].astype(F32) * (over_n * over_n)
        by_n = set_row(by_n, -1, 0.0 if i == tile_rows - 1 else by_n[EDGE - 1 :, :] * north_wet)
        faces = faces + fold(by_e + by_n)
        squares = squares + fold(field * field)
    for k, total in enumerate((rz, zq, rw, qw, faces + surface_term * squares)):
        sums_ref[k] = total


def early_middle_kernel(west_in, *refs):
    *arrays, to_w = refs
    to_w[...] = west_in[...]

    @pl.when(held_up())
    def _():
        middle(*arrays)


def late_middle_kernel(early_w, early_sums, *refs):
    w_ref, sums_ref = refs[-2:]
    early = held_up()

    @pl.when(early)
    def _():
        w_ref[...] = early_w[...]
        sums_ref[...] = early_sums[...]

    @pl.when(jnp.logical_not(early))
    def _():
        middle(*refs)


def sums_kernel(
    sums_in, east_ref, west_ref, to_e, to_w, lat_ref, flux_e1, flux_w1, coef_w, own_l, own_l2, in_l, from_w, in_l2,
    packed_ref, flux_w, flux_l,
):
    over_w = west_ref[...] - from_w[:ROWS, :]
    flux_w[...] = coef_w[...] * over_w
    top, bottom = lat_flux(own_l[1:2, :] * in_l[1:2, :], own_l2[0:1, :], in_l2[0:1, :])
    flux_l[...] = jnp.zeros_like(flux_l)
    flux_l[0:1, :] = top
    flux_l[1:2, :] = -bottom

    outer = {
        1: total(flux_e1[...] * to_e[:ROWS, :] + flux_w1[...] * to_w[:ROWS, :])
        + total(lat_ref[2:3, :] * own_l[0:1, :]),
        3: total(flux_e1[...] * east_ref[...] + flux_w1[...] * west_ref[...])
        + total(lat_ref[2:3, :] * own_l2[0:1, :]),
        4: total(flux_w[...] * over_w) + total((top - bottom) * own_l2[0:1, :]),
    }
    lane = lane_index(1, EDGE)
    packed = jnp.zeros((1, EDGE), F32)
    for k in range(5):
        value = total(sums_in[k])
        packed = jnp.where(lane == k, value + outer[k] if k in outer else value, packed)
    packed_ref[...] = jnp.broadcast_to(packed, packed_ref.shape)


def outer_kernel(
    left_hbm, right_hbm, ef_hbm, nf_hbm, w_ref, wet_ref, east_ref, coef_e, from_e, flux_w, flux_l, sums_ref,
    u_ref, share_ref, left_ref, right_ref, ef_ref, nf_ref, flux_e, sems,
):
    tile_rows = w_ref.shape[0] // EDGE
    step = tile_rows // 2
    loads = []
    for k in range(tile_rows // step):
        rows, some = pl.ds(k * step * EDGE, step * EDGE), pl.ds(k * step, step)
        group = [
            pltpu.make_async_copy(source.at[place], target.at[place], sems.at[4 * k + n])
            for n, (source, target, place) in enumerate(
                ((ef_hbm, ef_ref, rows), (nf_hbm, nf_ref, rows), (left_hbm, left_ref, some), (right_hbm, right_ref, some))
            )
        ]
        for copy in group:
            copy.start()
        loads.append(group)
    flux_e[...] = coef_e[...] * (east_ref[...] - from_e[...])
    lane = lane_index(EDGE, EDGE)
    south, top = -flux_l[1:2, :], flux_l[0:1, :]
    zq, qw = (total(sums_ref[k]) for k in (1, 3))
    share = jnp.where(zq > 0.0, qw / jnp.where(zq > 0.0, zq, 1.0), 0.0)
    share_ref[...] = jnp.broadcast_to(share, share_ref.shape)
    for i in range(tile_rows):
        if i % step == 0:
            for copy in loads[i // step]:
                copy.wait()
        _, image, south = stencil(i, tile_rows, w_ref, ef_ref, nf_ref, wet_ref, south, top)
        image = image + jnp.concatenate(
            [jnp.where(lane == 0, column(flux_w, i), 0.0), jnp.where(lane == EDGE - 1, column(flux_e, i), 0.0)], axis=1
        )
        parts = [
            wide_product(left_ref[i, k], image[:, k * EDGE : (k + 1) * EDGE], right_ref[i, k]) for k in range(2)
        ]
        rows = slice(i * EDGE, (i + 1) * EDGE)
        u_ref[rows, :] = (jnp.concatenate(parts, axis=1) - share * w_ref[rows, :]).astype(BF16)


def last_kernel(all_ref, z_ref, w_ref, u_ref, share_ref, sol_hbm, pre_hbm, sol_ref, pre_ref, sems):
    tile_rows = z_ref.shape[0] // EDGE
    totals = jnp.sum(all_ref[...], axis=0, keepdims=True)
    lane = lane_index(1, EDGE)
    rz, zq, rw, qw, waw = (jnp.sum(jnp.where(lane == k, totals, 0.0), axis=1, keepdims=True) for k in range(5))
    step0 = rz / zq
    rz1 = step0 * (step0 * qw - rw)
    grow = 1.0 + rz1 / rz
    step1 = rz1 / (grow * grow * zq - 2.0 * grow * step0 * qw + step0 * step0 * waw)
    with_z = step0 + step1 * grow
    with_w = -step1 * step0
    less_w = with_z + with_w * share_ref[0:1, 0:1]
    group = EDGE
    stores = []
    for i in range(tile_rows * EDGE // group):
        rows = slice(i * group, (i + 1) * group)
        precond, product = z_ref[rows, :].astype(F32), w_ref[rows, :]
        sol_ref[rows, :] = with_z * precond + with_w * product
        pre_ref[rows, :] = (precond - less_w * product - with_w * u_ref[rows, :].astype(F32)).astype(BF16)
        place = pl.ds(i * group, group)
        for k, (source, target) in enumerate(((sol_ref, sol_hbm), (pre_ref, pre_hbm))):
            copy = pltpu.make_async_copy(source.at[place], target.at[place], sems.at[2 * i + k])
            copy.start()
            stores.append(copy)
    for copy in stores:
        copy.wait()


def call(kernel, outs, args, name, scratch=(), in_space=pltpu.VMEM, out_space=pltpu.VMEM, flops=0):
    if not isinstance(in_space, list):
        in_space = [in_space] * len(args)
    return pl.pallas_call(
        kernel,
        out_shape=outs,
        in_specs=[pl.BlockSpec(memory_space=space) for space in in_space],
        out_specs=[pl.BlockSpec(memory_space=out_space)] * len(outs),
        scratch_shapes=scratch,
        compiler_params=pltpu.CompilerParams(vmem_limit_bytes=VMEM_LIMIT),
        cost_estimate=pl.CostEstimate(flops=flops, bytes_accessed=0, transcendentals=0),
        name=name,
    )(*args)


def per_device(right_side, east_face, north_face, left_factor, right_factor, wet_list):
    rows, cols = right_side.shape
    lons, lats = lax.axis_size("lon"), lax.axis_size("lat")
    tile_rows = rows // EDGE
    shape = functools.partial(jax.ShapeDtypeStruct, dtype=F32)
    like = lambda a: jax.ShapeDtypeStruct(a.shape, a.dtype)
    field = shape((rows, cols))
    half = jax.ShapeDtypeStruct((rows, cols), BF16)
    edge = shape((ROWS, EDGE))
    message = shape((2 * ROWS, EDGE))
    strip = shape((8, cols))
    across = [(0, 1), (1, 0)]

    def pairs(parity):
        forward = [(i, (i + 1) % lons) for i in range(parity, lons, 2)]
        return forward + [(b, a) for a, b in forward]

    by_place = (tile_rows, 2, EDGE, EDGE)
    left_factor, right_factor = left_factor.reshape(by_place), right_factor.reshape(by_place)
    arguments = [
        pltpu.with_memory_space_constraint(a, pltpu.HBM)
        for a in (wet_list, right_side, left_factor, right_factor, east_face, north_face)
    ]
    short, rhs, left, right, ef, nf, wet, to_e, to_w, to_a, to_b, to_l = call(
        first_kernel,
        [half, field, like(left_factor), like(right_factor), like(east_face), like(north_face),
         shape((ROWS, cols)), message, message, message, message, strip],
        arguments, "first",
        [pltpu.SMEM(wet_list.shape, jnp.int32), pltpu.SMEM((32,), F32),
         pltpu.SemaphoreType.DMA((9,))],
        in_space=pltpu.HBM,
    )
    arrays = (short, left, right, ef, nf, wet)
    wide = [pltpu.VMEM((rows, cols), F32)]
    results = [field, field, edge, edge]
    *early, far_a, far_b = call(early_inner_kernel, results + [message, message], (to_a, to_b, *arrays), "early_inner", wide)
    in_b = lax.ppermute(far_b, "lon", pairs(0))
    in_a = lax.ppermute(far_a, "lon", pairs(1))
    in_l = lax.ppermute(to_l, "lat", across)
    late = call(late_inner_kernel, results, arrays, "late_inner", wide)
    lat, row_e, row_w = call(
        lat_kernel, [strip, edge, edge], (early[1], late[1], left, right, to_l, in_l), "lat"
    )
    east, coef_e, flux_e1, turn_e, west, coef_w, flux_w1, turn_w, to_l2, send_e = call(
        edge_kernel, [edge] * 8 + [strip, message],
        (left, lat, row_e, row_w, early[2], late[2], early[3], late[3], to_e, to_w, in_b, in_a), "edges",
    )
    from_w2 = lax.ppermute(send_e, "lon", [(i, (i + 1) % lons) for i in range(lons)])
    in_l2 = lax.ppermute(to_l2, "lat", across)
    results = [field, shape((5, 8, cols))]
    faces = (ef, nf, wet, lat, turn_e, turn_w, row_e, row_w)
    *done, to_w2 = call(early_middle_kernel, results + [edge], (west, short, rhs, *early[:2], *faces), "early_middle")
    from_e2 = lax.ppermute(to_w2, "lon", [((i + 1) % lons, i) for i in range(lons)])
    w, sums = call(late_middle_kernel, results, (*done, short, rhs, *late[:2], *faces), "late_middle")
    packed, flux_w, flux_l = call(
        sums_kernel, [shape((lons * lats, EDGE)), edge, strip],
        (sums, east, west, to_e, to_w, lat, flux_e1, flux_w1, coef_w, to_l, to_l2, in_l, from_w2, in_l2), "sums",
    )
    everyone = lax.all_to_all(packed, ("lon", "lat"), 0, 0, tiled=True)
    u, share = call(
        outer_kernel, [half, shape((8, EDGE))],
        (*arguments[2:], w, wet, east, coef_e, from_e2, flux_w, flux_l, sums), "outer",
        [pltpu.VMEM(a.shape, a.dtype) for a in arguments[2:]]
        + [pltpu.VMEM((ROWS, EDGE), F32), pltpu.SemaphoreType.DMA((8,))],
        in_space=[pltpu.HBM] * 4 + [pltpu.VMEM] * 8, flops=100_000_000_000,
    )
    return tuple(
        call(
            last_kernel, [field, half], (everyone, short, w, u, share), "last",
            [pltpu.VMEM((rows, cols), F32), pltpu.VMEM((rows, cols), BF16), pltpu.SemaphoreType.DMA((2 * tile_rows,))],
            out_space=pltpu.HBM,
        )
    )


def solution(mesh):
    tiles = P("lat", "lon", None, None)
    cells = P("lat", "lon")
    return jax.shard_map(
        per_device,
        mesh=mesh,
        in_specs=(cells, cells, cells, tiles, tiles, cells),
        out_specs=(cells, cells),
        check_vma=False,
    )
```
